32 devices in a mesh: wide: 8 (over z, x), narrow: 4 (over y, core).
Axes of the slice: x: 2, y: 2, z: 4, core: 2. Of those that a mesh axis runs over, the one named last changes fastest.
Arguments:
- passage_tokens: bfloat16 [16384, 768], P(('wide', 'narrow')), may hold values from -6 to 6
- query_tokens: bfloat16 [8192, 768], P(('wide', 'narrow')), may hold values from -6 to 6
- passage_lengths: int32 [32, 4], P(('wide', 'narrow')), may hold values from 1 to 256, 512 in all within a row
- query_lengths: int32 [32, 4], P(('wide', 'narrow')), may hold values from 1 to 128, 256 in all within a row
- pair_index: int32 [128], P(('wide', 'narrow')), may hold values from 0 to 127, each once
- attn_gain: bfloat16 [768], replicated, may hold values from 0.5 to 1.5
- w_query: bfloat16 [768, 768], replicated, may hold values from -0.02734375 to 0.02734375
- w_key: bfloat16 [768, 768], replicated, may hold values from -0.21875 to 0.21875
- w_value: bfloat16 [768, 768], replicated, may hold values from -0.21875 to 0.21875
- w_out: bfloat16 [768, 768], replicated, may hold values from -1.75 to 1.75
- bias_table: bfloat16 [32, 12], replicated, may hold values from -4 to 4
- ffn_gain: bfloat16 [768], replicated, may hold values from 0.5 to 1.5
- w_in: bfloat16 [768, 3072], replicated, may hold values from -0.21875 to 0.21875
- w_back: bfloat16 [3072, 768], replicated, may hold values from -0.109375 to 0.109375
- final_gain: bfloat16 [768], replicated, may hold values from 0.5 to 1.5
- w_proj: bfloat16 [768, 768], replicated, may hold values from -0.21875 to 0.21875
Outputs:
- query_loss: float32 [128], P(('wide', 'narrow'))
- passage_grad: float32 [16384, 768], P(('wide', 'narrow'))
- query_grad: float32 [8192, 768], P(('wide', 'narrow'))
- attn_gain_grad: float32 [768], replicated
- query_w_grad: float32 [768, 768], P('wide', 'narrow')
- key_w_grad: float32 [768, 768], P('wide', 'narrow')
- value_w_grad: float32 [768, 768], P('wide', 'narrow')
- out_w_grad: float32 [768, 768], P('wide', 'narrow')
- bias_grad: float32 [32, 12], replicated
- ffn_gain_grad: float32 [768], replicated
- in_ff_grad: float32 [768, 3072], P('wide', 'narrow')
- out_ff_grad: float32 [3072, 768], P('wide', 'narrow')
- final_gain_grad: float32 [768], replicated
- proj_grad: float32 [768, 768], P('wide', 'narrow')
The draws below stay inside these ranges and needn't reach their ends.
Inputs may be any that keep to these rules, and one draw needn't show every extreme that they name: `passage_lengths`: the 4 lengths of a passage row sum to 512; every row holds a passage of 256 tokens. `query_lengths`: the 4 lengths of a query row sum to 256; every row holds a query of 128 tokens. `pair_index`: every passage is the positive of exactly one query.
All inputs are finite; a program needn't handle non-finite values.
Results may differ from the reference program's by a relative error of at most 0.015.
Values may be sent and summed in bfloat16 or wider, within the bound.
No kernel may reach another device: no remote copies, remote signals or barrier semaphores. Data moves between devices by JAX's collectives and lax.ppermute only.
A program may use at most 256 MiB of HBM per device.

```python
import math
import jax
import jax.numpy as jnp
import numpy as np
from jax import lax

D = 768
HEADS = 12
DK = 64
FF = 3072
BUCKETS = 32
MAX_DIST = 128
SEGS = 4
PROW = 512
QROW = 256
ROWS = 32
PASSAGES = 128
PASS_TOKENS = 16384
QUERY_TOKENS = 8192


def levels(rng, extent, split, smallest, high):
    gain = 1.0
    for dim, blocks in split:
        steps = jax.random.uniform(jax.random.fold_in(jax.random.fold_in(rng, 6), dim), (blocks,), jnp.float32, smallest / len(split), high / len(split))
        gain = gain * jnp.repeat(jnp.exp(steps), extent[dim] // blocks).reshape((-1,) + (1,) * (len(extent) - 1 - dim))
    return gain


def length_profile(count, total, bound, lean):
    weights = [(1 << 20) // math.isqrt(rank ** lean) + 1 for rank in range(2, count + 1)]
    rest, holding = total - bound - (count - 1), [1] * (count - 1)
    while rest > 0:
        candidates = [i for i in range(count - 1) if holding[i] < bound]
        pool, remaining = sum([weights[i] for i in candidates]), rest
        for i in candidates:
            addition = min(bound - holding[i], max(1, remaining * weights[i] // pool), rest)
            holding[i] = holding[i] + addition
            rest = rest - addition
    return np.array([bound] + holding)


def ragged(key, count, total, bound, slope):
    if count == 2:
        one = jax.random.randint(key, (), max(1, total - bound), min(bound, total - 1) + 1)
        return jnp.stack([one, total - one])
    sizes = jnp.asarray(length_profile(count, total, bound, slope), jnp.int32)
    pairs = (count - 1) // 2
    giver, taker = sizes[1:1 + 2 * pairs:2], sizes[2:2 + 2 * pairs:2]
    slack = jnp.minimum(giver - 1, bound - taker)
    moved = jax.random.randint(jax.random.fold_in(key, 1), (pairs,), 0, 1 << 20) % (slack + 1)
    sizes = sizes.at[1:1 + 2 * pairs:2].set(giver - moved).at[2:2 + 2 * pairs:2].set(taker + moved)
    return sizes[jax.random.permutation(jax.random.fold_in(key, 2), count)]


def centred(key, shape, deviation, bound, cuts=(), kind=jnp.bfloat16):
    array = jax.random.normal(key, shape, jnp.float32) * deviation
    if len(cuts) > 0:
        array = levels(key, shape, cuts, -0.22, 0.18) * array
    return jnp.clip(array, min=-bound, max=bound).astype(kind)


def setup_inputs(seed: int = 0) -> dict:
    keys = jax.random.split(jax.random.key(seed), 17)
    passage_tokens = centred(keys[0], (PASS_TOKENS, D), 1.0, 6.0, ((0, 32),))
    query_tokens = centred(keys[1], (QUERY_TOKENS, D), 1.0, 6.0, ((0, 32),))
    passage_lengths = jax.vmap(lambda own: ragged(own, SEGS, PROW, PROW // 2, 2))(jax.random.split(keys[2], ROWS)).reshape((ROWS, SEGS)).astype(jnp.int32)
    query_lengths = jax.vmap(lambda own: ragged(own, SEGS, QROW, QROW // 2, 2))(jax.random.split(keys[3], ROWS)).reshape((ROWS, SEGS)).astype(jnp.int32)
    pair_index = jax.random.permutation(keys[4], PASSAGES).astype(jnp.int32)
    attn_gain = jnp.clip(1.0 + 0.1 * jax.random.normal(keys[5], (D,), jnp.float32), 0.5, 1.5).astype(jnp.bfloat16)
    w_query = centred(keys[6], (D, D), (D * DK) ** -0.5, 0.02734375)
    w_key = centred(keys[7], (D, D), D ** -0.5, 0.21875)
    w_value = centred(keys[8], (D, D), D ** -0.5, 0.21875)
    w_out = centred(keys[9], (D, D), (D // 64) ** -0.5, 1.75)
    bias_table = centred(keys[10], (BUCKETS, HEADS), 1.0, 4.0)
    ffn_gain = jnp.clip(1.0 + 0.1 * jax.random.normal(keys[11], (D,), jnp.float32), 0.5, 1.5).astype(jnp.bfloat16)
    w_in = centred(keys[12], (D, FF), D ** -0.5, 0.21875)
    w_back = centred(keys[13], (FF, D), FF ** -0.5, 0.109375)
    final_gain = jnp.clip(1.0 + 0.1 * jax.random.normal(keys[14], (D,), jnp.float32), 0.5, 1.5).astype(jnp.bfloat16)
    w_proj = centred(keys[15], (D, D), D ** -0.5, 0.21875)
    return dict(passage_tokens=passage_tokens, query_tokens=query_tokens, passage_lengths=passage_lengths, query_lengths=query_lengths, pair_index=pair_index, attn_gain=attn_gain, w_query=w_query, w_key=w_key, w_value=w_value, w_out=w_out, bias_table=bias_table, ffn_gain=ffn_gain, w_in=w_in, w_back=w_back, final_gain=final_gain, w_proj=w_proj)


logit_divisor_factor = 0.02
norm_eps = 1e-06
gelu_coef = 0.7978845608028654
cube_coef = 0.044715
HIGHEST = lax.Precision.HIGHEST

@jax.custom_vjp
def low(v):
    return lax.optimization_barrier(v.astype(jnp.bfloat16)).astype(jnp.float32)

@jax.custom_vjp
def low_back(v):
    return v

def low_keep(v):
    return (low(v), None)

def low_pass(kept, grad):
    return (grad,)

def back_keep(v):
    return (v, None)

def back_low(kept, grad):
    return (low(grad),)
low.defvjp(low_keep, low_pass)
low_back.defvjp(back_keep, back_low)

def inner_match_matrix(left, right):
    return jnp.dot(left, right, precision=HIGHEST, preferred_element_type=jnp.float32)

def bucket_edges():
    half_count = BUCKETS // 2
    exact_count = half_count // 2
    level_count = half_count - exact_count
    spread_ratio = MAX_DIST // exact_count
    edge_list = []
    for level_step in range(1, level_count):
        target = exact_count ** level_count * spread_ratio ** level_step
        candidate = exact_count
        while candidate ** level_count < target:
            candidate += 1
        edge_list.append(candidate)
    return edge_list

def relative_buckets(length):
    half_count = BUCKETS // 2
    exact_count = half_count // 2
    positions = jnp.arange(length, dtype=jnp.int32)
    relative = positions[None, :] - positions[:, None]
    distance = jnp.abs(relative)
    far_bucket = jnp.full_like(distance, exact_count)
    for edge_value in bucket_edges():
        far_bucket = far_bucket + (distance >= edge_value).astype(jnp.int32)
    far_bucket = jnp.minimum(far_bucket, half_count - 1)
    inside_part = jnp.where(distance < exact_count, distance, far_bucket)
    return jnp.where(relative > 0, half_count, 0).astype(jnp.int32) + inside_part

def segment_ids(row_lengths, length):
    seg_ends = jnp.cumsum(row_lengths.astype(jnp.int32))
    positions = jnp.arange(length, dtype=jnp.int32)
    return lax.optimization_barrier(jnp.sum((positions[:, None] >= seg_ends[None, :]).astype(jnp.int32), axis=1))

def rms_scale(values, gain_vec):
    return values * lax.rsqrt(lax.optimization_barrier(jnp.mean(values * values, axis=-1, keepdims=True)) + norm_eps) * gain_vec

def gelu_tanh(values):
    return 0.5 * values * (1.0 + jnp.tanh(gelu_coef * (values + cube_coef * values * values * values)))

def normalize_rows(values):
    return values * lax.rsqrt(lax.optimization_barrier(jnp.sum(values * values, axis=-1, keepdims=True)) + norm_eps)

def row_forward(row_tokens, row_lengths, layer_weights):
    attn_gain, w_query, w_key, w_value, w_out, bias_table, ffn_gain, w_in, w_back, final_gain = layer_weights
    length = row_tokens.shape[0]
    seg_of = segment_ids(row_lengths, length)
    same_seg = seg_of[:, None] == seg_of[None, :]
    seg_hot = (jnp.arange(SEGS, dtype=jnp.int32)[:, None] == seg_of[None, :]).astype(jnp.float32)
    normed = low(rms_scale(row_tokens, attn_gain))
    queries = low(low_back(inner_match_matrix(normed, w_query))).reshape(length, HEADS, DK)
    keys_low = low(low_back(inner_match_matrix(normed, w_key))).reshape(length, HEADS, DK)
    values_low = low(low_back(inner_match_matrix(normed, w_value))).reshape(length, HEADS, DK)
    rel_bias = jnp.transpose(bias_table[relative_buckets(length)], (2, 0, 1))
    scores = low_back(jnp.einsum('ihd,jhd->hij', queries, keys_low, precision=HIGHEST) + rel_bias)
    masked = jnp.where(same_seg[None], scores, -1000000000.0)
    shifted = masked - lax.optimization_barrier(jnp.max(masked, axis=-1, keepdims=True))
    exp_scores = jnp.exp(shifted)
    attn_probs = exp_scores / lax.optimization_barrier(jnp.sum(exp_scores, axis=-1, keepdims=True))
    probs_low = low(attn_probs)
    context = jnp.einsum('hij,jhd->ihd', probs_low, values_low, precision=HIGHEST).reshape(length, HEADS * DK)
    context = low(low_back(context))
    residual = row_tokens + low_back(inner_match_matrix(context, w_out))
    normed_two = low(rms_scale(residual, ffn_gain))
    up_proj = low_back(inner_match_matrix(normed_two, w_in))
    hidden = low(gelu_tanh(up_proj))
    output = residual + low_back(inner_match_matrix(hidden, w_back))
    final_out = rms_scale(output, final_gain)
    return inner_match_matrix(seg_hot, final_out) / row_lengths.astype(jnp.float32)[:, None]

def tower(rows, row_lengths, layer_weights):

    def single_line_entry(row_item):
        return row_forward(row_item[0], row_item[1], layer_weights)
    pooled = lax.map(jax.checkpoint(single_line_entry), (rows, row_lengths))
    return pooled.reshape(-1, pooled.shape[-1])

def reference(passage_tokens, query_tokens, passage_lengths, query_lengths, pair_index, attn_gain, w_query, w_key, w_value, w_out, bias_table, ffn_gain, w_in, w_back, final_gain, w_proj):
    weights32 = tuple((item_w.astype(jnp.float32) for item_w in (attn_gain, w_query, w_key, w_value, w_out, bias_table, ffn_gain, w_in, w_back, final_gain, w_proj)))

    def objective(passage_x, query_x, weights):
        layer_weights = weights[:10]
        proj_weight = weights[10]
        passage_pooled = tower(passage_x.reshape(-1, PROW, D), passage_lengths, layer_weights)
        query_pooled = tower(query_x.reshape(-1, QROW, D), query_lengths, layer_weights)
        document_unit_embeds = low(normalize_rows(low_back(inner_match_matrix(low(passage_pooled), proj_weight))))
        question_unit_embeds = low(normalize_rows(low_back(inner_match_matrix(low(query_pooled), proj_weight))))
        angle_match_matrix = inner_match_matrix(question_unit_embeds, document_unit_embeds.T) / logit_divisor_factor
        top_sim = lax.optimization_barrier(jnp.max(angle_match_matrix, axis=1, keepdims=True))
        log_total = top_sim[:, 0] + jnp.log(lax.optimization_barrier(jnp.sum(jnp.exp(angle_match_matrix - top_sim), axis=1)))
        target = jnp.take_along_axis(angle_match_matrix, pair_index[:, None].astype(jnp.int32), axis=1)[:, 0]
        return log_total - target
    query_loss, pullback = jax.vjp(objective, passage_tokens.astype(jnp.float32), query_tokens.astype(jnp.float32), weights32)
    document_adjoint, d_query, d_weights = pullback(jnp.ones_like(query_loss))
    return (query_loss, document_adjoint, d_query, d_weights[0], d_weights[1], d_weights[2], d_weights[3], d_weights[4], d_weights[5], d_weights[6], d_weights[7], d_weights[8], d_weights[9], d_weights[10])
```

```python
import functools

import jax
import jax.numpy as jnp
from jax import lax
from jax.experimental import pallas as pl
from jax.experimental.pallas import tpu as pltpu
from jax.sharding import PartitionSpec as P

BUCKETS = 32
MAX_DIST = 128
SCALE = 0.02
EPS = 1e-06
GELU = 0.7978845608028654
CUBE = 0.044715
HIGHEST = lax.Precision.HIGHEST
F32 = jnp.float32
BF16 = jnp.bfloat16
AXES = ("wide", "narrow")
NB = 4
WB = 8
CH = 128
LANES = 384
VMEM = 56 * 2**20


def bucket_edges():
    half = BUCKETS // 2
    exact = half // 2
    levels = half - exact
    ratio = MAX_DIST // exact
    edges = []
    for step in range(1, levels):
        target = exact**levels * ratio**step
        candidate = exact
        while candidate**levels < target:
            candidate += 1
        edges.append(candidate)
    return edges


def nn(a, b, **kw):
    return lax.dot_general(a, b, (((1,), (0,)), ((), ())), preferred_element_type=F32, **kw)


def nt(a, b, **kw):
    return lax.dot_general(a, b, (((1,), (1,)), ((), ())), preferred_element_type=F32, **kw)


def bucket_hot(span, shift=0):
    shape = (BUCKETS, 2 * span)
    rel = lax.broadcasted_iota(jnp.int32, shape, 1) - shift
    rel = jnp.where(rel < 0, rel + 2 * span, rel) - span
    dist = jnp.abs(rel)
    half = BUCKETS // 2
    exact = half // 2
    far = jnp.full(shape, exact, jnp.int32)
    for edge in bucket_edges():
        far = far + jnp.where(dist >= edge, 1, 0)
    far = jnp.minimum(far, half - 1)
    bucket = jnp.where(dist < exact, dist, far) + jnp.where(rel > 0, half, 0)
    return bucket == lax.broadcasted_iota(jnp.int32, shape, 0)


def seg_bounds(info, segs, span, shape, axis):
    at = lax.broadcasted_iota(jnp.int32, shape, axis)
    lo = jnp.zeros(shape, jnp.int32)
    hi = jnp.zeros(shape, jnp.int32)
    for tower in range(2):
        start = tower * span
        for s in range(segs):
            size = info[2 + tower * segs + s]
            here = at == tower * segs + s
            lo = jnp.where(here, start, lo)
            hi = jnp.where(here, start + size, hi)
            start = start + size
    return lo, hi


def seg_of(info, tower, segs, first, shape, axis):
    at = lax.broadcasted_iota(jnp.int32, shape, axis) + first
    seg = jnp.zeros(shape, jnp.int32)
    end = 0
    for s in range(segs - 1):
        end = end + info[2 + tower * segs + s]
        seg = seg + jnp.where(at >= end, 1, 0)
    return seg


def rms(v, gain):
    return v * lax.rsqrt(jnp.mean(v * v, axis=-1, keepdims=True) + EPS) * gain


def rms_back(v, gain, dy):
    r = lax.rsqrt(jnp.mean(v * v, axis=-1, keepdims=True) + EPS)
    gdy = gain * dy
    inner = jnp.mean(gdy * v, axis=-1, keepdims=True)
    return r * gdy - v * (r * r * r * inner), jnp.sum(dy * v * r, axis=0, keepdims=True)


def qkv_kernel(info, xp, xq, gain, wq, wk, wv, normed, q, k, v):
    lp = xp.shape[0]

    @pl.when(pl.program_id(0) == 0)
    def _():
        g = gain[...].astype(F32)
        normed[:lp, :] = rms(xp[...].astype(F32), g).astype(BF16)
        normed[lp:, :] = rms(xq[...].astype(F32), g).astype(BF16)

    n = normed[...]
    q[...] = nn(n, wq[...]).astype(BF16)
    k[...] = nn(n, wk[...]).astype(BF16)
    v[...] = nn(n, wv[...]).astype(BF16)


def attn_kernel(lp, lq, segs, dk, info, table, q, k, v, probs_p, probs_q, ctx, rows):
    @pl.when(pl.program_id(0) == 0)
    def _():
        rows[...] = nn(table[...], bucket_hot(lp).astype(F32).astype(BF16))

    for hh in range(2):
        row = rows[pl.ds(2 * pl.program_id(0) + hh, 1), :]
        bias = pltpu.roll(jnp.broadcast_to(row, (CH, 2 * lp)), 0, 1, stride=1, stride_axis=0)
        cols = slice(hh * dk, (hh + 1) * dk)
        for tower, off, span, probs in ((0, 0, lp, probs_p), (1, lp, lq, probs_q)):
            seg_j = seg_of(info, tower, segs, 0, (1, span), 1)
            kh = k[off : off + span, cols]
            vh = v[off : off + span, cols]
            for r0 in range(0, span, CH):
                seg_i = seg_of(info, tower, segs, r0, (CH, 1), 0)
                s = nt(q[off + r0 : off + r0 + CH, cols], kh)
                s = s + bias[:, lp - r0 : lp - r0 + span]
                s = jnp.where(seg_i == seg_j, s, -1000000000.0)
                e = jnp.exp(s - jnp.max(s, axis=-1, keepdims=True))
                p = e * (1.0 / jnp.sum(e, axis=-1, keepdims=True))
                p = p.astype(BF16)
                probs[hh, r0 : r0 + CH, :] = p
                ctx[off + r0 : off + r0 + CH, cols] = nn(p, vh).astype(BF16)


def ffn_kernel(
    lp, lq, segs, info, ctx, xp, xq, w_out, fgain, w_in, w_back, lgain,
    residual, normed_two, hidden, slope, output, pooled,
):
    step = pl.program_id(0)
    total = lp + lq

    @pl.when(step == 0)
    def _():
        g = fgain[...].astype(F32)
        for x, off, span in ((xp, 0, lp), (xq, lp, lq)):
            here = slice(off, off + span)
            res = x[...].astype(F32) + nn(ctx[here, :], w_out[...])
            residual[here, :] = res
            output[here, :] = res
            normed_two[here, :] = rms(res, g).astype(BF16)

    part = 256
    for r0 in range(0, total, part):
        here = slice(r0, r0 + part)
        u = nn(normed_two[here, :], w_in[...])
        uu = u * u
        t = jnp.tanh(u * (GELU + (GELU * CUBE) * uu))
        half = 0.5 + 0.5 * t
        h = (u * half).astype(BF16)
        hidden[here, :] = h
        slope[here, :] = (
            half + (0.5 * u) * (1.0 - t * t) * (GELU + (3.0 * GELU * CUBE) * uu)
        ).astype(BF16)
        output[here, :] += nn(h, w_back[...])

    @pl.when(step == pl.num_programs(0) - 1)
    def _():
        final = rms(output[...], lgain[...].astype(F32))
        lo, hi = seg_bounds(info, segs, lp, (2 * segs, 1), 0)
        at = lax.broadcasted_iota(jnp.int32, (2 * segs, total), 1)
        hot = jnp.where((at >= lo) & (at < hi), 1.0, 0.0)
        mean = nn(hot, final, precision=HIGHEST) / (hi - lo).astype(F32)
        width = final.shape[1]
        pooled[:, :width] = mean.astype(BF16)
        shape = (2 * segs, pooled.shape[1] - width)
        at_row = lax.broadcasted_iota(jnp.int32, shape, 0)
        at_col = lax.broadcasted_iota(jnp.int32, shape, 1)
        code = jnp.zeros(shape, jnp.int32)
        for s in range(segs):
            pair = info[2 + 2 * segs + s]
            code = jnp.where((at_row == segs + s) & (at_col == 0), pair // 64, code)
            code = jnp.where((at_row == segs + s) & (at_col == 1), pair % 64, code)
        pooled[:, width:] = code.astype(F32).astype(BF16)


def loss_math(segs, block_row, block_col, gathered, w_proj):
    count = gathered.shape[0]
    width = w_proj.shape[0]
    low = gathered[:, :width]
    code = gathered[:, width:].astype(F32)
    pair = code[:, 0:1] * 64.0 + code[:, 1:2]
    row = lax.broadcasted_iota(jnp.int32, (count, 1), 0) % (2 * segs)
    col = lax.broadcasted_iota(jnp.int32, (1, count), 1) % (2 * segs)
    number = (block_col * segs + col).astype(F32)
    is_query = row >= segs
    is_passage = col < segs
    proj = nn(low, w_proj)
    scale = lax.rsqrt(jnp.sum(proj * proj, axis=-1, keepdims=True) + EPS)
    embed = proj * scale
    embed_low = embed.astype(BF16)
    sims = nt(embed_low, embed_low) / SCALE
    masked = jnp.where(is_passage, sims, -1e30)
    top = jnp.max(masked, axis=1, keepdims=True)
    expo = jnp.where(is_passage, jnp.exp(masked - top), 0.0)
    total = jnp.sum(expo, axis=1, keepdims=True)
    hot = jnp.where(is_passage & (number == pair), 1.0, 0.0)
    loss = top + jnp.log(total) - jnp.sum(hot * sims, axis=1, keepdims=True)
    d_sims = jnp.where(is_query, (expo / total - hot) / SCALE, 0.0)
    d_embed = nn(d_sims + d_sims.T, embed_low.astype(F32), precision=HIGHEST)
    d_proj = (d_embed - embed * jnp.sum(embed * d_embed, axis=-1, keepdims=True)) * scale
    return loss, d_proj.astype(BF16)


def loss_kernel(segs, bits, info, gathered, w_proj, loss, d_proj, d_pooled):
    count = gathered.shape[0]

    def device(shape, axis):
        place = lax.broadcasted_iota(jnp.int32, shape, axis) // (2 * segs)
        other = jnp.zeros(shape, jnp.int32)
        for at, bit in enumerate(bits):
            other = other + ((place >> at) & 1) * bit
        return other ^ (info[0] * NB + info[1])

    value, d_low = loss_math(
        segs, device((count, 1), 0), device((1, count), 1), gathered[...], w_proj[...]
    )
    loss[...] = jnp.broadcast_to(value[: 2 * segs], loss.shape)
    d_proj[...] = d_low
    d_pooled[...] = nt(d_low[: 2 * segs], w_proj[...])


def out_ff_kernel(
    lp, lq, segs, info, d_pooled, output, lgain, hidden,
    d_output, d_ffn, gain_grad, send, keep, turned,
):
    total = lp + lq
    width = output.shape[1]
    rows = width // NB

    @pl.when(pl.program_id(0) == 0)
    def _():
        lo, hi = seg_bounds(info, segs, lp, (1, 2 * segs), 1)
        lo_c, hi_c = seg_bounds(info, segs, lp, (2 * segs, 1), 0)
        at = lax.broadcasted_iota(jnp.int32, (total, 2 * segs), 0)
        hot = jnp.where((at >= lo) & (at < hi), 1.0, 0.0)
        dy = nn(hot, d_pooled[...] / (hi_c - lo_c).astype(F32), precision=HIGHEST)
        dv, dg = rms_back(output[...], lgain[...].astype(F32), dy)
        d_output[...] = dv
        gain_grad[...] = dg
        d_ffn[...] = dv.astype(BF16)
        flipped = dv.T.astype(BF16)
        for n in range(NB):
            turned[pl.ds(pl.multiple_of((n ^ info[1]) * rows, rows), rows), :] = flipped[
                n * rows : (n + 1) * rows
            ]

    res = nn(turned[...], hidden[...])
    for n in range(NB):
        for x in range(2):
            part = res[n * rows : (n + 1) * rows, x * LANES : (x + 1) * LANES].astype(BF16)
            dst = (send if n % 2 else keep).at[n // 2, 0]
            dst[x ^ (info[0] % 2)] = part


def ffn_back_kernel(
    lp, lq, info, d_ffn, w_back, slope, w_in, normed_two, d_output, residual, fgain, ctx, w_out,
    send, keep, d_resid, gain_grad, d_ctx, turned, total,
):
    step = pl.program_id(0)
    width = residual.shape[1]
    rows = width // WB
    wide = info[0]

    @pl.when(step == 0)
    def _():
        flipped = normed_two[...].astype(F32).T.astype(BF16)
        for w in range(WB):
            turned[pl.ds(pl.multiple_of((w ^ wide) * rows, rows), rows), :] = flipped[
                w * rows : (w + 1) * rows
            ]
        total[...] = jnp.zeros_like(total)

    d_up = (nt(d_ffn[...], w_back[...]) * slope[...].astype(F32)).astype(BF16)
    total[...] += nt(d_up, w_in[...])
    res = nn(turned[...], d_up).astype(BF16)

    def put(dst):
        for half in range(2):
            dst[:, half * rows : (half + 1) * rows, :] = res[
                :, half * LANES : (half + 1) * LANES
            ].reshape(WB, rows, LANES)

    @pl.when(step < NB // 2)
    def _():
        put(send.at[step])

    @pl.when(step >= NB // 2)
    def _():
        put(keep.at[step - NB // 2])

    @pl.when(step == NB - 1)
    def _():
        dv, dg = rms_back(residual[...], fgain[...].astype(F32), total[...])
        dr = d_output[...] + dv
        d_resid[...] = dr
        gain_grad[...] = dg
        da = dr.astype(BF16)
        d_ctx[...] = nt(da, w_out[...]).astype(BF16)
        flipped = ctx[...].astype(F32).T.astype(BF16)
        for w in range(WB):
            turned[pl.ds(pl.multiple_of((w ^ wide) * rows, rows), rows), :] = flipped[
                w * rows : (w + 1) * rows
            ]
        grad = nn(turned[...], da)
        cols = width // NB
        for n in range(NB):
            part = grad[:, n * cols : (n + 1) * cols].reshape(WB, rows, cols)
            part = jnp.concatenate([part[:, : rows // 2], part[:, rows // 2 :]], axis=2)
            part = part.astype(BF16)
            y = (n // 2) ^ (info[1] // 2)

            @pl.when((n % 2) == (info[1] % 2))
            def _():
                keep[y, :, 2 * rows :, :] = part

            @pl.when((n % 2) != (info[1] % 2))
            def _():
                send[y, :, 2 * rows :, :] = part


def attn_back_kernel(
    lp, lq, dk, info, q, k, v, d_ctx, probs_p, probs_q, d_q, d_k, d_v, bias_grad,
    diag, d_s, turned, sums,
):
    step = pl.program_id(0)
    pair = slice(0, 2 * dk)

    @pl.when(step == 0)
    def _():
        sums[...] = jnp.zeros_like(sums)

    for tower, off, span, probs in ((0, 0, lp, probs_p), (1, lp, lq, probs_q)):
        here = slice(off, off + span)
        q_t = q[here, pair].astype(F32).T.astype(BF16)
        c_t = d_ctx[here, pair].astype(F32).T.astype(BF16)
        for hh in range(2):
            cols = slice(hh * dk, (hh + 1) * dk)
            kh = k[here, cols]
            vh = v[here, cols]
            for r0 in range(0, span, CH):
                rows = slice(off + r0, off + r0 + CH)
                p = probs[hh, r0 : r0 + CH, :].astype(F32)
                t = p * nt(d_ctx[rows, cols], vh)
                ds = t - p * jnp.sum(t, axis=-1, keepdims=True)
                if tower == 0 and r0 == 0:
                    diag[hh, :, :lp] = jnp.zeros((CH, lp), F32)
                    diag[hh, :, lp:] = ds
                else:
                    diag[hh, :, lp - r0 : lp - r0 + span] += ds
                low = ds.astype(BF16)
                d_s[hh, r0 : r0 + CH, :span] = low
                d_q[rows, cols] = nn(low, kh).astype(BF16)
            turned[0, cols, :span] = nn(q_t[cols], d_s[hh, :span, :span])
            turned[1, cols, :span] = nn(c_t[cols], probs[hh])
        d_k[here, pair] = turned[0, :, :span].T.astype(BF16)
        d_v[here, pair] = turned[1, :, :span].T.astype(BF16)
    at_i = lax.broadcasted_iota(jnp.int32, (CH, CH), 0)
    at_j = lax.broadcasted_iota(jnp.int32, (CH, CH), 1)
    mirror = jnp.where(at_i + at_j == CH - 1, 1.0, 0.0)
    for hh in range(2):
        flipped = nn(mirror, diag[hh], precision=HIGHEST)
        turn = pltpu.roll(flipped, 0, 1, stride=1, stride_axis=0)
        sums[pl.ds(2 * step + hh, 1), :] = jnp.sum(turn, axis=0, keepdims=True)

    @pl.when(step == pl.num_programs(0) - 1)
    def _():
        hot = bucket_hot(lp, CH - 1).astype(F32)
        bias_grad[...] = nt(hot, sums[...], precision=HIGHEST)


def qkv_grad_kernel(info, normed, d_q, d_k, d_v, send, keep, turned, blocks):
    width = normed.shape[1]
    rows, cols = width // WB, width // NB
    flipped = normed[...].astype(F32).T.astype(BF16)
    for w in range(WB):
        turned[pl.ds(pl.multiple_of((w ^ info[0]) * rows, rows), rows), :] = flipped[
            w * rows : (w + 1) * rows
        ]
    left = turned[...]
    gq, gk, gv = nn(left, d_q[...]), nn(left, d_k[...]), nn(left, d_v[...])
    for n in range(NB):
        here = slice(n * cols, (n + 1) * cols)
        both = jnp.concatenate([gq[:, here], gk[:, here]], axis=1).astype(BF16)
        blocks[n, :, :rows, :] = both.reshape(WB, rows, LANES)
        part = gv[:, here].reshape(WB, rows, cols)
        part = jnp.concatenate([part[:, : rows // 2], part[:, rows // 2 :]], axis=2)
        blocks[n, :, rows:, :] = part.astype(BF16)
    core, y0 = info[1] % 2, info[1] // 2
    for y in range(2):
        send[y] = blocks[(y ^ y0) * 2 + (1 - core)]
        keep[y] = blocks[(y ^ y0) * 2 + core]


def input_kernel(
    lp, lq, info, d_q, d_k, d_v, wq, wk, wv, d_resid, xp, xq, gain, grad_p, grad_q, gain_grad
):
    g = gain[...].astype(F32)
    sums = None
    for x, off, span, out in ((xp, 0, lp, grad_p), (xq, lp, lq, grad_q)):
        here = slice(off, off + span)
        dn = nt(d_q[here, :], wq[...]) + nt(d_k[here, :], wk[...]) + nt(d_v[here, :], wv[...])
        dv, dg = rms_back(x[...].astype(F32), g, dn)
        out[...] = d_resid[here, :] + dv
        sums = dg if sums is None else sums + dg
    gain_grad[...] = sums


def call(kernel, grid, info, args, in_specs, outs, out_specs, scratch=(), flops=0, moved=0):
    return pl.pallas_call(
        kernel,
        grid_spec=pltpu.PrefetchScalarGridSpec(
            num_scalar_prefetch=1,
            grid=grid,
            in_specs=in_specs,
            out_specs=out_specs,
            scratch_shapes=list(scratch),
        ),
        out_shape=[jax.ShapeDtypeStruct(s, t) for s, t in outs],
        compiler_params=pltpu.CompilerParams(vmem_limit_bytes=VMEM),
        cost_estimate=pl.CostEstimate(flops=flops, bytes_accessed=moved, transcendentals=0),
    )(info, *args)


def whole(*shape):
    return pl.BlockSpec(shape, lambda *_: (0,) * len(shape), pipeline_mode=pl.Buffered(1))


def out_whole(*shape):
    return pl.BlockSpec(shape, lambda *_: (0,) * len(shape))


def permute(array, bit, count):
    return lax.ppermute(array, AXES, [(i, i ^ bit) for i in range(count)])


CORE, Y, X, Z0, Z1 = 1, 2, 4, 8, 16
GATHER = (Y, X, Z0, Z1, CORE)


def take(array, dims, bit, which):
    return lax.index_in_dim(array, which, dims.index(bit), keepdims=False)


def encode(values):
    high = lax.reduce_precision(values, 8, 7)
    return jnp.concatenate([high, values - high], axis=0).astype(BF16)


def decode(coded):
    half = coded.shape[0] // 2
    return coded[:half].astype(F32) + coded[half:].astype(F32)


def reduce_scatter(send, keep, orders, count, late=None):
    got = permute(send, CORE, count)
    small = None
    if late is not None:
        coded = encode(late())
        small = encode(decode(coded) + decode(permute(coded, CORE, count)))
    rows = keep.shape[-2]
    share = rows // len(orders)
    states = []
    for i, order in enumerate(orders):
        dims = [Y, Z1, Z0, X]
        own = keep[..., i * share : (i + 1) * share, :]
        new = got[..., i * share : (i + 1) * share, :]
        first = take(own, dims, order[0], 1) + take(new, dims, order[0], 1)
        rest = take(own, dims, order[0], 0) + take(new, dims, order[0], 0)
        states.append((first, rest, [d for d in dims if d != order[0]], order))
    for stage in range(4):
        arrived = []
        for i, (first, _, _, order) in enumerate(states):
            if small is not None and i == 0:
                shape = first.shape
                flat = jnp.concatenate([small, first.reshape(-1, LANES)], axis=0)
                flat = permute(flat, order[stage], count)
                other = flat[: small.shape[0]]
                small = encode(decode(small) + decode(other))
                arrived.append(flat[small.shape[0] :].reshape(shape))
            else:
                arrived.append(permute(first, order[stage], count))
        later = []
        for (_, rest, dims, order), new in zip(states, arrived):
            if stage == 3:
                later.append((None, rest + new, dims, order))
                continue
            bit = order[stage + 1]
            later.append(
                (
                    take(rest, dims, bit, 1) + take(new, dims, bit, 1),
                    take(rest, dims, bit, 0) + take(new, dims, bit, 0),
                    [d for d in dims if d != bit],
                    order,
                )
            )
        states = later
    done = jnp.concatenate([rest for _, rest, _, _ in states], axis=0)
    return done, (None if small is None else decode(small))


ORDERS = ((Y, X, Z0, Z1), (X, Y, Z0, Z1), (Z0, X, Y, Z1))


def per_device(
    fast, n_wide, n_narrow,
    xp, xq, passage_lengths, query_lengths, pair_index, attn_gain, w_query, w_key, w_value, w_out,
    bias_table, ffn_gain, w_in, w_back, final_gain, w_proj,
):
    lp, width = xp.shape
    lq = xq.shape[0]
    total = lp + lq
    heads = bias_table.shape[1]
    dk = width // heads
    ff = w_in.shape[1]
    segs = passage_lengths.shape[1]
    count = n_wide * n_narrow
    pairs = heads // 2
    rows, cols = width // WB, width // NB
    wide_at, narrow_at = lax.axis_index("wide"), lax.axis_index("narrow")
    place = jnp.stack([wide_at, narrow_at]) if fast else jnp.zeros((2,), jnp.int32)
    info = jnp.concatenate(
        [place.astype(jnp.int32), passage_lengths[0], query_lengths[0], pair_index]
    )
    g_attn, g_ffn, g_final = (g.reshape(1, width) for g in (attn_gain, ffn_gain, final_gain))
    table = jnp.pad(bias_table.T, ((0, 16 - heads), (0, 0)))
    mm = 2 * total * width * width

    tile = 256
    col_tile = pl.BlockSpec((width, tile), lambda i, *_: (0, i))
    act_tile = pl.BlockSpec((total, tile), lambda i, *_: (0, i))
    normed, q, k, v = call(
        qkv_kernel,
        (width // tile,),
        info,
        (xp, xq, g_attn, w_query, w_key, w_value),
        [whole(lp, width), whole(lq, width), whole(1, width), col_tile, col_tile, col_tile],
        [((total, width), BF16)] * 4,
        [out_whole(total, width), act_tile, act_tile, act_tile],
        flops=3 * mm,
        moved=10 * 2**20,
    )

    head_tile = pl.BlockSpec((total, 2 * dk), lambda i, *_: (0, i))
    probs_p_spec = pl.BlockSpec((2, lp, lp), lambda i, *_: (i, 0, 0))
    probs_q_spec = pl.BlockSpec((2, lq, lq), lambda i, *_: (i, 0, 0))
    probs_p, probs_q, ctx = call(
        functools.partial(attn_kernel, lp, lq, segs, dk),
        (pairs,),
        info,
        (table, q, k, v),
        [whole(16, BUCKETS), head_tile, head_tile, head_tile],
        [((heads, lp, lp), BF16), ((heads, lq, lq), BF16), ((total, width), BF16)],
        [probs_p_spec, probs_q_spec, head_tile],
        [pltpu.VMEM((16, 2 * lp), F32)],
        flops=20 * 10**9,
        moved=13 * 2**20,
    )

    ff_tile = ff // NB
    w_in_spec = pl.BlockSpec((width, ff_tile), lambda i, *_: (0, i))
    w_back_spec = pl.BlockSpec((ff_tile, width), lambda i, *_: (i, 0))
    ff_spec = pl.BlockSpec((total, ff_tile), lambda i, *_: (0, i))
    message = width + 128
    residual, normed_two, hidden, slope, output, pooled = call(
        functools.partial(ffn_kernel, lp, lq, segs),
        (NB,),
        info,
        (ctx, xp, xq, w_out, g_ffn, w_in, w_back, g_final),
        [
            whole(total, width), whole(lp, width), whole(lq, width), whole(width, width),
            whole(1, width), w_in_spec, w_back_spec, whole(1, width),
        ],
        [
            ((total, width), F32), ((total, width), BF16), ((total, ff), BF16),
            ((total, ff), BF16), ((total, width), F32), ((2 * segs, message), BF16),
        ],
        [
            out_whole(total, width), out_whole(total, width), ff_spec, ff_spec,
            out_whole(total, width), out_whole(2 * segs, message),
        ],
        flops=9 * mm,
        moved=30 * 2**20,
    )

    if fast:
        gathered = pooled
        for bit in GATHER:
            gathered = jnp.concatenate([gathered, permute(gathered, bit, count)], axis=0)
        every = gathered.shape[0]
        loss, d_proj, d_pooled = call(
            functools.partial(loss_kernel, segs, GATHER),
            (1,),
            info,
            (gathered, w_proj),
            [whole(every, message), whole(width, width)],
            [((2 * segs, 128), F32), ((every, width), BF16), ((2 * segs, width), F32)],
            [out_whole(2 * segs, 128), out_whole(every, width), out_whole(2 * segs, width)],
            flops=10**10,
            moved=3 * 2**20,
        )
        query_loss = loss[segs:, 0]
    else:
        gathered = lax.all_gather(pooled, AXES, axis=0, tiled=True)
        every = gathered.shape[0]
        block = jnp.arange(every, dtype=jnp.int32) // (2 * segs)
        loss, d_proj = loss_math(segs, block[:, None], block[None, :], gathered, w_proj)
        mine = (wide_at * n_narrow + narrow_at) * 2 * segs
        query_loss = lax.dynamic_slice_in_dim(loss, mine + segs, segs, 0)[:, 0]
        d_pooled = nt(lax.dynamic_slice_in_dim(d_proj, mine, 2 * segs, 0), w_proj)

    own_rows, own_cols = width // n_wide, width // n_narrow
    proj_left = lax.dynamic_slice(gathered, (0, wide_at * own_rows), (every, own_rows))
    proj_right = lax.dynamic_slice(d_proj, (0, narrow_at * own_cols), (every, own_cols))

    half_ff = rows * 2
    d_output, d_ffn, final_gain_grad, send1, keep1 = call(
        functools.partial(out_ff_kernel, lp, lq, segs),
        (WB // 2,),
        info,
        (d_pooled, output, g_final, hidden),
        [
            whole(2 * segs, width), whole(total, width), whole(1, width),
            pl.BlockSpec((total, 2 * LANES), lambda i, s: (0, i ^ (s[0] // 2))),
        ],
        [
            ((total, width), F32), ((total, width), BF16), ((1, width), F32),
            ((2, WB // 2, 2, cols, LANES), BF16), ((2, WB // 2, 2, cols, LANES), BF16),
        ],
        [
            out_whole(total, width), out_whole(total, width), out_whole(1, width),
            pl.BlockSpec((2, 1, 2, cols, LANES), lambda i, *_: (0, i, 0, 0, 0)),
            pl.BlockSpec((2, 1, 2, cols, LANES), lambda i, *_: (0, i, 0, 0, 0)),
        ],
        [pltpu.VMEM((width, total), BF16)],
        flops=4 * mm,
        moved=16 * 2**20,
    )

    def turn(i, s):
        return (((i % 2) * 2) + (1 - i // 2)) ^ s[1]

    two = 2 * rows + rows // 2
    send2, keep2, d_resid, ffn_gain_grad, d_ctx = call(
        functools.partial(ffn_back_kernel, lp, lq),
        (NB,),
        info,
        (d_ffn, w_back, slope, w_in, normed_two, d_output, residual, g_ffn, ctx, w_out),
        [
            whole(total, width),
            pl.BlockSpec((ff_tile, width), lambda i, s: (turn(i, s), 0)),
            pl.BlockSpec((total, ff_tile), lambda i, s: (0, turn(i, s))),
            pl.BlockSpec((width, ff_tile), lambda i, s: (0, turn(i, s))),
            whole(total, width), whole(total, width), whole(total, width), whole(1, width),
            whole(total, width), whole(width, width),
        ],
        [
            ((2, WB, two, LANES), BF16), ((2, WB, two, LANES), BF16), ((total, width), F32),
            ((1, width), F32), ((total, width), BF16),
        ],
        [
            out_whole(2, WB, two, LANES), out_whole(2, WB, two, LANES), out_whole(total, width),
            out_whole(1, width), out_whole(total, width),
        ],
        [pltpu.VMEM((width, total), BF16), pltpu.VMEM((total, width), F32)],
        flops=14 * mm,
        moved=40 * 2**20,
    )

    d_q, d_k, d_v, bias_grad = call(
        functools.partial(attn_back_kernel, lp, lq, dk),
        (pairs,),
        info,
        (q, k, v, d_ctx, probs_p, probs_q),
        [head_tile] * 4 + [probs_p_spec, probs_q_spec],
        [((total, width), BF16)] * 3 + [((BUCKETS, 16), F32)],
        [head_tile] * 3 + [out_whole(BUCKETS, 16)],
        [
            pltpu.VMEM((2, CH, 2 * lp), F32), pltpu.VMEM((2, lp, lp), BF16),
            pltpu.VMEM((2, 2 * dk, lp), F32), pltpu.VMEM((16, 2 * lp), F32),
        ],
        flops=30 * 10**9,
        moved=16 * 2**20,
    )

    three = rows + rows // 2
    send3, keep3 = call(
        qkv_grad_kernel,
        (1,),
        info,
        (normed, d_q, d_k, d_v),
        [whole(total, width)] * 4,
        [((2, WB, three, LANES), BF16)] * 2,
        [out_whole(2, WB, three, LANES)] * 2,
        [pltpu.VMEM((width, total), BF16), pltpu.VMEM((NB, WB, three, LANES), BF16)],
        flops=3 * mm,
        moved=9 * 2**20,
    )

    grad_p, grad_q, attn_gain_grad = call(
        functools.partial(input_kernel, lp, lq),
        (1,),
        info,
        (d_q, d_k, d_v, w_query, w_key, w_value, d_resid, xp, xq, g_attn),
        [whole(total, width)] * 3
        + [whole(width, width)] * 3
        + [whole(total, width), whole(lp, width), whole(lq, width), whole(1, width)],
        [((lp, width), F32), ((lq, width), F32), ((1, width), F32)],
        [out_whole(lp, width), out_whole(lq, width), out_whole(1, width)],
        flops=3 * mm,
        moved=14 * 2**20,
    )

    def small():
        flat = jnp.concatenate(
            [
                attn_gain_grad.reshape(-1),
                ffn_gain_grad.reshape(-1),
                final_gain_grad.reshape(-1),
                bias_grad[:, :heads].reshape(-1),
            ]
        )
        return jnp.pad(flat, (0, 8 * LANES - flat.size)).reshape(8, LANES)

    proj_grad = lax.dot_general(
        proj_left, proj_right, (((0,), (0,)), ((), ())), preferred_element_type=F32
    )
    if fast:
        split = (2, 2, 2, 2)
        done1, _ = reduce_scatter(
            send1.reshape(split + (cols, LANES)), keep1.reshape(split + (cols, LANES)),
            ORDERS, count,
        )
        done2, _ = reduce_scatter(
            send2.reshape(split + (two, LANES)), keep2.reshape(split + (two, LANES)),
            ORDERS, count,
        )
        done3, smalls = reduce_scatter(
            send3.reshape(split + (three, LANES)), keep3.reshape(split + (three, LANES)),
            ORDERS, count, small,
        )
        done1, done2, done3 = (d.astype(F32) for d in (done1, done2, done3))
        out_ff = done1.T
        in_ff = jnp.concatenate([done2[:rows], done2[rows : 2 * rows]], axis=1)
        out_w = jnp.concatenate(
            [done2[2 * rows : 2 * rows + rows // 2, :cols], done2[2 * rows : 2 * rows + rows // 2, cols:]],
            axis=0,
        )
        query_w, key_w = done3[:rows, :cols], done3[:rows, cols:]
        value_w = jnp.concatenate([done3[rows:, :cols], done3[rows:, cols:]], axis=0)
    else:
        def blocks(send, keep):
            both = jnp.stack([keep, send], axis=1).astype(F32)
            return both.reshape((NB, WB) + both.shape[-2:])

        def spread(matrix):
            matrix = lax.psum_scatter(matrix, "wide", scatter_dimension=0, tiled=True)
            return lax.psum_scatter(matrix, "narrow", scatter_dimension=1, tiled=True)

        def side(part):
            half = part.shape[2] // 2
            return jnp.concatenate([part[:, :, :half], part[:, :, half:]], axis=3)

        def stack(part):
            half = part.shape[3] // 2
            return jnp.concatenate([part[..., :half], part[..., half:]], axis=2)

        def matrix(part):
            return part.transpose(1, 2, 0, 3).reshape(WB * part.shape[2], NB * part.shape[3])

        b1 = blocks(send1.reshape(2, WB, cols, LANES), keep1.reshape(2, WB, cols, LANES))
        b2, b3 = blocks(send2, keep2), blocks(send3, keep3)
        out_ff = spread(matrix(b1.transpose(0, 1, 3, 2)))
        in_ff = spread(matrix(side(b2[:, :, : 2 * rows])))
        out_w = spread(matrix(stack(b2[:, :, 2 * rows :])))
        query_w = spread(matrix(b3[:, :, :rows, :cols]))
        key_w = spread(matrix(b3[:, :, :rows, cols:]))
        value_w = spread(matrix(stack(b3[:, :, rows:])))
        smalls = lax.psum(small(), AXES)
    smalls = smalls.reshape(-1)
    gain_a, gain_f, gain_l = (smalls[i * width : (i + 1) * width] for i in range(3))
    bias = smalls[3 * width : 3 * width + BUCKETS * heads].reshape(BUCKETS, heads)
    return (
        query_loss, grad_p, grad_q, gain_a, query_w, key_w, value_w, out_w, bias, gain_f,
        in_ff, out_ff, gain_l, proj_grad,
    )


def solution(mesh):
    n_wide, n_narrow = mesh.shape["wide"], mesh.shape["narrow"]
    fast = (n_wide, n_narrow) == (WB, NB)
    rows = P(AXES, None)
    owned = P("wide", "narrow")
    return jax.shard_map(
        functools.partial(per_device, fast, n_wide, n_narrow),
        mesh=mesh,
        in_specs=(rows, rows, rows, rows, P(AXES)) + (P(),) * 11,
        out_specs=(
            P(AXES), rows, rows, P(), owned, owned, owned, owned, P(), P(),
            owned, owned, P(), owned,
        ),
        check_vma=False,
    )
```

```python
import functools

import jax
import jax.numpy as jnp
from jax import lax
from jax.experimental import pallas as pl
from jax.experimental.pallas import tpu as pltpu
from jax.sharding import PartitionSpec as P

BUCKETS = 32
MAX_DIST = 128
SCALE = 0.02
EPS = 1e-06
GELU = 0.7978845608028654
CUBE = 0.044715
HIGHEST = lax.Precision.HIGHEST
F32 = jnp.float32
BF16 = jnp.bfloat16
AXES = ("wide", "narrow")
NB = 4
WB = 8
CH = 128
LANES = 384


def bucket_edges():
    half = BUCKETS // 2
    exact = half // 2
    levels = half - exact
    ratio = MAX_DIST // exact
    edges = []
    for step in range(1, levels):
        target = exact**levels * ratio**step
        candidate = exact
        while candidate**levels < target:
            candidate += 1
        edges.append(candidate)
    return edges


def nn(a, b, **kw):
    return lax.dot_general(a, b, (((1,), (0,)), ((), ())), preferred_element_type=F32, **kw)


def tn(a, b):
    return lax.dot_general(a, b, (((0,), (0,)), ((), ())), preferred_element_type=F32)


def nt(a, b, **kw):
    return lax.dot_general(a, b, (((1,), (1,)), ((), ())), preferred_element_type=F32, **kw)


def bucket_hot(span, shift=0):
    shape = (BUCKETS, 2 * span)
    rel = lax.broadcasted_iota(jnp.int32, shape, 1) - shift
    rel = span - jnp.where(rel < 0, rel + 2 * span, rel)
    dist = jnp.abs(rel)
    half = BUCKETS // 2
    exact = half // 2
    far = jnp.full(shape, exact, jnp.int32)
    for edge in bucket_edges():
        far = far + jnp.where(dist >= edge, 1, 0)
    far = jnp.minimum(far, half - 1)
    bucket = jnp.where(dist < exact, dist, far) + jnp.where(rel > 0, half, 0)
    return bucket == lax.broadcasted_iota(jnp.int32, shape, 0)


def seg_bounds(info, segs, span, shape, axis):
    at = lax.broadcasted_iota(jnp.int32, shape, axis)
    lo = jnp.zeros(shape, jnp.int32)
    hi = jnp.zeros(shape, jnp.int32)
    for tower in range(2):
        start = tower * span
        for s in range(segs):
            size = info[2 + tower * segs + s]
            here = at == tower * segs + s
            lo = jnp.where(here, start, lo)
            hi = jnp.where(here, start + size, hi)
            start = start + size
    return lo, hi


def seg_of(info, tower, segs, shape, axis):
    at = lax.broadcasted_iota(jnp.int32, shape, axis)
    seg = jnp.zeros(shape, jnp.int32)
    end = 0
    for s in range(segs - 1):
        end = end + info[2 + tower * segs + s]
        seg = seg + jnp.where(at >= end, 1, 0)
    return seg


def rms(v, gain):
    return v * lax.rsqrt(jnp.mean(v * v, axis=-1, keepdims=True) + EPS) * gain


def rms_back(v, gain, dy):
    r = lax.rsqrt(jnp.mean(v * v, axis=-1, keepdims=True) + EPS)
    gdy = gain * dy
    inner = jnp.mean(gdy * v, axis=-1, keepdims=True)
    return r * gdy - v * (r * r * r * inner), jnp.sum(dy * v * r, axis=0, keepdims=True)


def wide_row(gain):
    return gain[...].astype(F32).reshape(1, gain.shape[0])


def qkv_kernel(info, xp, xq, gain, wq, wk, wv, normed, q, k, v):
    lp = xp.shape[0]

    @pl.when(pl.program_id(0) == 0)
    def _():
        g = wide_row(gain)
        normed[:lp, :] = rms(xp[...].astype(F32), g).astype(BF16)
        normed[lp:, :] = rms(xq[...].astype(F32), g).astype(BF16)

    n = normed[...]
    q[...] = nn(n, wq[...]).astype(BF16)
    k[...] = nn(n, wk[...]).astype(BF16)
    v[...] = nn(n, wv[...]).astype(BF16)


def attn_kernel(lp, lq, segs, dk, info, table, q, k, v, probs_p, probs_q, ctx, rows):
    @pl.when(pl.program_id(0) == 0)
    def _():
        heads = table.shape[1]
        rows[:heads, :] = tn(table[...], bucket_hot(lp).astype(F32).astype(BF16))

    units = []
    for hh in range(2):
        row = rows[pl.ds(2 * pl.program_id(0) + hh, 1), :]
        bias = pltpu.roll(jnp.broadcast_to(row, (CH, 2 * lp)), 0, 1, stride=1, stride_axis=0)
        cols = slice(hh * dk, (hh + 1) * dk)
        units.append((hh, bias, cols, 0, 0, lp, probs_p))
        units.append((hh, bias, cols, 1, lp, lq, probs_q))
    scores = []
    for hh, bias, cols, tower, off, span, probs in units:
        here = slice(off, off + span)
        s = nt(k[here, cols], q[here, cols])
        s = s + jnp.concatenate(
            [bias[:, lp - r0 : lp - r0 + span] for r0 in range(0, span, CH)], axis=0
        )
        seg_j = seg_of(info, tower, segs, (span, 1), 0)
        seg_i = seg_of(info, tower, segs, (1, span), 1)
        scores.append(jnp.where(seg_i == seg_j, s, -1000000000.0))
    lows = []
    for (hh, _, _, _, _, _, probs), s in zip(units, scores):
        e = jnp.exp(s - jnp.max(s, axis=0, keepdims=True))
        p = e * (1.0 / jnp.sum(e, axis=0, keepdims=True))
        p = p.astype(BF16)
        probs[hh] = p
        lows.append(p)
    for (_, _, cols, _, off, span, _), p in zip(units, lows):
        ctx[off : off + span, cols] = tn(p, v[off : off + span, cols]).astype(BF16)


def ffn_kernel(
    lp, lq, segs, info, ctx, xp, xq, w_out, fgain, w_in, w_back, lgain,
    residual, normed_two, hidden, slope, output, pooled,
):
    step = pl.program_id(0)
    total = lp + lq

    @pl.when(step == 0)
    def _():
        g = wide_row(fgain)
        for x, off, span in ((xp, 0, lp), (xq, lp, lq)):
            here = slice(off, off + span)
            res = x[...].astype(F32) + nn(ctx[here, :], w_out[...])
            residual[here, :] = res
            output[here, :] = res
            normed_two[here, :] = rms(res, g).astype(BF16)

    part = 256
    for r0 in range(0, total, part):
        here = slice(r0, r0 + part)
        u = nn(normed_two[here, :], w_in[...])
        uu = u * u
        t = jnp.tanh(u * (GELU + (GELU * CUBE) * uu))
        half = 0.5 + 0.5 * t
        h = (u * half).astype(BF16)
        hidden[here, :] = h
        slope[here, :] = (
            half + (0.5 * u) * (1.0 - t * t) * (GELU + (3.0 * GELU * CUBE) * uu)
        ).astype(BF16)
        output[here, :] += nn(h, w_back[...])

    @pl.when(step == pl.num_programs(0) - 1)
    def _():
        final = rms(output[...], wide_row(lgain))
        lo, hi = seg_bounds(info, segs, lp, (2 * segs, 1), 0)
        at = lax.broadcasted_iota(jnp.int32, (2 * segs, total), 1)
        hot = jnp.where((at >= lo) & (at < hi), 1.0, 0.0)
        mean = nn(hot, final, precision=HIGHEST) / (hi - lo).astype(F32)
        width = final.shape[1]
        pooled[:, :width] = mean.astype(BF16)
        shape = (2 * segs, pooled.shape[1] - width)
        at_row = lax.broadcasted_iota(jnp.int32, shape, 0)
        at_col = lax.broadcasted_iota(jnp.int32, shape, 1)
        code = jnp.zeros(shape, jnp.int32)
        for s in range(segs):
            pair = info[2 + 2 * segs + s]
            code = jnp.where((at_row == segs + s) & (at_col == 0), pair // 64, code)
            code = jnp.where((at_row == segs + s) & (at_col == 1), pair % 64, code)
        pooled[:, width:] = code.astype(F32).astype(BF16)


def loss_math(segs, block_row, block_col, gathered, w_proj):
    count = gathered.shape[0]
    width = w_proj.shape[0]
    low = gathered[:, :width]
    code = gathered[:, width:].astype(F32)
    pair = code[:, 0:1] * 64.0 + code[:, 1:2]
    row = lax.broadcasted_iota(jnp.int32, (count, 1), 0) % (2 * segs)
    col = lax.broadcasted_iota(jnp.int32, (1, count), 1) % (2 * segs)
    number = (block_col * segs + col).astype(F32)
    is_query = row >= segs
    is_passage = col < segs
    proj = nn(low, w_proj)
    scale = lax.rsqrt(jnp.sum(proj * proj, axis=-1, keepdims=True) + EPS)
    embed = proj * scale
    embed_low = embed.astype(BF16)
    sims = nt(embed_low, embed_low) / SCALE
    masked = jnp.where(is_passage, sims, -1e30)
    top = jnp.max(masked, axis=1, keepdims=True)
    expo = jnp.where(is_passage, jnp.exp(masked - top), 0.0)
    total = jnp.sum(expo, axis=1, keepdims=True)
    hot = jnp.where(is_passage & (number == pair), 1.0, 0.0)
    loss = top + jnp.log(total) - jnp.sum(hot * sims, axis=1, keepdims=True)
    d_sims = jnp.where(is_query, (expo / total - hot) / SCALE, 0.0)
    d_embed = nn(d_sims + d_sims.T, embed_low.astype(F32), precision=HIGHEST)
    d_proj = (d_embed - embed * jnp.sum(embed * d_embed, axis=-1, keepdims=True)) * scale
    return loss, d_proj.astype(BF16)


def loss_kernel(segs, bits, info, near, far, w_proj, loss, d_proj, d_pooled, every):
    gathered = jnp.concatenate([near[...], far[...]], axis=0)
    every[...] = gathered
    count = gathered.shape[0]

    def device(shape, axis):
        place = lax.broadcasted_iota(jnp.int32, shape, axis) // (2 * segs)
        other = jnp.zeros(shape, jnp.int32)
        for at, bit in enumerate(bits):
            other = other + ((place >> at) & 1) * bit
        return other ^ (info[0] * NB + info[1])

    value, d_low = loss_math(
        segs, device((count, 1), 0), device((1, count), 1), gathered, w_proj[...]
    )
    loss[...] = jnp.broadcast_to(value[: 2 * segs], loss.shape)
    d_proj[...] = d_low
    d_pooled[...] = nt(d_low[: 2 * segs], w_proj[...])


def out_ff_blocks(info, rows, hidden, dst):
    res = nn(rows, hidden[...]).astype(BF16)
    cols = res.shape[0] // 2
    for y in range(2):
        for x in range(2):
            dst.at[y, 0][x ^ (info[0] % 2)] = res[
                y * cols : (y + 1) * cols, x * LANES : (x + 1) * LANES
            ]


def out_ff_send_kernel(
    lp, lq, segs, info, d_pooled, output, lgain, hidden,
    d_output, d_ffn, gain_grad, turned, send,
):
    total = lp + lq
    rows = output.shape[1] // NB
    half = 2 * rows

    @pl.when(pl.program_id(0) == 0)
    def _():
        lo, hi = seg_bounds(info, segs, lp, (1, 2 * segs), 1)
        lo_c, hi_c = seg_bounds(info, segs, lp, (2 * segs, 1), 0)
        at = lax.broadcasted_iota(jnp.int32, (total, 2 * segs), 0)
        hot = jnp.where((at >= lo) & (at < hi), 1.0, 0.0)
        dy = nn(hot, d_pooled[...] / (hi_c - lo_c).astype(F32), precision=HIGHEST)
        dv, dg = rms_back(output[...], wide_row(lgain), dy)
        d_output[...] = dv
        gain_grad[...] = dg
        low = dv.astype(BF16)
        d_ffn[...] = low
        flipped = low.T
        for n in range(NB):
            other = n ^ info[1]
            at_row = (other % 2) * half + (other // 2) * rows
            turned[pl.ds(pl.multiple_of(at_row, rows), rows), :] = flipped[
                n * rows : (n + 1) * rows
            ]

    out_ff_blocks(info, turned[half:, :], hidden, send)


def out_ff_keep_kernel(info, turned, hidden, keep):
    out_ff_blocks(info, turned[: turned.shape[0] // 2, :], hidden, keep)


def turn_rows(dst, value, wide):
    rows = value.shape[1] // WB
    flipped = value.T
    for w in range(WB):
        dst[pl.ds(pl.multiple_of((w ^ wide) * rows, rows), rows), :] = flipped[
            w * rows : (w + 1) * rows
        ]


def ffn_step(d_ffn, w_back, slope, w_in, turned, total, out):
    d_up = (nt(d_ffn[...], w_back[...]) * slope[...].astype(F32)).astype(BF16)
    total[...] += nt(d_up, w_in[...])
    res = nn(turned[...], d_up).astype(BF16)
    rows = res.shape[0] // WB
    for half in range(2):
        out[pl.program_id(0), :, half * rows : (half + 1) * rows, :] = res[
            :, half * LANES : (half + 1) * LANES
        ].reshape(WB, rows, LANES)


def ffn_back_send_kernel(
    info, d_ffn, w_back, slope, w_in, normed_two, send, turned, total
):
    @pl.when(pl.program_id(0) == 0)
    def _():
        turn_rows(turned, normed_two[...], info[0])
        total[...] = jnp.zeros_like(total)

    ffn_step(d_ffn, w_back, slope, w_in, turned, total, send)


def ffn_back_keep_kernel(
    info, d_ffn, w_back, slope, w_in, turned, so_far, d_output, residual, fgain, ctx, w_out,
    keep, d_resid, gain_grad, d_ctx, send_o, keep_o, total, turned_ctx,
):
    step = pl.program_id(0)

    @pl.when(step == 0)
    def _():
        total[...] = so_far[...]

    ffn_step(d_ffn, w_back, slope, w_in, turned, total, keep)

    @pl.when(step == pl.num_programs(0) - 1)
    def _():
        width = residual.shape[1]
        rows, cols = width // WB, width // NB
        dv, dg = rms_back(residual[...], wide_row(fgain), total[...])
        dr = d_output[...] + dv
        d_resid[...] = dr
        gain_grad[...] = dg
        da = dr.astype(BF16)
        d_ctx[...] = nt(da, w_out[...]).astype(BF16)
        turn_rows(turned_ctx, ctx[...], info[0])
        grad = nn(turned_ctx[...], da)
        for n in range(NB):
            part = grad[:, n * cols : (n + 1) * cols].reshape(WB, rows, cols)
            part = jnp.concatenate([part[:, : rows // 2], part[:, rows // 2 :]], axis=2)
            part = part.astype(BF16)
            y = (n // 2) ^ (info[1] // 2)

            @pl.when((n % 2) == (info[1] % 2))
            def _():
                keep_o[y] = part

            @pl.when((n % 2) != (info[1] % 2))
            def _():
                send_o[y] = part


def attn_back_kernel(
    dk, lp, lq, info, q, k, v, d_ctx, probs_p, probs_q, d_q, d_k, d_v, sums
):
    step = pl.program_id(0)

    @pl.when(step == 0)
    def _():
        sums[...] = jnp.zeros_like(sums)

    units = []
    for hh in range(2):
        cols = slice(hh * dk, (hh + 1) * dk)
        units.append((hh, cols, slice(0, lp), lp, probs_p))
        units.append((hh, cols, slice(lp, lp + lq), lq, probs_q))
    d_probs = [nt(v[here, cols], d_ctx[here, cols]) for _, cols, here, _, _ in units]
    tiles = [[jnp.zeros((CH, CH), F32)] * (2 * lp // CH) for _ in range(2)]
    lows = []
    for (hh, _, _, span, probs), d_prob in zip(units, d_probs):
        p = probs[hh].astype(F32)
        t = p * d_prob
        ds = t - p * jnp.sum(t, axis=0, keepdims=True)
        lows.append(ds.astype(BF16))
        for a in range(span // CH):
            for b in range(span // CH):
                at = b + lp // CH - a
                piece = ds[a * CH : (a + 1) * CH, b * CH : (b + 1) * CH]
                tiles[hh][at] = tiles[hh][at] + piece
    for (hh, cols, here, _, probs), low in zip(units, lows):
        d_q[here, cols] = tn(low, k[here, cols]).astype(BF16)
        d_k[here, cols] = nn(low, q[here, cols]).astype(BF16)
        d_v[here, cols] = nn(probs[hh], d_ctx[here, cols]).astype(BF16)
    at_i = lax.broadcasted_iota(jnp.int32, (CH, CH), 0)
    at_j = lax.broadcasted_iota(jnp.int32, (CH, CH), 1)
    mirror = jnp.where(at_i + at_j == CH - 1, 1.0, 0.0).astype(BF16)
    for hh in range(2):
        flipped = nn(mirror, jnp.concatenate(tiles[hh], axis=1).astype(BF16))
        turn = pltpu.roll(flipped, 0, 1, stride=1, stride_axis=0)
        sums[pl.ds(2 * step + hh, 1), :] = jnp.sum(turn, axis=0, keepdims=True)


def qkv_grad_kernel(
    lp, heads, info, normed, d_q, d_k, d_v, wq, wk, wv, gain, g_ffn, g_final, sums,
    send, keep, turned, blocks, column,
):
    width = normed.shape[1]
    rows, cols = width // WB, width // NB
    turn_rows(turned, normed[...], info[0])
    left = turned[...]
    gq, gk, gv = (nn(left, r[...]) for r in (d_q, d_k, d_v))
    for n in range(NB):
        here = slice(n * cols, (n + 1) * cols)
        both = jnp.concatenate([gq[:, here], gk[:, here]], axis=1).astype(BF16)
        blocks[n, :, :rows, :] = both.reshape(WB, rows, LANES)
        part = gv[:, here].reshape(WB, rows, cols)
        part = jnp.concatenate([part[:, : rows // 2], part[:, rows // 2 :]], axis=2)
        blocks[n, :, rows:, :] = part.astype(BF16)
    size = blocks.shape[1] * blocks.shape[2]
    core, y0 = info[1] % 2, info[1] // 2
    for y in range(2):
        here = slice(y * size, (y + 1) * size)
        send[here, :] = blocks[(y ^ y0) * 2 + (1 - core)].reshape(size, LANES)
        keep[here, :] = blocks[(y ^ y0) * 2 + core].reshape(size, LANES)
    for w in range(WB):
        at = pl.ds(pl.multiple_of((w ^ info[0]) * rows, rows), rows)
        here = slice(w * rows, (w + 1) * rows)
        total = jnp.zeros((rows, 1), F32)
        for grad, weight in ((gq, wq), (gk, wk), (gv, wv)):
            total = total + jnp.sum(
                grad[here, :] * weight[at, :].astype(F32), axis=1, keepdims=True
            )
        column[at, :] = jnp.broadcast_to(total, (rows, column.shape[1]))
    g_attn = column[...].T[:1, :] / wide_row(gain)
    hot = bucket_hot(lp, CH - 1).astype(F32)
    bias = nt(sums[...], hot, precision=HIGHEST)
    pieces = []
    for grad in (g_attn, g_ffn[...], g_final[...]):
        pieces += [grad[:, i : i + LANES] for i in range(0, width, LANES)]
    pieces.append(jnp.concatenate([bias[h : h + 1, :] for h in range(heads)], axis=1))
    pieces.append(jnp.zeros((8 - len(pieces), LANES), F32))
    small = jnp.concatenate(pieces, axis=0)
    high = small.astype(BF16)
    small = jnp.concatenate([high.astype(F32), small - high.astype(F32)], axis=0).astype(BF16)
    send[2 * size :, :] = small
    keep[2 * size :, :] = small


def input_kernel(
    lp, info, d_q, d_k, d_v, wq, wk, wv, d_resid, xp, xq, gain, every, d_proj,
    grad_p, grad_q, proj_grad, full,
):
    step, last = pl.program_id(0), pl.num_programs(0) - 1
    width, size = xp.shape[1], xp.shape[0]
    dn = nt(d_q[...], wq[...]) + nt(d_k[...], wk[...]) + nt(d_v[...], wv[...])
    passages = step < lp // size
    x = jnp.where(passages, xp[...].astype(F32), xq[...].astype(F32))
    r = lax.rsqrt(jnp.mean(x * x, axis=-1, keepdims=True) + EPS)
    gdy = wide_row(gain) * dn
    inner = jnp.mean(gdy * x, axis=-1, keepdims=True)
    out = d_resid[...] + (r * gdy - x * (r * r * r * inner))

    @pl.when(passages)
    def _():
        grad_p[...] = out

    @pl.when(jnp.logical_not(passages))
    def _():
        grad_q[...] = out

    @pl.when(step == last)
    def _():
        full[...] = tn(every[:, :width], d_proj[...])
        rows, cols = proj_grad.shape
        mine = full[pl.ds(pl.multiple_of(info[0] * rows, 8), rows), :]
        for n in range(width // cols):

            @pl.when(info[1] == n)
            def _():
                proj_grad[...] = mine[:, n * cols : (n + 1) * cols]


class Info:
    def __init__(self, place, passages, queries, pairs):
        segs = passages.shape[1]
        self.at = [lambda: place[0], lambda: place[1]]
        self.at += [functools.partial(lambda r, i: r[0, i], passages, i) for i in range(segs)]
        self.at += [functools.partial(lambda r, i: r[0, i], queries, i) for i in range(segs)]
        self.at += [functools.partial(lambda r, i: r[i], pairs, i) for i in range(segs)]

    def __getitem__(self, i):
        return self.at[i]()


def call(
    kernel, grid, info, args, in_specs, outs, out_specs, scratch=(), flops=0, moved=0,
    vmem=16, after=(),
):
    count = len(args)

    def body(place, passages, queries, pairs, *refs):
        kernel(Info(place, passages, queries, pairs), *refs[:count], *refs[count + len(after) :])

    return pl.pallas_call(
        body,
        grid_spec=pltpu.PrefetchScalarGridSpec(
            num_scalar_prefetch=4,
            grid=grid,
            in_specs=list(in_specs) + [pl.BlockSpec(memory_space=pl.ANY)] * len(after),
            out_specs=out_specs,
            scratch_shapes=list(scratch),
        ),
        out_shape=outs,
        compiler_params=pltpu.CompilerParams(vmem_limit_bytes=vmem * 2**20),
        cost_estimate=pl.CostEstimate(flops=flops, bytes_accessed=moved, transcendentals=0),
    )(*info, *args, *after)


def hbm(array):
    return pltpu.with_memory_space_constraint(array, pltpu.HBM)


def near(*shape):
    return pl.BlockSpec(memory_space=pltpu.VMEM)


def whole(*shape):
    return pl.BlockSpec(shape, lambda *_: (0,) * len(shape), pipeline_mode=pl.Buffered(1))


def shaped(shape, dtype):
    return jax.ShapeDtypeStruct(shape, dtype)


def permute(array, bit, count):
    return lax.ppermute(array, AXES, [(i, i ^ bit) for i in range(count)])


CORE, Y, X, Z0, Z1 = 1, 2, 4, 8, 16
GATHER = (Y, X, Z0, Z1, CORE)


def take(array, dims, bit, which):
    return lax.index_in_dim(array, which, dims.index(bit), keepdims=False)


def encode(values):
    high = lax.reduce_precision(values, 8, 7)
    return jnp.concatenate([high, values - high], axis=0).astype(BF16)


def decode(coded):
    half = coded.shape[0] // 2
    return coded[:half].astype(F32) + coded[half:].astype(F32)


def sum_all(refs):
    parts = [r[...].astype(F32) for r in refs]
    while len(parts) > 1:
        parts = [a + b for a, b in zip(parts[::2], parts[1::2])]
    return parts[0]


def out_ff_finish_kernel(info, *refs):
    refs[-1][...] = sum_all(refs[:-1]).T


def in_ff_finish_kernel(info, *refs):
    *parts, in_ff, out_w = refs
    total = sum_all(parts)
    rows, cols = out_w.shape
    in_ff[...] = jnp.concatenate([total[:rows], total[rows : 2 * rows]], axis=1)
    out_w[...] = jnp.concatenate([total[2 * rows :, :cols], total[2 * rows :, cols:]], axis=0)


def qkv_finish_kernel(info, *refs):
    *parts, query_w, key_w, value_w = refs
    total = sum_all(parts)
    rows, cols = query_w.shape
    query_w[...] = total[:rows, :cols]
    key_w[...] = total[:rows, cols:]
    value_w[...] = jnp.concatenate([total[rows:, :cols], total[rows:, cols:]], axis=0)


class Scatter:
    def __init__(self, groups, count, quad=False):
        self.count, self.groups, self.quad = count, groups, quad
        self.sources = []
        self.small = None
        self.stage = -1

    def permute(self, array, bit):
        flat = permute(array.reshape(-1, LANES), bit, self.count)
        return flat.reshape(array.shape)

    def source(self, send, keep, rows):
        shape = (2, 2, 2, 2, rows, LANES)
        size = 16 * rows
        send, keep = send.reshape(-1, LANES), keep.reshape(-1, LANES)
        got = permute(send, CORE, self.count)
        if keep.shape[0] > size:
            self.small = encode(decode(keep[size:]) + decode(got[size:]))
        self.sources.append((keep[:size].reshape(shape), got[:size].reshape(shape)))

    def add(self):
        self.stage += 1
        if self.stage == 0:

            def cut(bit, which, part):
                dims = [Y, Z1, Z0, X]
                return jnp.concatenate(
                    [
                        take(self.sources[n][0][..., lo:hi, :], dims, bit, which)
                        + take(self.sources[n][1][..., lo:hi, :], dims, bit, which)
                        for n, lo, hi in part
                    ],
                    axis=-2,
                )

            self.first = [cut(b, 1, p) for b, p in zip((Y, X), self.groups)]
            self.rest = [cut(b, 0, p) for b, p in zip((Y, X), self.groups)]
        elif self.stage == 1:
            pairs = list(zip(self.rest, self.got))
            self.first = [
                pairs[0][0][:, :, 1] + pairs[0][1][:, :, 1],
                pairs[1][0][1] + pairs[1][1][1],
            ]
            self.rest = [
                pairs[0][0][:, :, 0] + pairs[0][1][:, :, 0],
                pairs[1][0][0] + pairs[1][1][0],
            ]
        elif self.stage == 2:

            def block(*at):
                return jnp.concatenate(
                    [r[at] + g[at] for r, g in zip(self.rest, self.got)], axis=-2
                )

            every = slice(None)
            if self.quad:
                self.first = [block(0, 1), block(1, 0), block(1, 1)]
                self.rest = block(0, 0)
            else:
                self.first = [block(every, 1)]
                self.rest = block(every, 0)
        else:
            self.first = [self.rest[1] + self.got[0][1]]
            self.rest = self.rest[0] + self.got[0][0]
        return self.first

    def send(self):
        last = (Z0, Z1, Z0 | Z1) if self.quad else (Z0,)
        bits = ((Y, X), (X, Y), last, (Z1,))[self.stage]
        self.got, coded = [], []
        for i, (first, bit) in enumerate(zip(self.first, bits)):
            if self.small is None or (self.stage < 2 and i > 0):
                self.got.append(self.permute(first, bit))
                continue
            rows = self.small.shape[0]
            flat = jnp.concatenate([self.small, first.reshape(-1, LANES)], axis=0)
            flat = permute(flat, bit, self.count)
            coded.append(decode(flat[:rows]))
            self.got.append(flat[rows:].reshape(first.shape))
        if self.small is not None:
            self.sums = decode(self.small) + coded[0]
            if len(coded) > 1:
                self.sums = self.sums + (coded[1] + coded[2])
            self.small = encode(self.sums)

    def parts(self):
        return [self.rest, *self.got]


def per_device(
    fast, n_wide, n_narrow,
    xp, xq, passage_lengths, query_lengths, pair_index, g_attn, w_query, w_key, w_value, w_out,
    bias_table, g_ffn, w_in, w_back, g_final, w_proj,
):
    lp, width = xp.shape
    lq = xq.shape[0]
    total = lp + lq
    heads = bias_table.shape[1]
    dk = width // heads
    ff = w_in.shape[1]
    segs = passage_lengths.shape[1]
    count = n_wide * n_narrow
    pairs = heads // 2
    rows, cols = width // WB, width // NB
    wide_at, narrow_at = lax.axis_index("wide"), lax.axis_index("narrow")
    place = jnp.stack([wide_at, narrow_at]) if fast else jnp.zeros((2,), jnp.int32)
    info = (place.astype(jnp.int32), passage_lengths, query_lengths, pair_index)
    mm = 2 * total * width * width
    act, act32 = shaped((total, width), BF16), shaped((total, width), F32)
    act_hbm = pltpu.HBM((total, width), BF16)

    tile = 256
    col_tile = pl.BlockSpec((width, tile), lambda i, *_: (0, i))
    act_tile = pl.BlockSpec((total, tile), lambda i, *_: (0, i))
    normed, q, k, v = call(
        qkv_kernel,
        (width // tile,),
        info,
        tuple(hbm(a) for a in (xp, xq, g_attn, w_query, w_key, w_value)),
        [whole(lp, width), whole(lq, width), whole(width), col_tile, col_tile, col_tile],
        [act_hbm, act_hbm, act_hbm, act_hbm],
        [whole(total, width), act_tile, act_tile, act_tile],
        flops=3 * mm,
        moved=10 * 2**20,
    )

    head_tile = pl.BlockSpec((total, 2 * dk), lambda i, *_: (0, i))
    probs_p, probs_q, ctx = call(
        functools.partial(attn_kernel, lp, lq, segs, dk),
        (pairs,),
        info,
        (bias_table, hbm(q), hbm(k), hbm(v)),
        [near(), head_tile, head_tile, head_tile],
        [pltpu.HBM((heads, lp, lp), BF16), pltpu.HBM((heads, lq, lq), BF16), act],
        [
            pl.BlockSpec((2, lp, lp), lambda i, *_: (i, 0, 0)),
            pl.BlockSpec((2, lq, lq), lambda i, *_: (i, 0, 0)),
            head_tile,
        ],
        [pltpu.VMEM((16, 2 * lp), F32)],
        flops=14 * 10**9,
        moved=13 * 2**20,
    )

    ff_tile = ff // NB
    w_in_spec = pl.BlockSpec((width, ff_tile), lambda i, *_: (0, i))
    w_back_spec = pl.BlockSpec((ff_tile, width), lambda i, *_: (i, 0))
    ff_spec = pl.BlockSpec((total, ff_tile), lambda i, *_: (0, i))
    message = width + 128
    residual, normed_two, hidden, slope, output, pooled = call(
        functools.partial(ffn_kernel, lp, lq, segs),
        (NB,),
        info,
        (ctx, xp, xq, w_out, g_ffn, hbm(w_in), hbm(w_back), g_final),
        [near(), near(), near(), near(), near(), w_in_spec, w_back_spec, near()],
        [
            act32, act, pltpu.HBM((total, ff), BF16), pltpu.HBM((total, ff), BF16), act32,
            shaped((2 * segs, message), BF16),
        ],
        [near(), near(), ff_spec, ff_spec, near(), near()],
        flops=9 * mm,
        moved=30 * 2**20,
        vmem=24,
    )

    if fast:
        one = jnp.concatenate([pooled] + [permute(pooled, b, count) for b in (Y, X, X | Y)], axis=0)
        two = jnp.concatenate([one] + [permute(one, b, count) for b in (Z0, Z1, Z0 | Z1)], axis=0)
        every = 2 * two.shape[0]
        loss, d_proj, d_pooled, gathered = call(
            functools.partial(loss_kernel, segs, GATHER),
            (1,),
            info,
            (two, permute(two, CORE, count), w_proj),
            [near(), near(), near()],
            [
                shaped((2 * segs, 128), F32), shaped((every, width), BF16),
                shaped((2 * segs, width), F32), shaped((every, message), BF16),
            ],
            [near(), near(), near(), near()],
            flops=10**9,
            moved=2**20,
        )
        query_loss = loss[segs:, 0]
    else:
        gathered = lax.all_gather(pooled, AXES, axis=0, tiled=True)
        every = gathered.shape[0]
        block = jnp.arange(every, dtype=jnp.int32) // (2 * segs)
        loss, d_proj = loss_math(segs, block[:, None], block[None, :], gathered, w_proj)
        mine = (wide_at * n_narrow + narrow_at) * 2 * segs
        query_loss = lax.dynamic_slice_in_dim(loss, mine + segs, segs, 0)[:, 0]
        d_pooled = nt(lax.dynamic_slice_in_dim(d_proj, mine, 2 * segs, 0), w_proj)

    part1 = (2, WB // 2, 2, cols, LANES)
    block1 = pl.BlockSpec((2, 1, 2, cols, LANES), lambda i, *_: (0, i, 0, 0, 0))
    hidden_spec = pl.BlockSpec((total, 2 * LANES), lambda i, s, *_: (0, i ^ (s[0] // 2)))
    d_output, d_ffn, final_gain_grad, turned_ff, send1 = call(
        functools.partial(out_ff_send_kernel, lp, lq, segs),
        (WB // 2,),
        info,
        (d_pooled, output, g_final, hbm(hidden)),
        [near(), near(), near(), hidden_spec],
        [act32, act, shaped((1, width), F32), shaped((width, total), BF16), shaped(part1, BF16)],
        [near(), near(), near(), near(), block1],
        flops=3 * mm,
        moved=10 * 2**20,
    )
    (keep1,) = call(
        out_ff_keep_kernel,
        (WB // 2,),
        info,
        (turned_ff, hbm(hidden)),
        [near(), hidden_spec],
        [shaped(part1, BF16)],
        [block1],
        flops=2 * mm,
        moved=8 * 2**20,
    )

    def waits(*lists):
        return [a for arrays in lists for a in arrays] if fast else []

    sc1 = Scatter((((0, 0, cols // 2),), ((0, cols // 2, cols),)), count)
    if fast:
        sc1.source(send1, keep1, cols)

    def turn(i, s):
        return (((i % 2) * 2) + (1 - i // 2)) ^ s[1]

    size2, size_o = 2 * rows, rows // 2
    part2 = shaped((2, WB, size2, LANES), BF16)
    part_o = shaped((2, WB, size_o, LANES), BF16)

    def tiles_at(first):
        return [
            near(),
            pl.BlockSpec((ff_tile, width), lambda i, s, *_: (turn(i + first, s), 0)),
            pl.BlockSpec((total, ff_tile), lambda i, s, *_: (0, turn(i + first, s))),
            pl.BlockSpec((width, ff_tile), lambda i, s, *_: (0, turn(i + first, s))),
        ]

    after = []
    if fast:
        after = sc1.add()
        sc1.send()
    send2, turned, so_far = call(
        ffn_back_send_kernel,
        (NB // 2,),
        info,
        (d_ffn, hbm(w_back), hbm(slope), hbm(w_in), normed_two),
        tiles_at(0) + [near()],
        [part2, shaped((width, total), BF16), act32],
        [near(), near(), near()],
        flops=6 * mm,
        moved=16 * 2**20,
        vmem=16,
        after=waits(after),
    )
    sc2 = Scatter((((0, 0, 128),), ((0, 128, size2), (1, 0, size_o))), count)
    after = []
    if fast:
        after = sc1.add()
        sc1.send()
    keep2, d_resid, ffn_gain_grad, d_ctx, send_o, keep_o = call(
        ffn_back_keep_kernel,
        (NB // 2,),
        info,
        (
            d_ffn, hbm(w_back), hbm(slope), hbm(w_in), turned, so_far, d_output, residual, g_ffn,
            ctx, w_out,
        ),
        tiles_at(NB // 2) + [near()] * 7,
        [part2, act32, shaped((1, width), F32), act, part_o, part_o],
        [near()] * 6,
        [pltpu.VMEM((total, width), F32), pltpu.VMEM((width, total), BF16)],
        flops=8 * mm,
        moved=20 * 2**20,
        vmem=18,
        after=waits(after),
    )
    if fast:
        sc2.source(send2, keep2, size2)
        sc2.source(send_o, keep_o, size_o)

    after = []
    if fast:
        after = sc1.add() + sc2.add()
        sc1.send()
        sc2.send()
    d_q, d_k, d_v, sums = call(
        functools.partial(attn_back_kernel, dk, lp, lq),
        (pairs,),
        info,
        (hbm(q), hbm(k), hbm(v), d_ctx, hbm(probs_p), hbm(probs_q)),
        [head_tile] * 4
        + [pl.BlockSpec((2, span, span), lambda i, *_: (i, 0, 0)) for span in (lp, lq)],
        [act_hbm, act_hbm, act_hbm, shaped((16, 2 * lp), F32)],
        [head_tile, head_tile, head_tile, near()],
        flops=8 * 10**9,
        moved=16 * 2**20,
        after=waits(after),
    )

    after = []
    if fast:
        after = sc1.add() + sc2.add()
        sc1.send()
        sc2.send()
    size3 = rows + rows // 2
    flat3 = shaped((16 * size3 + 16, LANES), BF16)
    send3, keep3 = call(
        functools.partial(qkv_grad_kernel, lp, heads),
        (1,),
        info,
        (
            hbm(normed), hbm(d_q), hbm(d_k), hbm(d_v), w_query, w_key, w_value, g_attn,
            ffn_gain_grad, final_gain_grad, sums,
        ),
        [whole(total, width)] * 4 + [near()] * 7,
        [flat3, flat3],
        [near(), near()],
        [
            pltpu.VMEM((width, total), BF16), pltpu.VMEM((NB, WB, size3, LANES), BF16),
            pltpu.VMEM((width, 128), F32),
        ],
        flops=3 * mm,
        moved=9 * 2**20,
        vmem=24,
        after=waits(after),
    )

    after = []
    own_rows, own_cols = width // WB, width // NB
    square = shaped((own_rows, own_cols), F32)
    if fast:
        after = sc2.add()
        sc2.send()
        sc3 = Scatter((((0, 0, 80),), ((0, 80, size3),)), count, quad=True)
        sc3.source(send3, keep3, size3)
        after = after + sc3.add()
        sc3.send()
    size = lq
    steps_p = lp // size

    def p_at(i, *_):
        return (jnp.minimum(i, steps_p - 1), 0)

    def q_at(i, *_):
        return (jnp.maximum(i - steps_p, 0), 0)

    row_tile = pl.BlockSpec((size, width), lambda i, *_: (i, 0))
    grad_p, grad_q, proj_grad = call(
        functools.partial(input_kernel, lp),
        (total // size,),
        info,
        (
            hbm(d_q), hbm(d_k), hbm(d_v), w_query, w_key, w_value, hbm(d_resid), hbm(xp), hbm(xq),
            g_attn, gathered[:256], d_proj[:256],
        ),
        [row_tile, row_tile, row_tile, near(), near(), near(), row_tile]
        + [pl.BlockSpec((size, width), p_at), pl.BlockSpec((size, width), q_at)]
        + [near()] * 3,
        [shaped((lp, width), F32), shaped((lq, width), F32), square],
        [pl.BlockSpec((size, width), p_at), pl.BlockSpec((size, width), q_at), near()],
        [pltpu.VMEM((width, width), F32)],
        flops=4 * mm,
        moved=14 * 2**20,
        vmem=20,
        after=waits(after),
    )

    if fast:

        def finish(kernel, parts, outs, after=()):
            return call(
                kernel, (1,), info, parts, [near()] * len(parts), outs, [near()] * len(outs),
                flops=10**6, moved=2**20, after=after,
            )

        after = sc3.add()
        sc3.send()
        (out_ff,) = finish(
            out_ff_finish_kernel, sc1.parts(), [shaped((ff // WB, cols), F32)], after
        )
        sc2.add()
        sc2.send()
        after = sc3.add()
        sc3.send()
        in_ff, out_w = finish(
            in_ff_finish_kernel, sc2.parts(), [shaped((rows, ff // NB), F32), square], after
        )
        query_w, key_w, value_w = finish(qkv_finish_kernel, sc3.parts(), [square] * 3)
        smalls = sc3.sums
    else:
        own_rows, own_cols = width // n_wide, width // n_narrow
        left = lax.dynamic_slice(gathered, (0, wide_at * own_rows), (every, own_rows))
        right = lax.dynamic_slice(d_proj, (0, narrow_at * own_cols), (every, own_cols))
        proj_grad = tn(left, right)

        def blocks(send, keep):
            both = jnp.stack([keep, send], axis=1).astype(F32)
            return both.reshape((NB, WB) + both.shape[-2:])

        def spread(matrix):
            matrix = lax.psum_scatter(matrix, "wide", scatter_dimension=0, tiled=True)
            return lax.psum_scatter(matrix, "narrow", scatter_dimension=1, tiled=True)

        def side(part):
            half = part.shape[2] // 2
            return jnp.concatenate([part[:, :, :half], part[:, :, half:]], axis=3)

        def stack(part):
            half = part.shape[3] // 2
            return jnp.concatenate([part[..., :half], part[..., half:]], axis=2)

        def matrix(part):
            return part.transpose(1, 2, 0, 3).reshape(WB * part.shape[2], NB * part.shape[3])

        b1 = blocks(send1.reshape(2, WB, cols, LANES), keep1.reshape(2, WB, cols, LANES))
        b2 = blocks(send2, keep2)
        coded = keep3[16 * size3 :]
        b3 = blocks(*(a[: 16 * size3].reshape(2, WB, size3, LANES) for a in (send3, keep3)))
        out_ff = spread(matrix(b1.transpose(0, 1, 3, 2)))
        in_ff = spread(matrix(side(b2)))
        out_w = spread(matrix(stack(blocks(send_o, keep_o))))
        query_w = spread(matrix(b3[:, :, :rows, :cols]))
        key_w = spread(matrix(b3[:, :, :rows, cols:]))
        value_w = spread(matrix(stack(b3[:, :, rows:])))
        smalls = lax.psum(decode(coded), AXES)
    gains = smalls[: 3 * width // LANES].reshape(3, width)
    bias = smalls[3 * width // LANES].reshape(heads, BUCKETS).T
    return (
        query_loss, grad_p, grad_q, gains[0], query_w, key_w, value_w, out_w, bias, gains[1],
        in_ff, out_ff, gains[2], proj_grad,
    )


def solution(mesh):
    n_wide, n_narrow = mesh.shape["wide"], mesh.shape["narrow"]
    fast = (n_wide, n_narrow) == (WB, NB)
    rows = P(AXES, None)
    owned = P("wide", "narrow")
    return jax.shard_map(
        functools.partial(per_device, fast, n_wide, n_narrow),
        mesh=mesh,
        in_specs=(rows, rows, rows, rows, P(AXES)) + (P(),) * 11,
        out_specs=(
            P(AXES), rows, rows, P(), owned, owned, owned, owned, P(), P(),
            owned, owned, P(), owned,
        ),
        check_vma=False,
    )
```

```python
import functools

import jax
import jax.numpy as jnp
from jax import lax
from jax.experimental import pallas as pl
from jax.experimental.pallas import tpu as pltpu
from jax.sharding import PartitionSpec as P

BUCKETS = 32
MAX_DIST = 128
SCALE = 0.02
EPS = 1e-06
GELU = 0.7978845608028654
CUBE = 0.044715
HIGHEST = lax.Precision.HIGHEST
F32 = jnp.float32
BF16 = jnp.bfloat16
AXES = ("wide", "narrow")
NB = 4
WB = 8
CH = 128
LANES = 384
SMALL = 8


def bucket_edges():
    half = BUCKETS // 2
    exact = half // 2
    levels = half - exact
    ratio = MAX_DIST // exact
    edges = []
    for step in range(1, levels):
        target = exact**levels * ratio**step
        candidate = exact
        while candidate**levels < target:
            candidate += 1
        edges.append(candidate)
    return edges


def nn(a, b, **kw):
    return lax.dot_general(a, b, (((1,), (0,)), ((), ())), preferred_element_type=F32, **kw)


def tn(a, b):
    return lax.dot_general(a, b, (((0,), (0,)), ((), ())), preferred_element_type=F32)


def nt(a, b, **kw):
    return lax.dot_general(a, b, (((1,), (1,)), ((), ())), preferred_element_type=F32, **kw)


def bucket_hot(span, shift=0):
    shape = (BUCKETS, 2 * span)
    rel = lax.broadcasted_iota(jnp.int32, shape, 1) - shift
    rel = span - jnp.where(rel < 0, rel + 2 * span, rel)
    dist = jnp.abs(rel)
    half = BUCKETS // 2
    exact = half // 2
    far = jnp.full(shape, exact, jnp.int32)
    for edge in bucket_edges():
        far = far + jnp.where(dist >= edge, 1, 0)
    far = jnp.minimum(far, half - 1)
    bucket = jnp.where(dist < exact, dist, far) + jnp.where(rel > 0, half, 0)
    return bucket == lax.broadcasted_iota(jnp.int32, shape, 0)


def seg_bounds(info, segs, span, shape, axis):
    at = lax.broadcasted_iota(jnp.int32, shape, axis)
    lo = jnp.zeros(shape, jnp.int32)
    hi = jnp.zeros(shape, jnp.int32)
    for tower in range(2):
        start = tower * span
        for s in range(segs):
            size = info[2 + tower * segs + s]
            here = at == tower * segs + s
            lo = jnp.where(here, start, lo)
            hi = jnp.where(here, start + size, hi)
            start = start + size
    return lo, hi


def seg_of(info, tower, segs, shape, axis):
    at = lax.broadcasted_iota(jnp.int32, shape, axis)
    seg = jnp.zeros(shape, jnp.int32)
    end = 0
    for s in range(segs - 1):
        end = end + info[2 + tower * segs + s]
        seg = seg + jnp.where(at >= end, 1, 0)
    return seg


def rms(v, gain):
    return v * lax.rsqrt(jnp.mean(v * v, axis=-1, keepdims=True) + EPS) * gain


def rms_back(v, gain, dy):
    r = lax.rsqrt(jnp.mean(v * v, axis=-1, keepdims=True) + EPS)
    gdy = gain * dy
    inner = jnp.mean(gdy * v, axis=-1, keepdims=True)
    return r * gdy - v * (r * r * r * inner), jnp.sum(dy * v * r, axis=0, keepdims=True)


def wide_row(gain):
    return gain[...].astype(F32).reshape(1, gain.shape[0])


def qkv_kernel(info, xp, xq, gain, wq, wk, wv, normed, q, k, v):
    lp = xp.shape[0]

    @pl.when(pl.program_id(0) == 0)
    def _():
        g = wide_row(gain)
        normed[:lp, :] = rms(xp[...].astype(F32), g).astype(BF16)
        normed[lp:, :] = rms(xq[...].astype(F32), g).astype(BF16)

    n = normed[...]
    q[...] = nn(n, wq[...]).astype(BF16)
    k[...] = nn(n, wk[...]).astype(BF16)
    v[...] = nn(n, wv[...]).astype(BF16)


def attn_kernel(lp, lq, segs, dk, info, table, q, k, v, probs_p, probs_q, ctx, rows):
    @pl.when(pl.program_id(0) == 0)
    def _():
        heads = table.shape[1]
        rows[:heads, :] = tn(table[...], bucket_hot(lp).astype(F32).astype(BF16))

    units = []
    for hh in range(2):
        row = rows[pl.ds(2 * pl.program_id(0) + hh, 1), :]
        bias = pltpu.roll(jnp.broadcast_to(row, (CH, 2 * lp)), 0, 1, stride=1, stride_axis=0)
        cols = slice(hh * dk, (hh + 1) * dk)
        units.append((hh, bias, cols, 0, 0, lp, probs_p))
        units.append((hh, bias, cols, 1, lp, lq, probs_q))
    scores = []
    for hh, bias, cols, tower, off, span, probs in units:
        here = slice(off, off + span)
        s = nt(k[here, cols], q[here, cols])
        s = s + jnp.concatenate(
            [bias[:, lp - r0 : lp - r0 + span] for r0 in range(0, span, CH)], axis=0
        )
        seg_j = seg_of(info, tower, segs, (span, 1), 0)
        seg_i = seg_of(info, tower, segs, (1, span), 1)
        scores.append(jnp.where(seg_i == seg_j, s, -1000000000.0))
    lows = []
    for (hh, _, _, _, _, _, probs), s in zip(units, scores):
        e = jnp.exp(s - jnp.max(s, axis=0, keepdims=True))
        p = e * (1.0 / jnp.sum(e, axis=0, keepdims=True))
        p = p.astype(BF16)
        probs[hh] = p
        lows.append(p)
    for (_, _, cols, _, off, span, _), p in zip(units, lows):
        ctx[off : off + span, cols] = tn(p, v[off : off + span, cols]).astype(BF16)


def ffn_kernel(
    lp, lq, segs, info, ctx, xp, xq, w_out, fgain, w_in, w_back, lgain,
    residual, normed_two, hidden, slope, output, pooled,
):
    step = pl.program_id(0)
    total = lp + lq

    @pl.when(step == 0)
    def _():
        g = wide_row(fgain)
        for x, off, span in ((xp, 0, lp), (xq, lp, lq)):
            here = slice(off, off + span)
            res = x[...].astype(F32) + nn(ctx[here, :], w_out[...])
            residual[here, :] = res
            output[here, :] = res
            normed_two[here, :] = rms(res, g).astype(BF16)

    part = 256
    for r0 in range(0, total, part):
        here = slice(r0, r0 + part)
        u = nn(normed_two[here, :], w_in[...])
        uu = u * u
        t = jnp.tanh(u * (GELU + (GELU * CUBE) * uu))
        half = 0.5 + 0.5 * t
        h = (u * half).astype(BF16)
        hidden[here, :] = h
        slope[here, :] = (
            half + (0.5 * u) * (1.0 - t * t) * (GELU + (3.0 * GELU * CUBE) * uu)
        ).astype(BF16)
        output[here, :] += nn(h, w_back[...])

    @pl.when(step == pl.num_programs(0) - 1)
    def _():
        final = rms(output[...], wide_row(lgain))
        lo, hi = seg_bounds(info, segs, lp, (2 * segs, 1), 0)
        at = lax.broadcasted_iota(jnp.int32, (2 * segs, total), 1)
        hot = jnp.where((at >= lo) & (at < hi), 1.0, 0.0)
        mean = nn(hot, final, precision=HIGHEST) / (hi - lo).astype(F32)
        width = final.shape[1]
        pooled[:, :width] = mean.astype(BF16)
        shape = (2 * segs, pooled.shape[1] - width)
        at_row = lax.broadcasted_iota(jnp.int32, shape, 0)
        at_col = lax.broadcasted_iota(jnp.int32, shape, 1)
        code = jnp.zeros(shape, jnp.int32)
        for s in range(segs):
            pair = info[2 + 2 * segs + s]
            code = jnp.where((at_row == segs + s) & (at_col == 0), pair // 64, code)
            code = jnp.where((at_row == segs + s) & (at_col == 1), pair % 64, code)
        pooled[:, width:] = code.astype(F32).astype(BF16)


def loss_math(segs, block_row, block_col, gathered, w_proj):
    count = gathered.shape[0]
    width = w_proj.shape[0]
    low = gathered[:, :width]
    code = gathered[:, width:].astype(F32)
    pair = code[:, 0:1] * 64.0 + code[:, 1:2]
    row = lax.broadcasted_iota(jnp.int32, (count, 1), 0) % (2 * segs)
    col = lax.broadcasted_iota(jnp.int32, (1, count), 1) % (2 * segs)
    number = (block_col * segs + col).astype(F32)
    is_query = row >= segs
    is_passage = col < segs
    proj = nn(low, w_proj)
    scale = lax.rsqrt(jnp.sum(proj * proj, axis=-1, keepdims=True) + EPS)
    embed = proj * scale
    embed_low = embed.astype(BF16)
    sims = nt(embed_low, embed_low) / SCALE
    masked = jnp.where(is_passage, sims, -1e30)
    top = jnp.max(masked, axis=1, keepdims=True)
    expo = jnp.where(is_passage, jnp.exp(masked - top), 0.0)
    total = jnp.sum(expo, axis=1, keepdims=True)
    hot = jnp.where(is_passage & (number == pair), 1.0, 0.0)
    loss = top + jnp.log(total) - jnp.sum(hot * sims, axis=1, keepdims=True)
    d_sims = jnp.where(is_query, (expo / total - hot) / SCALE, 0.0)
    d_embed = nn(d_sims + d_sims.T, embed_low.astype(F32), precision=HIGHEST)
    d_proj = (d_embed - embed * jnp.sum(embed * d_embed, axis=-1, keepdims=True)) * scale
    return loss, d_proj.astype(BF16)


def loss_kernel(segs, bits, info, near, far, w_proj, loss, d_proj, d_pooled, every):
    gathered = jnp.concatenate([near[...], far[...]], axis=0)
    every[...] = gathered
    count = gathered.shape[0]

    def device(shape, axis):
        place = lax.broadcasted_iota(jnp.int32, shape, axis) // (2 * segs)
        other = jnp.zeros(shape, jnp.int32)
        for at, bit in enumerate(bits):
            other = other + ((place >> at) & 1) * bit
        return other ^ (info[0] * NB + info[1])

    value, d_low = loss_math(
        segs, device((count, 1), 0), device((1, count), 1), gathered, w_proj[...]
    )
    flat = jnp.broadcast_to(value[: 2 * segs], (2 * segs, 128)).T
    loss[...] = flat[:1, segs : 2 * segs].reshape(segs)
    d_proj[...] = d_low
    d_pooled[...] = nt(d_low[: 2 * segs], w_proj[...])


def out_ff_blocks(info, rows, hidden, dst):
    res = nn(rows, hidden[...]).astype(BF16)
    cols = res.shape[0] // 2
    for y in range(2):
        for x in range(2):
            dst.at[y, 0][x ^ (info[0] % 2)] = res[
                y * cols : (y + 1) * cols, x * LANES : (x + 1) * LANES
            ]


def out_ff_send_kernel(
    lp, lq, segs, info, d_pooled, output, lgain, hidden,
    d_output, d_ffn, gain_grad, turned, send,
):
    total = lp + lq
    rows = output.shape[1] // NB
    half = 2 * rows

    @pl.when(pl.program_id(0) == 0)
    def _():
        lo, hi = seg_bounds(info, segs, lp, (1, 2 * segs), 1)
        lo_c, hi_c = seg_bounds(info, segs, lp, (2 * segs, 1), 0)
        at = lax.broadcasted_iota(jnp.int32, (total, 2 * segs), 0)
        hot = jnp.where((at >= lo) & (at < hi), 1.0, 0.0)
        dy = nn(hot, d_pooled[...] / (hi_c - lo_c).astype(F32), precision=HIGHEST)
        dv, dg = rms_back(output[...], wide_row(lgain), dy)
        d_output[...] = dv
        gain_grad[...] = dg
        low = dv.astype(BF16)
        d_ffn[...] = low
        flipped = low.T
        for n in range(NB):
            other = n ^ info[1]
            at_row = (other % 2) * half + (other // 2) * rows
            turned[pl.ds(pl.multiple_of(at_row, rows), rows), :] = flipped[
                n * rows : (n + 1) * rows
            ]

    out_ff_blocks(info, turned[half:, :], hidden, send)


def out_ff_keep_kernel(info, turned, hidden, keep):
    out_ff_blocks(info, turned[: turned.shape[0] // 2, :], hidden, keep)


def turn_rows(dst, value, wide):
    rows = value.shape[1] // WB
    flipped = value.T
    for w in range(WB):
        dst[pl.ds(pl.multiple_of((w ^ wide) * rows, rows), rows), :] = flipped[
            w * rows : (w + 1) * rows
        ]


def ffn_tile(d_ffn, w_back, slope, w_in, turned):
    d_up = (nt(d_ffn[...], w_back[...]) * slope[...].astype(F32)).astype(BF16)
    res = nn(turned[...], d_up).astype(BF16)
    rows = res.shape[0] // WB
    blocks = jnp.concatenate(
        [
            res[:, half * LANES : (half + 1) * LANES].reshape(WB, rows, LANES)
            for half in range(2)
        ],
        axis=1,
    )
    return nt(d_up, w_in[...]), blocks


def ffn_back_first_kernel(
    info, d_ffn, w_back, slope, w_in, normed_two, send, keep, turned, total
):
    step = pl.program_id(0)

    @pl.when(step == 0)
    def _():
        turn_rows(turned, normed_two[...], info[0])
        total[...] = jnp.zeros_like(total)

    part, blocks = ffn_tile(d_ffn, w_back, slope, w_in, turned)
    total[...] += part

    @pl.when(step < 2)
    def _():
        send[step] = blocks

    @pl.when(step == 2)
    def _():
        keep[...] = blocks


def ffn_back_last_kernel(
    info, d_ffn, w_back, slope, w_in, turned, so_far, d_output, residual, fgain, ctx, w_out,
    keep, d_resid, gain_grad, d_ctx, send_o, keep_o, turned_ctx,
):
    part, blocks = ffn_tile(d_ffn, w_back, slope, w_in, turned)
    keep[...] = blocks
    width = residual.shape[1]
    rows, cols = width // WB, width // NB
    dv, dg = rms_back(residual[...], wide_row(fgain), so_far[...] + part)
    dr = d_output[...] + dv
    d_resid[...] = dr
    gain_grad[...] = dg
    da = dr.astype(BF16)
    d_ctx[...] = nt(da, w_out[...]).astype(BF16)
    turn_rows(turned_ctx, ctx[...], info[0])
    grad = nn(turned_ctx[...], da)
    for n in range(NB):
        part = grad[:, n * cols : (n + 1) * cols].reshape(WB, rows, cols)
        part = jnp.concatenate([part[:, : rows // 2], part[:, rows // 2 :]], axis=2)
        part = part.astype(BF16)
        y = (n // 2) ^ (info[1] // 2)

        @pl.when((n % 2) == (info[1] % 2))
        def _():
            keep_o[y] = part

        @pl.when((n % 2) != (info[1] % 2))
        def _():
            send_o[y] = part


def attn_back_kernel(
    dk, lp, lq, info, q, k, v, d_ctx, probs_p, probs_q, d_q, d_k, d_v, sums
):
    step = pl.program_id(0)

    @pl.when(step == 0)
    def _():
        sums[...] = jnp.zeros_like(sums)

    units = []
    for hh in range(2):
        cols = slice(hh * dk, (hh + 1) * dk)
        units.append((hh, cols, slice(0, lp), lp, probs_p))
        units.append((hh, cols, slice(lp, lp + lq), lq, probs_q))
    d_probs = [nt(v[here, cols], d_ctx[here, cols]) for _, cols, here, _, _ in units]
    tiles = [[jnp.zeros((CH, CH), F32)] * (2 * lp // CH) for _ in range(2)]
    lows = []
    for (hh, _, _, span, probs), d_prob in zip(units, d_probs):
        p = probs[hh].astype(F32)
        t = p * d_prob
        ds = t - p * jnp.sum(t, axis=0, keepdims=True)
        lows.append(ds.astype(BF16))
        for a in range(span // CH):
            for b in range(span // CH):
                at = b + lp // CH - a
                piece = ds[a * CH : (a + 1) * CH, b * CH : (b + 1) * CH]
                tiles[hh][at] = tiles[hh][at] + piece
    for (hh, cols, here, _, probs), low in zip(units, lows):
        d_q[here, cols] = tn(low, k[here, cols]).astype(BF16)
        d_k[here, cols] = nn(low, q[here, cols]).astype(BF16)
        d_v[here, cols] = nn(probs[hh], d_ctx[here, cols]).astype(BF16)
    at_i = lax.broadcasted_iota(jnp.int32, (CH, CH), 0)
    at_j = lax.broadcasted_iota(jnp.int32, (CH, CH), 1)
    mirror = jnp.where(at_i + at_j == CH - 1, 1.0, 0.0).astype(BF16)
    for hh in range(2):
        flipped = nn(mirror, jnp.concatenate(tiles[hh], axis=1).astype(BF16))
        turn = pltpu.roll(flipped, 0, 1, stride=1, stride_axis=0)
        sums[pl.ds(2 * step + hh, 1), :] = jnp.sum(turn, axis=0, keepdims=True)


def qkv_grad_kernel(
    lp, heads, info, normed, d_q, d_k, d_v, wq, wk, wv, gain, g_ffn, g_final, sums,
    send, keep, turned, blocks, column,
):
    width = normed.shape[1]
    rows, cols = width // WB, width // NB
    turn_rows(turned, normed[...], info[0])
    left = turned[...]
    gq, gk, gv = (nn(left, r[...]) for r in (d_q, d_k, d_v))
    for n in range(NB):
        here = slice(n * cols, (n + 1) * cols)
        both = jnp.concatenate([gq[:, here], gk[:, here]], axis=1).astype(BF16)
        blocks[n, :, :rows, :] = both.reshape(WB, rows, LANES)
        part = gv[:, here].reshape(WB, rows, cols)
        part = jnp.concatenate([part[:, : rows // 2], part[:, rows // 2 :]], axis=2)
        blocks[n, :, rows:, :] = part.astype(BF16)
    size = blocks.shape[1] * blocks.shape[2]
    core, y0 = info[1] % 2, info[1] // 2
    for y in range(2):
        here = slice(y * size, (y + 1) * size)
        send[here, :] = blocks[(y ^ y0) * 2 + (1 - core)].reshape(size, LANES)
        keep[here, :] = blocks[(y ^ y0) * 2 + core].reshape(size, LANES)
    for w in range(WB):
        at = pl.ds(pl.multiple_of((w ^ info[0]) * rows, rows), rows)
        here = slice(w * rows, (w + 1) * rows)
        total = jnp.zeros((rows, 1), F32)
        for grad, weight in ((gq, wq), (gk, wk), (gv, wv)):
            total = total + jnp.sum(
                grad[here, :] * weight[at, :].astype(F32), axis=1, keepdims=True
            )
        column[at, :] = jnp.broadcast_to(total, (rows, column.shape[1]))
    g_attn = column[...].T[:1, :] / wide_row(gain)
    hot = bucket_hot(lp, CH - 1).astype(F32)
    bias = nt(sums[...], hot, precision=HIGHEST)
    pieces = []
    for grad in (g_attn, g_ffn[...], g_final[...]):
        pieces += [grad[:, i : i + LANES] for i in range(0, width, LANES)]
    pieces.append(jnp.concatenate([bias[h : h + 1, :] for h in range(heads)], axis=1))
    pieces.append(jnp.zeros((SMALL - len(pieces), LANES), F32))
    small = jnp.concatenate(pieces, axis=0)
    small = encode(small)
    send[2 * size :, :] = small
    keep[2 * size :, :] = small


def input_grad(d_q, d_k, d_v, wq, wk, wv, d_resid, x, gain):
    dn = nt(d_q[...], wq[...]) + nt(d_k[...], wk[...]) + nt(d_v[...], wv[...])
    r = lax.rsqrt(jnp.mean(x * x, axis=-1, keepdims=True) + EPS)
    gdy = wide_row(gain) * dn
    inner = jnp.mean(gdy * x, axis=-1, keepdims=True)
    return d_resid[...] + (r * gdy - x * (r * r * r * inner))


def first_input_kernel(info, d_q, d_k, d_v, wq, wk, wv, d_resid, xp, gain, grad_p):
    grad_p[...] = input_grad(d_q, d_k, d_v, wq, wk, wv, d_resid, xp[...].astype(F32), gain)


def input_kernel(
    lp, info, d_q, d_k, d_v, wq, wk, wv, d_resid, xp, xq, gain, every, d_proj,
    grad_q, proj_grad, grad_p, full,
):
    step, last = pl.program_id(0), pl.num_programs(0) - 1
    width, size = xp.shape[1], xp.shape[0]
    passages = step < lp // size - 1
    x = jnp.where(passages, xp[...].astype(F32), xq[...].astype(F32))
    out = input_grad(d_q, d_k, d_v, wq, wk, wv, d_resid, x, gain)

    @pl.when(passages)
    def _():
        grad_p[...] = out

    @pl.when(jnp.logical_not(passages))
    def _():
        grad_q[...] = out

    @pl.when(step == last)
    def _():
        full[...] = tn(every[:, :width], d_proj[...])
        rows, cols = proj_grad.shape
        mine = full[pl.ds(pl.multiple_of(info[0] * rows, 8), rows), :]
        for n in range(width // cols):

            @pl.when(info[1] == n)
            def _():
                proj_grad[...] = mine[:, n * cols : (n + 1) * cols]


class Info:
    def __init__(self, place, passages, queries, pairs):
        segs = passages.shape[1]
        self.at = [lambda: place[0], lambda: place[1]]
        self.at += [functools.partial(lambda r, i: r[0, i], passages, i) for i in range(segs)]
        self.at += [functools.partial(lambda r, i: r[0, i], queries, i) for i in range(segs)]
        self.at += [functools.partial(lambda r, i: r[i], pairs, i) for i in range(segs)]

    def __getitem__(self, i):
        return self.at[i]()


def call(
    kernel, grid, info, args, in_specs, outs, out_specs, scratch=(), flops=0, moved=0,
    vmem=16, after=(), through=(), through_specs=(),
):
    count, more = len(args), len(after) + len(through)
    outs, out_specs = list(outs), list(out_specs)
    made = len(outs)
    aliases = {len(info) + count + len(after) + i: made + i for i in range(len(through))}
    outs += [(hbm_out if through_specs else shaped)(a.shape, a.dtype) for a in through]
    out_specs += through_specs or [pl.BlockSpec(memory_space=pl.ANY)] * len(through)
    hidden = 0 if through_specs else len(through)

    def body(*refs):
        scalars, refs = refs[: len(info)], refs[len(info) :]
        results = refs[count + more :]
        kernel(
            Info(*scalars) if scalars else None,
            *refs[:count],
            *results[:made],
            *results[made + hidden :],
        )

    return pl.pallas_call(
        body,
        grid_spec=pltpu.PrefetchScalarGridSpec(
            num_scalar_prefetch=len(info),
            grid=grid,
            in_specs=list(in_specs) + [pl.BlockSpec(memory_space=pl.ANY)] * more,
            out_specs=out_specs,
            scratch_shapes=list(scratch),
        ),
        out_shape=outs,
        input_output_aliases=aliases,
        compiler_params=pltpu.CompilerParams(vmem_limit_bytes=vmem * 2**20),
        cost_estimate=pl.CostEstimate(flops=flops, bytes_accessed=moved, transcendentals=0),
    )(*info, *args, *after, *through)


def hbm(array):
    return pltpu.with_memory_space_constraint(array, pltpu.HBM)


def near(*shape):
    return pl.BlockSpec(memory_space=pltpu.VMEM)


def whole(*shape):
    return pl.BlockSpec(shape, lambda *_: (0,) * len(shape), pipeline_mode=pl.Buffered(1))


def hbm_out(shape, dtype):
    return pltpu.HBM(shape, dtype)


def out_shape_of(out):
    return out.inner_aval.shape


def shaped(shape, dtype):
    return jax.ShapeDtypeStruct(shape, dtype)


def permute(array, bit, count):
    return lax.ppermute(array, AXES, [(i, i ^ bit) for i in range(count)])


CORE, Y, X, Z0, Z1 = 1, 2, 4, 8, 16
GATHER = (Y, X, Z0, Z1, CORE)


def own_sum(base, refs):
    parts = [r[b:, :].astype(F32) for b, r in zip(base, refs)]
    while len(parts) > 1:
        parts = [a + b for a, b in zip(parts[::2], parts[1::2])]
    return parts[0]


def out_ff_finish_kernel(base, info, *refs):
    refs[-1][...] = own_sum(base, refs[:-1])


def in_ff_finish_kernel(base, info, *refs):
    *parts, in_ff, out_w = refs
    total = own_sum(base, parts)
    rows, cols = out_w.shape
    in_ff[...] = jnp.concatenate([total[:rows], total[rows : 2 * rows]], axis=1)
    out_w[...] = jnp.concatenate([total[2 * rows :, :cols], total[2 * rows :, cols:]], axis=0)


def split_small(small, width, heads):
    per = width // LANES
    gains = [
        jnp.concatenate([small[g * per + i : g * per + i + 1] for i in range(per)], axis=1)
        for g in range(3)
    ]
    row = small[3 * per : 3 * per + 1]
    bias = [row[:, h * BUCKETS : (h + 1) * BUCKETS] for h in range(heads)]
    return gains, jnp.concatenate(bias, axis=0)


def qkv_finish_kernel(heads, base, info, *refs):
    rest, own, *got, query_w, key_w, value_w, gain_a, gain_f, gain_l, bias = refs
    total = own_sum(base, (rest, *got))
    rows, cols = query_w.shape
    query_w[...] = total[:rows, :cols]
    key_w[...] = total[:rows, cols:]
    value_w[...] = jnp.concatenate([total[rows:, :cols], total[rows:, cols:]], axis=0)
    small = [decode(r[: 2 * SMALL, :]) for r in (own, *got)]
    small = (small[0] + small[1]) + (small[2] + small[3])
    gains, table = split_small(small, gain_a.shape[0], heads)
    for ref, gain in zip((gain_a, gain_f, gain_l), gains):
        ref[...] = gain.reshape(gain.shape[1])
    bias[...] = table


def encode(values):
    high = values.astype(BF16).astype(F32)
    return jnp.concatenate([high, values - high], axis=0).astype(BF16)


def decode(coded):
    half = coded.shape[0] // 2
    return coded[:half].astype(F32) + coded[half:].astype(F32)


class Part:
    def __init__(self, arrays, base, dims, rows, lo=0, hi=None):
        self.arrays, self.base, self.dims, self.rows = arrays, base, dims, rows
        self.lo, self.hi = lo, rows if hi is None else hi

    def at(self, where):
        dims, which = self.dims, 0
        if len(self.arrays) > 1:
            which, dims = where[dims[0]], dims[1:]
        index = 0
        for bit in dims:
            index = index * 2 + where[bit]
        return self.arrays[which], self.base + index * self.rows + self.lo


def add_kernel(plans, info, *refs):
    outs = refs[len(refs) - len(plans) :]
    for (sums, small), out in zip(plans, outs):
        if small:
            total = decode(refs[small[0]][small[1] : small[1] + 2 * SMALL, :])
            total = total + decode(refs[small[2]][small[3] : small[3] + 2 * SMALL, :])
            out[: 2 * SMALL, :] = encode(total)
        for to, a, at_a, b, at_b, rows in sums:
            out[to : to + rows, :] = (
                refs[a][at_a : at_a + rows, :] + refs[b][at_b : at_b + rows, :]
            )


class Scatter:
    def __init__(self, groups, count, quad=False):
        self.count, self.groups, self.quad = count, groups, quad
        self.sources = []
        self.small = None
        self.stage = -1

    def source(self, send, keeps, rows, small=False):
        send = send.reshape(-1, LANES)
        keeps = [k.reshape(-1, LANES) for k in keeps]
        got = permute(send, CORE, self.count)
        self.sources.append((keeps, got, rows))
        if small:
            at = 16 * rows
            self.small = (keeps[0], at, got, at)

    def jobs(self):
        self.stage += 1
        stage = self.stage
        if stage == 0:
            dims = (Y, Z1, Z0, X)
            groups = [
                [
                    (
                        Part(self.sources[n][0], 0, dims, self.sources[n][2], lo, hi),
                        Part([self.sources[n][1]], 0, dims, self.sources[n][2], lo, hi),
                    )
                    for n, lo, hi in group
                ]
                for group in self.groups
            ]
        else:
            groups = [[pair] for pair in zip(self.rest, self.got)]
        if stage < 2:
            bits = ((Y, X), (X, Y))[stage]
            first = [(g, {b: 1}) for g, b in zip(groups, bits)]
            rest = [(g, {b: 0}) for g, b in zip(groups, bits)]
            self.bits = bits
        else:
            merged = [pair for group in groups for pair in group]
            if self.quad:
                self.bits = (Z0, Z1, Z0 | Z1)
                first = [(merged, {Z0: a, Z1: b}) for a, b in ((1, 0), (0, 1), (1, 1))]
                rest = [(merged, {Z0: 0, Z1: 0})]
            else:
                bit = (Z0, Z1)[stage - 2]
                self.bits = (bit,)
                first, rest = [(merged, {bit: 1})], [(merged, {bit: 0})]
        carry = [self.small is not None and (stage >= 2 or i == 0) for i in range(len(first))]
        return first, rest, carry

    def take(self, first, rest):
        self.first, self.rest, self.got = first, rest, []
        for part, bit in zip(first, self.bits):
            got = permute(part.arrays[0], bit, self.count)
            self.got.append(Part([got], part.base, part.dims, part.rows))
        if self.small is not None:
            self.small = (first[0].arrays[0], 0, self.got[0].arrays[0], 0)

    def finish(self):
        parts = [self.rest[0], *self.got]
        return [p.arrays[0] for p in parts], tuple(p.base for p in parts)


def advance(info, scatters, after=(), through=()):
    inputs, plans, shapes, slots = [], [], [], []

    def find(array):
        for i, known in enumerate(inputs):
            if known is array:
                return i
        inputs.append(array)
        return len(inputs) - 1

    for scatter in scatters:
        first, rest, carry = scatter.jobs()
        for n, (pairs, fixed) in enumerate(first + rest):
            dims = tuple(d for d in pairs[0][0].dims if d not in fixed)
            rows = sum(a.hi - a.lo for a, _ in pairs)
            base, small = 0, ()
            if n < len(first) and carry[n]:
                own, at_own, got, at_got = scatter.small
                base, small = 2 * SMALL, (find(own), at_own, find(got), at_got)
            sums = []
            for index in range(2 ** len(dims)):
                where = dict(fixed)
                for i, d in enumerate(reversed(dims)):
                    where[d] = (index >> i) & 1
                to = base + index * rows
                for a, b in pairs:
                    (array_a, row_a), (array_b, row_b) = a.at(where), b.at(where)
                    size = a.hi - a.lo
                    sums.append((to, find(array_a), row_a, find(array_b), row_b, size))
                    to += size
            plans.append((sums, small))
            shapes.append(shaped((base + 2 ** len(dims) * rows, LANES), BF16))
            slots.append((base, dims, rows))
        scatter.counts = (len(first), len(rest))
    outs = call(
        functools.partial(add_kernel, plans), (1,), info, inputs, [near()] * len(inputs), shapes,
        [near()] * len(shapes), flops=10**6, moved=2**20, after=after, through=through,
    )
    handed = outs[len(slots) :]
    parts = [Part([out], *slot) for out, slot in zip(outs, slots)]
    sent = []
    for scatter in scatters:
        many, more = scatter.counts
        scatter.take(parts[:many], parts[many : many + more])
        sent += [p.arrays[0] for p in parts[:many]]
        parts = parts[many + more :]
    return sent, handed


def per_device(
    fast, n_wide, n_narrow,
    xp, xq, passage_lengths, query_lengths, pair_index, g_attn, w_query, w_key, w_value, w_out,
    bias_table, g_ffn, w_in, w_back, g_final, w_proj,
):
    lp, width = xp.shape
    lq = xq.shape[0]
    total = lp + lq
    heads = bias_table.shape[1]
    dk = width // heads
    ff = w_in.shape[1]
    segs = passage_lengths.shape[1]
    count = n_wide * n_narrow
    pairs = heads // 2
    rows, cols = width // WB, width // NB
    wide_at, narrow_at = lax.axis_index("wide"), lax.axis_index("narrow")
    place = jnp.stack([wide_at, narrow_at]) if fast else jnp.zeros((2,), jnp.int32)
    info = (place.astype(jnp.int32), passage_lengths, query_lengths, pair_index)
    mm = 2 * total * width * width
    act, act32 = shaped((total, width), BF16), shaped((total, width), F32)
    act_hbm = pltpu.HBM((total, width), BF16)

    tile = 256
    col_tile = pl.BlockSpec((width, tile), lambda i, *_: (0, i))
    act_tile = pl.BlockSpec((total, tile), lambda i, *_: (0, i))
    normed, q, k, v = call(
        qkv_kernel,
        (width // tile,),
        (),
        tuple(hbm(a) for a in (xp, xq, g_attn, w_query, w_key, w_value)),
        [whole(lp, width), whole(lq, width), whole(width), col_tile, col_tile, col_tile],
        [act_hbm, act_hbm, act_hbm, act_hbm],
        [whole(total, width), act_tile, act_tile, act_tile],
        flops=3 * mm,
        moved=10 * 2**20,
    )

    head_tile = pl.BlockSpec((total, 2 * dk), lambda i, *_: (0, i))
    probs_p, probs_q, ctx = call(
        functools.partial(attn_kernel, lp, lq, segs, dk),
        (pairs,),
        info,
        (bias_table, hbm(q), hbm(k), hbm(v)),
        [near(), head_tile, head_tile, head_tile],
        [pltpu.HBM((heads, lp, lp), BF16), pltpu.HBM((heads, lq, lq), BF16), act],
        [
            pl.BlockSpec((2, lp, lp), lambda i, *_: (i, 0, 0)),
            pl.BlockSpec((2, lq, lq), lambda i, *_: (i, 0, 0)),
            head_tile,
        ],
        [pltpu.VMEM((16, 2 * lp), F32)],
        flops=14 * 10**9,
        moved=13 * 2**20,
    )

    ff_tile = ff // NB
    w_in_spec = pl.BlockSpec((width, ff_tile), lambda i, *_: (0, i))
    w_back_spec = pl.BlockSpec((ff_tile, width), lambda i, *_: (i, 0))
    ff_spec = pl.BlockSpec((total, ff_tile), lambda i, *_: (0, i))
    message = width + 128
    residual, normed_two, hidden, slope, output, pooled = call(
        functools.partial(ffn_kernel, lp, lq, segs),
        (NB,),
        info,
        (ctx, xp, xq, w_out, g_ffn, hbm(w_in), hbm(w_back), g_final),
        [near(), near(), near(), near(), near(), w_in_spec, w_back_spec, near()],
        [
            act32, act, pltpu.HBM((total, ff), BF16), pltpu.HBM((total, ff), BF16), act32,
            shaped((2 * segs, message), BF16),
        ],
        [near(), near(), ff_spec, ff_spec, near(), near()],
        flops=9 * mm,
        moved=30 * 2**20,
        vmem=24,
    )

    if fast:
        one = jnp.concatenate([pooled] + [permute(pooled, b, count) for b in (Y, X, X | Y)], axis=0)
        two = jnp.concatenate([one] + [permute(one, b, count) for b in (Z0, Z1, Z0 | Z1)], axis=0)
        every = 2 * two.shape[0]
        query_loss, d_proj, d_pooled, gathered = call(
            functools.partial(loss_kernel, segs, GATHER),
            (1,),
            info,
            (two, permute(two, CORE, count), w_proj),
            [near(), near(), near()],
            [
                hbm_out((segs,), F32), shaped((every, width), BF16),
                shaped((2 * segs, width), F32), shaped((every, message), BF16),
            ],
            [whole(segs), near(), near(), near()],
            flops=10**9,
            moved=2**20,
        )
    else:
        gathered = lax.all_gather(pooled, AXES, axis=0, tiled=True)
        every = gathered.shape[0]
        block = jnp.arange(every, dtype=jnp.int32) // (2 * segs)
        loss, d_proj = loss_math(segs, block[:, None], block[None, :], gathered, w_proj)
        mine = (wide_at * n_narrow + narrow_at) * 2 * segs
        query_loss = lax.dynamic_slice_in_dim(loss, mine + segs, segs, 0)[:, 0]
        d_pooled = nt(lax.dynamic_slice_in_dim(d_proj, mine, 2 * segs, 0), w_proj)

    part1 = (2, WB // 2, 2, cols, LANES)
    block1 = pl.BlockSpec((2, 1, 2, cols, LANES), lambda i, *_: (0, i, 0, 0, 0))
    hidden_spec = pl.BlockSpec((total, 2 * LANES), lambda i, s, *_: (0, i ^ (s[0] // 2)))
    d_output, d_ffn, final_gain_grad, turned_ff, send1 = call(
        functools.partial(out_ff_send_kernel, lp, lq, segs),
        (WB // 2,),
        info,
        (d_pooled, output, g_final, hbm(hidden)),
        [near(), near(), near(), hidden_spec],
        [act32, act, shaped((1, width), F32), shaped((width, total), BF16), shaped(part1, BF16)],
        [near(), near(), near(), near(), block1],
        flops=3 * mm,
        moved=10 * 2**20,
    )
    (keep1,) = call(
        out_ff_keep_kernel,
        (WB // 2,),
        info,
        (turned_ff, hbm(hidden)),
        [near(), hidden_spec],
        [shaped(part1, BF16)],
        [block1],
        flops=2 * mm,
        moved=8 * 2**20,
    )

    after = []
    if fast:
        sc1 = Scatter((((0, 0, cols // 2),), ((0, cols // 2, cols),)), count)
        sc1.source(send1, [keep1], cols)
        after, _ = advance(info, [sc1])

    def turn(i, s):
        return (((i % 2) * 2) + (1 - i // 2)) ^ s[1]

    size2, size_o = 2 * rows, rows // 2
    part2 = shaped((2, WB, size2, LANES), BF16)
    part_o = shaped((2, WB, size_o, LANES), BF16)

    def tiles_at(first):
        return [
            near(),
            pl.BlockSpec((ff_tile, width), lambda i, s, *_: (turn(i + first, s), 0)),
            pl.BlockSpec((total, ff_tile), lambda i, s, *_: (0, turn(i + first, s))),
            pl.BlockSpec((width, ff_tile), lambda i, s, *_: (0, turn(i + first, s))),
        ]

    half2 = shaped((WB, size2, LANES), BF16)
    send2, keep2a, turned, so_far = call(
        ffn_back_first_kernel,
        (3,),
        info,
        (d_ffn, hbm(w_back), hbm(slope), hbm(w_in), normed_two),
        tiles_at(0) + [near()],
        [part2, half2, shaped((width, total), BF16), act32],
        [near()] * 4,
        flops=9 * mm,
        moved=16 * 2**20,
        vmem=16,
        after=after,
    )
    after = []
    if fast:
        after, (send2,) = advance(info, [sc1], [so_far], [send2])
    keep2b, d_resid, ffn_gain_grad, d_ctx, send_o, keep_o = call(
        ffn_back_last_kernel,
        (1,),
        info,
        (
            d_ffn, hbm(w_back), hbm(slope), hbm(w_in), turned, so_far, d_output, residual, g_ffn,
            ctx, w_out,
        ),
        tiles_at(3) + [near()] * 7,
        [half2, act32, shaped((1, width), F32), act, part_o, part_o],
        [near()] * 6,
        [pltpu.VMEM((width, total), BF16)],
        flops=5 * mm,
        moved=20 * 2**20,
        vmem=18,
        after=after,
    )

    after = []
    if fast:
        sc2 = Scatter((((0, 0, 128),), ((0, 128, size2), (1, 0, size_o))), count)
        sc2.source(send2, [keep2a, keep2b], size2)
        after, (send_o,) = advance(info, [sc1], [d_ctx], [send_o])
        sc2.source(send_o, [keep_o], size_o)
        more, _ = advance(info, [sc2], after)
        after = after + more
    d_q, d_k, d_v, sums = call(
        functools.partial(attn_back_kernel, dk, lp, lq),
        (pairs,),
        info,
        (hbm(q), hbm(k), hbm(v), d_ctx, hbm(probs_p), hbm(probs_q)),
        [head_tile] * 4
        + [pl.BlockSpec((2, span, span), lambda i, *_: (i, 0, 0)) for span in (lp, lq)],
        [act_hbm, act_hbm, act_hbm, shaped((16, 2 * lp), F32)],
        [head_tile, head_tile, head_tile, near()],
        flops=8 * 10**9,
        moved=16 * 2**20,
        after=after,
    )

    after = []
    if fast:
        after, _ = advance(info, [sc1, sc2], [sums])
    size3 = rows + rows // 2
    flat3 = shaped((16 * size3 + 16, LANES), BF16)
    send3, keep3 = call(
        functools.partial(qkv_grad_kernel, lp, heads),
        (1,),
        info,
        (
            hbm(normed), hbm(d_q), hbm(d_k), hbm(d_v), w_query, w_key, w_value, g_attn,
            ffn_gain_grad, final_gain_grad, sums,
        ),
        [whole(total, width)] * 4 + [near()] * 7,
        [flat3, flat3],
        [near(), near()],
        [
            pltpu.VMEM((width, total), BF16), pltpu.VMEM((NB, WB, size3, LANES), BF16),
            pltpu.VMEM((width, 128), F32),
        ],
        flops=3 * mm,
        moved=9 * 2**20,
        vmem=24,
        after=after,
    )

    after = []
    own_rows, own_cols = width // WB, width // NB
    square = hbm_out((own_rows, own_cols), F32)
    if fast:

        def finish(kernel, scatter, outs, after, more=()):
            parts, base = scatter.finish()
            parts = parts[:1] + list(more) + parts[1:]
            return call(
                functools.partial(kernel, base), (1,), info, parts, [near()] * len(parts), outs,
                [whole(*out_shape_of(out)) for out in outs], flops=10**6, moved=2**20, after=after,
            )

        (out_ff,) = finish(out_ff_finish_kernel, sc1, [hbm_out((cols, ff // WB), F32)], [keep3])
        out_ff = out_ff.T
        sc3 = Scatter((((0, 0, 80),), ((0, 80, size3),)), count, quad=True)
        after, (send3,) = advance(info, [sc2], [hbm(out_ff.T)], [send3])
        sc3.source(send3, [keep3], size3, small=True)

    size = lq
    steps_p = lp // size
    (grad_p,) = call(
        functools.partial(first_input_kernel),
        (1,),
        info,
        (hbm(d_q), hbm(d_k), hbm(d_v), w_query, w_key, w_value, hbm(d_resid), hbm(xp), g_attn),
        [whole(size, width)] * 3 + [near()] * 3 + [whole(size, width)] * 2 + [near()],
        [hbm_out((lp, width), F32)],
        [whole(size, width)],
        flops=mm,
        moved=6 * 2**20,
        after=after,
    )
    after = []
    if fast:
        after, _ = advance(info, [sc3], [hbm(grad_p)])

    def p_at(i, *_):
        return (jnp.minimum(i + 1, steps_p - 1), 0)

    def q_at(i, *_):
        return (jnp.maximum(i + 1 - steps_p, 0), 0)

    row_tile = pl.BlockSpec((size, width), lambda i, *_: (i + 1, 0))
    grad_q, proj_grad, grad_p = call(
        functools.partial(input_kernel, lp),
        (total // size - 1,),
        info,
        (
            hbm(d_q), hbm(d_k), hbm(d_v), w_query, w_key, w_value, hbm(d_resid), hbm(xp), hbm(xq),
            g_attn, gathered[:256], d_proj[:256],
        ),
        [row_tile, row_tile, row_tile, near(), near(), near(), row_tile]
        + [pl.BlockSpec((size, width), p_at), pl.BlockSpec((size, width), q_at)]
        + [near()] * 3,
        [hbm_out((lq, width), F32), square],
        [pl.BlockSpec((size, width), q_at), whole(own_rows, own_cols)],
        [pltpu.VMEM((width, width), F32)],
        flops=3 * mm,
        moved=10 * 2**20,
        vmem=20,
        after=after,
        through=[grad_p],
        through_specs=[pl.BlockSpec((size, width), p_at)],
    )

    if fast:
        after, _ = advance(info, [sc3, sc2], [hbm(proj_grad)])
        after, _ = advance(info, [sc3], after)
        in_ff, out_w = finish(
            in_ff_finish_kernel, sc2, [hbm_out((rows, ff // NB), F32), square], after
        )
        query_w, key_w, value_w, gain_a, gain_f, gain_l, bias = finish(
            functools.partial(qkv_finish_kernel, heads), sc3,
            [square] * 3 + [hbm_out((width,), F32)] * 3 + [hbm_out((heads, BUCKETS), F32)],
            [hbm(out_w)], [sc3.first[0].arrays[0]],
        )
    else:
        own_rows, own_cols = width // n_wide, width // n_narrow
        left = lax.dynamic_slice(gathered, (0, wide_at * own_rows), (every, own_rows))
        right = lax.dynamic_slice(d_proj, (0, narrow_at * own_cols), (every, own_cols))
        proj_grad = tn(left, right)

        def blocks(send, keep):
            both = jnp.stack([keep, send], axis=1).astype(F32)
            return both.reshape((NB, WB) + both.shape[-2:])

        def spread(matrix):
            matrix = lax.psum_scatter(matrix, "wide", scatter_dimension=0, tiled=True)
            return lax.psum_scatter(matrix, "narrow", scatter_dimension=1, tiled=True)

        def side(part):
            half = part.shape[2] // 2
            return jnp.concatenate([part[:, :, :half], part[:, :, half:]], axis=3)

        def stack(part):
            half = part.shape[3] // 2
            return jnp.concatenate([part[..., :half], part[..., half:]], axis=2)

        def matrix(part):
            return part.transpose(1, 2, 0, 3).reshape(WB * part.shape[2], NB * part.shape[3])

        b1 = blocks(send1.reshape(2, WB, cols, LANES), keep1.reshape(2, WB, cols, LANES))
        b2 = blocks(send2, jnp.stack([keep2a, keep2b]))
        coded = keep3[16 * size3 :]
        b3 = blocks(*(a[: 16 * size3].reshape(2, WB, size3, LANES) for a in (send3, keep3)))
        out_ff = spread(matrix(b1.transpose(0, 1, 3, 2)))
        in_ff = spread(matrix(side(b2)))
        out_w = spread(matrix(stack(blocks(send_o, keep_o))))
        query_w = spread(matrix(b3[:, :, :rows, :cols]))
        key_w = spread(matrix(b3[:, :, :rows, cols:]))
        value_w = spread(matrix(stack(b3[:, :, rows:])))
        gains, bias = split_small(lax.psum(decode(coded), AXES), width, heads)
        gain_a, gain_f, gain_l = (gain[0] for gain in gains)
    return (
        query_loss, grad_p, grad_q, gain_a, query_w, key_w, value_w, out_w, bias.T, gain_f,
        in_ff, out_ff, gain_l, proj_grad,
    )


def solution(mesh):
    n_wide, n_narrow = mesh.shape["wide"], mesh.shape["narrow"]
    fast = (n_wide, n_narrow) == (WB, NB)
    rows = P(AXES, None)
    owned = P("wide", "narrow")
    return jax.shard_map(
        functools.partial(per_device, fast, n_wide, n_narrow),
        mesh=mesh,
        in_specs=(rows, rows, rows, rows, P(AXES)) + (P(),) * 11,
        out_specs=(
            P(AXES), rows, rows, P(), owned, owned, owned, owned, P(), P(),
            owned, owned, P(), owned,
        ),
        check_vma=False,
    )
```

```python
import functools

import jax
import jax.numpy as jnp
from jax import lax
from jax.experimental import pallas as pl
from jax.experimental.pallas import tpu as pltpu
from jax.sharding import PartitionSpec as P

BUCKETS = 32
MAX_DIST = 128
SCALE = 0.02
EPS = 1e-06
GELU = 0.7978845608028654
CUBE = 0.044715
HIGHEST = lax.Precision.HIGHEST
F32 = jnp.float32
BF16 = jnp.bfloat16
AXES = ("wide", "narrow")
NB = 4
WB = 8
CH = 128
LANES = 384
HS = 4
SMALL = 8


def bucket_edges():
    half = BUCKETS // 2
    exact = half // 2
    levels = half - exact
    ratio = MAX_DIST // exact
    edges = []
    for step in range(1, levels):
        target = exact**levels * ratio**step
        candidate = exact
        while candidate**levels < target:
            candidate += 1
        edges.append(candidate)
    return edges


def nn(a, b, **kw):
    return lax.dot_general(a, b, (((1,), (0,)), ((), ())), preferred_element_type=F32, **kw)


def tn(a, b):
    return lax.dot_general(a, b, (((0,), (0,)), ((), ())), preferred_element_type=F32)


def nt(a, b, **kw):
    return lax.dot_general(a, b, (((1,), (1,)), ((), ())), preferred_element_type=F32, **kw)


def bucket_hot(span, shift=0):
    shape = (BUCKETS, 2 * span)
    rel = lax.broadcasted_iota(jnp.int32, shape, 1) - shift
    rel = span - jnp.where(rel < 0, rel + 2 * span, rel)
    dist = jnp.abs(rel)
    half = BUCKETS // 2
    exact = half // 2
    far = jnp.full(shape, exact, jnp.int32)
    for edge in bucket_edges():
        far = far + jnp.where(dist >= edge, 1, 0)
    far = jnp.minimum(far, half - 1)
    bucket = jnp.where(dist < exact, dist, far) + jnp.where(rel > 0, half, 0)
    return bucket == lax.broadcasted_iota(jnp.int32, shape, 0)


def half_at(info, tower, segs, span):
    at, start = 0, 0
    for s in range(segs):
        size = info[2 + tower * segs + s]
        at = jnp.where(size == span // 2, start, at)
        start = start + size
    return at


def rolled_starts(info, tower, segs, span):
    at, start, starts = half_at(info, tower, segs, span), 0, []
    for s in range(segs):
        starts.append(jnp.where(start >= at, start - at, start - at + span))
        start = start + info[2 + tower * segs + s]
    return starts


def seg_bounds(info, segs, spans, shape, axis):
    at = lax.broadcasted_iota(jnp.int32, shape, axis)
    lo = jnp.zeros(shape, jnp.int32)
    hi = jnp.zeros(shape, jnp.int32)
    for tower, span in enumerate(spans):
        starts = rolled_starts(info, tower, segs, span)
        for s in range(segs):
            here = at == tower * segs + s
            start = starts[s] + tower * spans[0]
            lo = jnp.where(here, start, lo)
            hi = jnp.where(here, start + info[2 + tower * segs + s], hi)
    return lo, hi


def seg_of(info, tower, segs, span, shape, axis):
    at = lax.broadcasted_iota(jnp.int32, shape, axis) + span // 2
    seg = jnp.zeros(shape, jnp.int32)
    for start in rolled_starts(info, tower, segs, span):
        seg = seg + jnp.where(at >= start, 1, 0)
    return seg


def rms(v, gain):
    return v * lax.rsqrt(jnp.mean(v * v, axis=-1, keepdims=True) + EPS) * gain


def rms_back(v, gain, dy):
    r = lax.rsqrt(jnp.mean(v * v, axis=-1, keepdims=True) + EPS)
    gdy = gain * dy
    inner = jnp.mean(gdy * v, axis=-1, keepdims=True)
    return r * gdy - v * (r * r * r * inner), jnp.sum(dy * v * r, axis=0, keepdims=True)


def wide_row(gain):
    return gain[...].astype(F32).reshape(1, gain.shape[0])


def front_kernel(
    lp, lq, segs, dk, info, xp, xq, gain, wq, wk, wv, table,
    x, normed, q, k, v, probs_p, probs_q, ctx, rows,
):
    reach = lp // 2

    @pl.when(pl.program_id(0) == 0)
    def _():
        heads = table.shape[0]
        rows[:heads, :] = nn(table[...], bucket_hot(reach).astype(F32).astype(BF16))
        g = wide_row(gain)
        for tower, tokens, off, span in ((0, xp, 0, lp), (1, xq, lp, lq)):
            at = half_at(info, tower, segs, span)
            rolled = pltpu.roll(tokens[...].astype(F32), jnp.where(at == 0, 0, span - at), 0)
            here = slice(off, off + span)
            x[here, :] = rolled.astype(BF16)
            normed[here, :] = rms(rolled, g).astype(BF16)

    weights = jnp.concatenate([wq[...], wk[...], wv[...]], axis=1)
    qkv = nn(normed[...], weights).astype(BF16)
    cut = HS * dk
    q[...] = qkv[:, :cut]
    k[...] = qkv[:, cut : 2 * cut]
    v[...] = qkv[:, 2 * cut :]
    units = []
    for hh in range(HS):
        row = rows[pl.ds(HS * pl.program_id(0) + hh, 1), :]
        bias = pltpu.roll(jnp.broadcast_to(row, (CH, 2 * reach)), 0, 1, stride=1, stride_axis=0)
        cols = slice(hh * dk, (hh + 1) * dk)
        for tower, off, span, probs in ((0, 0, lp, probs_p), (1, lp, lq, probs_q)):
            half = span // 2
            full = jnp.concatenate(
                [bias[:, reach - r0 : reach - r0 + half] for r0 in range(0, half, CH)], axis=0
            )
            for part in range(2):
                here = slice(off + part * half, off + (part + 1) * half)
                units.append((tower, span, cols, here, full, probs, 2 * hh + part))
    scores = []
    for tower, span, cols, here, full, _, at in units:
        s = nt(k[here, cols], q[here, cols]) + full
        if at % 2:
            half = span // 2
            seg_j = seg_of(info, tower, segs, span, (half, 1), 0)
            seg_i = seg_of(info, tower, segs, span, (1, half), 1)
            s = jnp.where(seg_i == seg_j, s, -1000000000.0)
        scores.append(s)
    lows = []
    for (_, _, _, _, _, probs, at), s in zip(units, scores):
        e = jnp.exp(s - jnp.max(s, axis=0, keepdims=True))
        p = e * (1.0 / jnp.sum(e, axis=0, keepdims=True))
        p = p.astype(BF16)
        probs[at] = p
        lows.append(p)
    for (_, _, cols, here, _, _, _), p in zip(units, lows):
        ctx[here, cols] = tn(p, v[here, cols]).astype(BF16)


def ffn_kernel(
    lp, lq, segs, info, ctx, x, w_out, fgain, w_in, w_back, lgain,
    residual, normed_two, hidden, slope, output, pooled,
):
    step = pl.program_id(0)
    total = lp + lq

    @pl.when(step == 0)
    def _():
        g = wide_row(fgain)
        res = x[...].astype(F32) + nn(ctx[...], w_out[...])
        residual[...] = res
        output[...] = res
        normed_two[...] = rms(res, g).astype(BF16)

    part = 256
    parts = [slice(r0, r0 + part) for r0 in range(0, total, part)]

    tile = pl.ds(pl.multiple_of(step * slope.shape[1], slope.shape[1]), slope.shape[1])

    def up(here):
        return nn(normed_two[here, :], w_in[:, tile])

    u = up(parts[0])
    for n, here in enumerate(parts):
        following = up(parts[n + 1]) if n + 1 < len(parts) else None
        uu = u * u
        t = jnp.tanh(u * (GELU + (GELU * CUBE) * uu))
        half = 0.5 + 0.5 * t
        h = (u * half).astype(BF16)
        hidden[here, tile] = h
        slope[here, :] = (
            half + (u * (0.5 - (0.5 * t) * t)) * (GELU + (3.0 * GELU * CUBE) * uu)
        ).astype(BF16)
        output[here, :] += nn(h, w_back[tile, :])
        u = following

    @pl.when(step == pl.num_programs(0) - 1)
    def _():
        final = rms(output[...], wide_row(lgain))
        lo, hi = seg_bounds(info, segs, (lp, lq), (2 * segs, 1), 0)
        at = lax.broadcasted_iota(jnp.int32, (2 * segs, total), 1)
        hot = jnp.where((at >= lo) & (at < hi), 1.0, 0.0).astype(BF16)
        high = final.astype(BF16)
        mean = nn(hot, high) + nn(hot, (final - high.astype(F32)).astype(BF16))
        mean = mean / (hi - lo).astype(F32)
        width = final.shape[1]
        pooled[:, :width] = mean.astype(BF16)
        shape = (2 * segs, pooled.shape[1] - width)
        at_row = lax.broadcasted_iota(jnp.int32, shape, 0)
        at_col = lax.broadcasted_iota(jnp.int32, shape, 1)
        code = jnp.zeros(shape, jnp.int32)
        for s in range(segs):
            pair = info[2 + 2 * segs + s]
            code = jnp.where((at_row == segs + s) & (at_col == 0), pair // 64, code)
            code = jnp.where((at_row == segs + s) & (at_col == 1), pair % 64, code)
        pooled[:, width:] = code.astype(F32).astype(BF16)


def loss_math(segs, block_row, block_col, gathered, w_proj):
    count = gathered.shape[0]
    width = w_proj.shape[0]
    low = gathered[:, :width]
    code = gathered[:, width:].astype(F32)
    pair = code[:, 0:1] * 64.0 + code[:, 1:2]
    row = lax.broadcasted_iota(jnp.int32, (count, 1), 0) % (2 * segs)
    col = lax.broadcasted_iota(jnp.int32, (1, count), 1) % (2 * segs)
    number = (block_col * segs + col).astype(F32)
    is_query = row >= segs
    is_passage = col < segs
    proj = nn(low, w_proj)
    scale = lax.rsqrt(jnp.sum(proj * proj, axis=-1, keepdims=True) + EPS)
    embed = proj * scale
    embed_low = embed.astype(BF16)
    sims = nt(embed_low, embed_low) / SCALE
    masked = jnp.where(is_passage, sims, -1e30)
    top = jnp.max(masked, axis=1, keepdims=True)
    expo = jnp.where(is_passage, jnp.exp(masked - top), 0.0)
    total = jnp.sum(expo, axis=1, keepdims=True)
    hot = jnp.where(is_passage & (number == pair), 1.0, 0.0)
    loss = top + jnp.log(total) - jnp.sum(hot * sims, axis=1, keepdims=True)
    d_sims = jnp.where(is_query, (expo / total - hot) / SCALE, 0.0)
    d_embed = nn(d_sims + d_sims.T, embed_low.astype(F32), precision=HIGHEST)
    d_proj = (d_embed - embed * jnp.sum(embed * d_embed, axis=-1, keepdims=True)) * scale
    return loss, d_proj.astype(BF16)


def loss_kernel(segs, bits, info, near, far, w_proj, loss, d_proj, d_pooled, every):
    gathered = jnp.concatenate([near[...], far[...]], axis=0)
    every[...] = gathered
    count = gathered.shape[0]

    def device(shape, axis):
        place = lax.broadcasted_iota(jnp.int32, shape, axis) // (2 * segs)
        other = jnp.zeros(shape, jnp.int32)
        for at, bit in enumerate(bits):
            other = other + ((place >> at) & 1) * bit
        return other ^ (info[0] * NB + info[1])

    value, d_low = loss_math(
        segs, device((count, 1), 0), device((1, count), 1), gathered, w_proj[...]
    )
    flat = jnp.broadcast_to(value[: 2 * segs], (2 * segs, 128)).T
    loss[...] = flat[:1, segs : 2 * segs].reshape(segs)
    d_proj[...] = d_low
    d_pooled[...] = nt(d_low[: 2 * segs], w_proj[...])


def out_ff_blocks(info, rows, hidden, dst):
    size = 2 * LANES
    at = (pl.program_id(0) ^ (info[0] // 2)) * size
    res = nn(rows, hidden[:, pl.ds(pl.multiple_of(at, size), size)]).astype(BF16)
    cols = res.shape[0] // 2
    for y in range(2):
        for x in range(2):
            dst.at[y, 0][x ^ (info[0] % 2)] = res[
                y * cols : (y + 1) * cols, x * LANES : (x + 1) * LANES
            ]


def out_ff_send_kernel(
    lp, lq, segs, info, d_pooled, output, lgain, hidden,
    d_output, d_ffn, gain_grad, turned, send,
):
    total = lp + lq
    rows = output.shape[1] // NB
    half = 2 * rows

    @pl.when(pl.program_id(0) == 0)
    def _():
        lo, hi = seg_bounds(info, segs, (lp, lq), (1, 2 * segs), 1)
        lo_c, hi_c = seg_bounds(info, segs, (lp, lq), (2 * segs, 1), 0)
        at = lax.broadcasted_iota(jnp.int32, (total, 2 * segs), 0)
        hot = jnp.where((at >= lo) & (at < hi), 1.0, 0.0).astype(BF16)
        each = d_pooled[...] / (hi_c - lo_c).astype(F32)
        high = each.astype(BF16)
        dy = nn(hot, high) + nn(hot, (each - high.astype(F32)).astype(BF16))
        dv, dg = rms_back(output[...], wide_row(lgain), dy)
        d_output[...] = dv
        gain_grad[...] = dg
        low = dv.astype(BF16)
        d_ffn[...] = low
        flipped = low.T
        for n in range(NB):
            other = n ^ info[1]
            at_row = (other % 2) * half + (other // 2) * rows
            turned[pl.ds(pl.multiple_of(at_row, rows), rows), :] = flipped[
                n * rows : (n + 1) * rows
            ]

    out_ff_blocks(info, turned[half:, :], hidden, send)


def out_ff_keep_kernel(info, turned, hidden, keep):
    out_ff_blocks(info, turned[: turned.shape[0] // 2, :], hidden, keep)


def turn_rows(dst, value, wide):
    rows = value.shape[1] // WB
    flipped = value.T
    for w in range(WB):
        dst[pl.ds(pl.multiple_of((w ^ wide) * rows, rows), rows), :] = flipped[
            w * rows : (w + 1) * rows
        ]


def turn(step, narrow):
    return ((step % 2) * 2 + (1 - step // 2)) ^ narrow


def ffn_tile(number, d_ffn, w_back, slope, w_in, turned):
    size = slope.shape[1]
    tile = pl.ds(pl.multiple_of(number * size, size), size)
    d_up = (nt(d_ffn[...], w_back[tile, :]) * slope[...].astype(F32)).astype(BF16)
    res = nn(turned[...], d_up).astype(BF16)
    rows = res.shape[0] // WB
    blocks = jnp.concatenate(
        [
            res[:, half * LANES : (half + 1) * LANES].reshape(WB, rows, LANES)
            for half in range(2)
        ],
        axis=1,
    )
    return nt(d_up, w_in[:, tile]), blocks


def ffn_back_first_kernel(
    info, d_ffn, w_back, slope, w_in, normed_two, send, keep, turned, total
):
    step = pl.program_id(0)

    @pl.when(step == 0)
    def _():
        turn_rows(turned, normed_two[...], info[0])
        total[...] = jnp.zeros_like(total)

    part, blocks = ffn_tile(turn(step, info[1]), d_ffn, w_back, slope, w_in, turned)
    total[...] += part

    @pl.when(step < 2)
    def _():
        send[step] = blocks

    @pl.when(step == 2)
    def _():
        keep[...] = blocks


def ffn_back_last_kernel(
    info, d_ffn, w_back, slope, w_in, turned, so_far, d_output, residual, fgain, ctx, w_out,
    keep, d_resid, gain_grad, d_ctx, send_o, keep_o, turned_ctx,
):
    part, blocks = ffn_tile(turn(3, info[1]), d_ffn, w_back, slope, w_in, turned)
    keep[...] = blocks
    width = residual.shape[1]
    rows, cols = width // WB, width // NB
    dv, dg = rms_back(residual[...], wide_row(fgain), so_far[...] + part)
    dr = d_output[...] + dv
    d_resid[...] = dr
    gain_grad[...] = dg
    da = dr.astype(BF16)
    d_ctx[...] = nt(da, w_out[...]).astype(BF16)
    turn_rows(turned_ctx, ctx[...], info[0])
    grad = nn(turned_ctx[...], da)
    for n in range(NB):
        part = grad[:, n * cols : (n + 1) * cols].reshape(WB, rows, cols)
        part = jnp.concatenate([part[:, : rows // 2], part[:, rows // 2 :]], axis=2)
        part = part.astype(BF16)
        y = (n // 2) ^ (info[1] // 2)

        @pl.when((n % 2) == (info[1] % 2))
        def _():
            keep_o[y] = part

        @pl.when((n % 2) != (info[1] % 2))
        def _():
            send_o[y] = part


def attn_back_kernel(dk, lp, lq, info, q, k, v, d_ctx, probs_p, probs_q, d_qkv, sums):
    step = pl.program_id(0)
    reach = lp // 2

    @pl.when(step == 0)
    def _():
        sums[...] = jnp.zeros_like(sums)

    units = []
    for hh in range(HS):
        cols = slice(hh * dk, (hh + 1) * dk)
        for off, span, probs in ((0, lp, probs_p), (lp, lq, probs_q)):
            half = span // 2
            for part in range(2):
                here = slice(off + part * half, off + (part + 1) * half)
                units.append((hh, cols, here, half, probs, 2 * hh + part))
    d_probs = [nt(v[here, cols], d_ctx[here, cols]) for _, cols, here, _, _, _ in units]
    tiles = [[jnp.zeros((CH, CH), F32)] * (2 * reach // CH) for _ in range(HS)]
    lows = []
    for (hh, _, _, half, probs, at), d_prob in zip(units, d_probs):
        p = probs[at].astype(F32)
        t = p * d_prob
        ds = t - p * jnp.sum(t, axis=0, keepdims=True)
        lows.append(ds.astype(BF16))
        for a in range(half // CH):
            for b in range(half // CH):
                to = b + reach // CH - a
                piece = ds[a * CH : (a + 1) * CH, b * CH : (b + 1) * CH]
                tiles[hh][to] = tiles[hh][to] + piece
    for (_, cols, here, _, probs, at), low in zip(units, lows):
        d_qkv[0, here, cols] = tn(low, k[here, cols]).astype(BF16)
        d_qkv[1, here, cols] = nn(low, q[here, cols]).astype(BF16)
        d_qkv[2, here, cols] = nn(probs[at], d_ctx[here, cols]).astype(BF16)
    at_i = lax.broadcasted_iota(jnp.int32, (CH, CH), 0)
    at_j = lax.broadcasted_iota(jnp.int32, (CH, CH), 1)
    mirror = jnp.where(at_i + at_j == CH - 1, 1.0, 0.0).astype(BF16)
    for hh in range(HS):
        flipped = nn(mirror, jnp.concatenate(tiles[hh], axis=1).astype(BF16))
        turn = pltpu.roll(flipped, 0, 1, stride=1, stride_axis=0)
        sums[pl.ds(HS * step + hh, 1), :] = jnp.sum(turn, axis=0, keepdims=True)


def qkv_grad_kernel(
    lp, heads, info, normed, d_qkv, wq, wk, wv, gain, g_ffn, g_final, sums,
    send, keep, turned, blocks, saved, column,
):
    width = normed.shape[1]
    rows, cols = width // WB, width // NB
    size = blocks.shape[1] * blocks.shape[2]
    step = pl.program_id(0)

    def gradient(weight):
        grad = nn(turned[...], d_qkv[0])
        for w in range(WB):
            at = pl.ds(pl.multiple_of((w ^ info[0]) * rows, rows), rows)
            part = grad[w * rows : (w + 1) * rows, :] * weight[at, :].astype(F32)
            column[at, :] += jnp.broadcast_to(
                jnp.sum(part, axis=1, keepdims=True), (rows, column.shape[1])
            )
        return grad

    @pl.when(step == 0)
    def _():
        turn_rows(turned, normed[...], info[0])
        column[...] = jnp.zeros_like(column)
        saved[...] = gradient(wq)

    @pl.when(step == 1)
    def _():
        grad = gradient(wk)
        for n in range(NB):
            here = slice(n * cols, (n + 1) * cols)
            both = jnp.concatenate([saved[:, here], grad[:, here]], axis=1).astype(BF16)
            blocks[n, :, :rows, :] = both.reshape(WB, rows, LANES)

    @pl.when(step == 2)
    def _():
        grad = gradient(wv)
        for n in range(NB):
            part = grad[:, n * cols : (n + 1) * cols].reshape(WB, rows, cols)
            part = jnp.concatenate([part[:, : rows // 2], part[:, rows // 2 :]], axis=2)
            blocks[n, :, rows:, :] = part.astype(BF16)
        core, y0 = info[1] % 2, info[1] // 2
        for y in range(2):
            here = slice(y * size, (y + 1) * size)
            send[here, :] = blocks[(y ^ y0) * 2 + (1 - core)].reshape(size, LANES)
            keep[here, :] = blocks[(y ^ y0) * 2 + core].reshape(size, LANES)
        g_attn = column[...].T[:1, :] / wide_row(gain)
        hot = bucket_hot(lp // 2, CH - 1).astype(F32)
        bias = nt(sums[...], hot, precision=HIGHEST)
        pieces = []
        for grad in (g_attn, g_ffn[...], g_final[...]):
            pieces += [grad[:, i : i + LANES] for i in range(0, width, LANES)]
        pieces.append(jnp.concatenate([bias[h : h + 1, :] for h in range(heads)], axis=1))
        pieces.append(jnp.zeros((SMALL - len(pieces), LANES), F32))
        small = encode(jnp.concatenate(pieces, axis=0))
        send[2 * size :, :] = small
        keep[2 * size :, :] = small


def input_kernel(tower, segs, info, d_qkv, wq, wk, wv, d_resid, x, gain, grad):
    span = grad.shape[0]
    dn = nt(d_qkv[0], wq[...]) + nt(d_qkv[1], wk[...]) + nt(d_qkv[2], wv[...])
    v = x[...].astype(F32)
    r = lax.rsqrt(jnp.mean(v * v, axis=-1, keepdims=True) + EPS)
    gdy = wide_row(gain) * dn
    inner = jnp.mean(gdy * v, axis=-1, keepdims=True)
    out = d_resid[...] + (r * gdy - v * (r * r * r * inner))
    grad[...] = pltpu.roll(out, half_at(info, tower, segs, span), 0)


def proj_kernel(info, every, d_proj, proj_grad, full):
    rows, cols = proj_grad.shape
    width = full.shape[0]
    full[...] = tn(every[:, :width], d_proj[...])
    mine = full[pl.ds(pl.multiple_of(info[0] * rows, 8), rows), :]
    for n in range(width // cols):

        @pl.when(info[1] == n)
        def _():
            proj_grad[...] = mine[:, n * cols : (n + 1) * cols]


class Info:
    def __init__(self, place, passages, queries, pairs):
        segs = passages.shape[1]
        self.at = [lambda: place[0], lambda: place[1]]
        self.at += [functools.partial(lambda r, i: r[0, i], passages, i) for i in range(segs)]
        self.at += [functools.partial(lambda r, i: r[0, i], queries, i) for i in range(segs)]
        self.at += [functools.partial(lambda r, i: r[i], pairs, i) for i in range(segs)]

    def __getitem__(self, i):
        return self.at[i]()


def call(
    kernel, grid, info, args, in_specs, outs, out_specs, scratch=(), flops=0, moved=0,
    vmem=16, after=(), through=(), through_specs=(),
):
    count, more = len(args), len(after) + len(through)
    outs, out_specs = list(outs), list(out_specs)
    made = len(outs)
    aliases = {len(info) + count + len(after) + i: made + i for i in range(len(through))}
    outs += [(hbm_out if through_specs else shaped)(a.shape, a.dtype) for a in through]
    out_specs += through_specs or [pl.BlockSpec(memory_space=pl.ANY)] * len(through)
    hidden = 0 if through_specs else len(through)

    def body(*refs):
        scalars, refs = refs[: len(info)], refs[len(info) :]
        results = refs[count + more :]
        kernel(
            Info(*scalars) if scalars else None,
            *refs[:count],
            *results[:made],
            *results[made + hidden :],
        )

    return pl.pallas_call(
        body,
        grid_spec=pltpu.PrefetchScalarGridSpec(
            num_scalar_prefetch=len(info),
            grid=grid,
            in_specs=list(in_specs) + [pl.BlockSpec(memory_space=pl.ANY)] * more,
            out_specs=out_specs,
            scratch_shapes=list(scratch),
        ),
        out_shape=outs,
        input_output_aliases=aliases,
        compiler_params=pltpu.CompilerParams(vmem_limit_bytes=vmem * 2**20),
        cost_estimate=pl.CostEstimate(flops=flops, bytes_accessed=moved, transcendentals=0),
    )(*info, *args, *after, *through)


def hbm(array):
    return pltpu.with_memory_space_constraint(array, pltpu.HBM)


def near(*shape):
    return pl.BlockSpec(memory_space=pltpu.VMEM)


def whole(*shape):
    return pl.BlockSpec(shape, lambda *_: (0,) * len(shape), pipeline_mode=pl.Buffered(1))


def hbm_out(shape, dtype):
    return pltpu.HBM(shape, dtype)


def out_shape_of(out):
    return out.inner_aval.shape


def shaped(shape, dtype):
    return jax.ShapeDtypeStruct(shape, dtype)


def permute(array, bit, count):
    return lax.ppermute(array, AXES, [(i, i ^ bit) for i in range(count)])


CORE, Y, X, Z0, Z1 = 1, 2, 4, 8, 16
GATHER = (Z0, Z1, Y, X, CORE)


def own_sum(base, refs):
    parts = [r[b:, :].astype(F32) for b, r in zip(base, refs)]
    while len(parts) > 1:
        parts = [a + b for a, b in zip(parts[::2], parts[1::2])]
    return parts[0]


def out_ff_finish_kernel(base, info, *refs):
    refs[-1][...] = own_sum(base, refs[:-1])


def in_ff_finish_kernel(base, info, *refs):
    *parts, in_ff, out_w = refs
    total = own_sum(base, parts)
    rows, cols = out_w.shape
    in_ff[...] = jnp.concatenate([total[:rows], total[rows : 2 * rows]], axis=1)
    out_w[...] = jnp.concatenate([total[2 * rows :, :cols], total[2 * rows :, cols:]], axis=0)


def split_small(small, width, heads):
    per = width // LANES
    gains = [
        jnp.concatenate([small[g * per + i : g * per + i + 1] for i in range(per)], axis=1)
        for g in range(3)
    ]
    row = small[3 * per : 3 * per + 1]
    bias = [row[:, h * BUCKETS : (h + 1) * BUCKETS] for h in range(heads)]
    return gains, jnp.concatenate(bias, axis=0)


def qkv_finish_kernel(heads, base, info, *refs):
    rest, own, *got, query_w, key_w, value_w, gain_a, gain_f, gain_l, bias = refs
    total = own_sum(base, (rest, *got))
    rows, cols = query_w.shape
    query_w[...] = total[:rows, :cols]
    key_w[...] = total[:rows, cols:]
    value_w[...] = jnp.concatenate([total[rows:, :cols], total[rows:, cols:]], axis=0)
    small = [decode(r[: 2 * SMALL, :]) for r in (own, *got)]
    small = (small[0] + small[1]) + (small[2] + small[3])
    gains, table = split_small(small, gain_a.shape[0], heads)
    for ref, gain in zip((gain_a, gain_f, gain_l), gains):
        ref[...] = gain.reshape(gain.shape[1])
    bias[...] = table


def encode(values):
    high = values.astype(BF16).astype(F32)
    return jnp.concatenate([high, values - high], axis=0).astype(BF16)


def decode(coded):
    half = coded.shape[0] // 2
    return coded[:half].astype(F32) + coded[half:].astype(F32)


class Part:
    def __init__(self, arrays, base, dims, rows, lo=0, hi=None):
        self.arrays, self.base, self.dims, self.rows = arrays, base, dims, rows
        self.lo, self.hi = lo, rows if hi is None else hi

    def at(self, where):
        dims, which = self.dims, 0
        if len(self.arrays) > 1:
            which, dims = where[dims[0]], dims[1:]
        index = 0
        for bit in dims:
            index = index * 2 + where[bit]
        return self.arrays[which], self.base + index * self.rows + self.lo


def add_kernel(plans, info, *refs):
    outs = refs[len(refs) - len(plans) :]
    for (sums, small), out in zip(plans, outs):
        if small:
            total = decode(refs[small[0]][small[1] : small[1] + 2 * SMALL, :])
            total = total + decode(refs[small[2]][small[3] : small[3] + 2 * SMALL, :])
            out[: 2 * SMALL, :] = encode(total)
        for to, a, at_a, b, at_b, rows in sums:
            out[to : to + rows, :] = (
                refs[a][at_a : at_a + rows, :] + refs[b][at_b : at_b + rows, :]
            )


class Scatter:
    def __init__(self, groups, count, quad=False):
        self.count, self.groups, self.quad = count, groups, quad
        self.sources = []
        self.small = None
        self.stage = -1

    def source(self, send, keeps, rows, small=False):
        send = send.reshape(-1, LANES)
        keeps = [k.reshape(-1, LANES) for k in keeps]
        got = permute(send, CORE, self.count)
        self.sources.append((keeps, got, rows))
        if small:
            at = 16 * rows
            self.small = (keeps[0], at, got, at)

    def jobs(self):
        self.stage += 1
        stage = self.stage
        if stage == 0:
            dims = (Y, Z1, Z0, X)
            groups = [
                [
                    (
                        Part(self.sources[n][0], 0, dims, self.sources[n][2], lo, hi),
                        Part([self.sources[n][1]], 0, dims, self.sources[n][2], lo, hi),
                    )
                    for n, lo, hi in group
                ]
                for group in self.groups
            ]
        else:
            groups = [[pair] for pair in zip(self.rest, self.got)]
        if stage < 2:
            bits = ((Y, X), (X, Y))[stage]
            first = [(g, {b: 1}) for g, b in zip(groups, bits)]
            rest = [(g, {b: 0}) for g, b in zip(groups, bits)]
            self.bits = bits
        else:
            merged = [pair for group in groups for pair in group]
            if self.quad:
                self.bits = (Z0, Z1, Z0 | Z1)
                first = [(merged, {Z0: a, Z1: b}) for a, b in ((1, 0), (0, 1), (1, 1))]
                rest = [(merged, {Z0: 0, Z1: 0})]
            else:
                bit = (Z0, Z1)[stage - 2]
                self.bits = (bit,)
                first, rest = [(merged, {bit: 1})], [(merged, {bit: 0})]
        carry = [self.small is not None and (stage >= 2 or i == 0) for i in range(len(first))]
        return first, rest, carry

    def take(self, first, rest):
        self.first, self.rest, self.got = first, rest, []
        for part, bit in zip(first, self.bits):
            got = permute(part.arrays[0], bit, self.count)
            self.got.append(Part([got], part.base, part.dims, part.rows))
        if self.small is not None:
            self.small = (first[0].arrays[0], 0, self.got[0].arrays[0], 0)

    def finish(self):
        parts = [self.rest[0], *self.got]
        return [p.arrays[0] for p in parts], tuple(p.base for p in parts)


def advance(info, scatters, after=(), through=()):
    inputs, plans, shapes, slots = [], [], [], []

    def find(array):
        for i, known in enumerate(inputs):
            if known is array:
                return i
        inputs.append(array)
        return len(inputs) - 1

    for scatter in scatters:
        first, rest, carry = scatter.jobs()
        for n, (pairs, fixed) in enumerate(first + rest):
            dims = tuple(d for d in pairs[0][0].dims if d not in fixed)
            rows = sum(a.hi - a.lo for a, _ in pairs)
            base, small = 0, ()
            if n < len(first) and carry[n]:
                own, at_own, got, at_got = scatter.small
                base, small = 2 * SMALL, (find(own), at_own, find(got), at_got)
            sums = []
            for index in range(2 ** len(dims)):
                where = dict(fixed)
                for i, d in enumerate(reversed(dims)):
                    where[d] = (index >> i) & 1
                to = base + index * rows
                for a, b in pairs:
                    (array_a, row_a), (array_b, row_b) = a.at(where), b.at(where)
                    size = a.hi - a.lo
                    sums.append((to, find(array_a), row_a, find(array_b), row_b, size))
                    to += size
            plans.append((sums, small))
            shapes.append(shaped((base + 2 ** len(dims) * rows, LANES), BF16))
            slots.append((base, dims, rows))
        scatter.counts = (len(first), len(rest))
    outs = call(
        functools.partial(add_kernel, plans), (1,), info, inputs, [near()] * len(inputs), shapes,
        [near()] * len(shapes), flops=10**6, moved=2**20, after=after, through=through,
    )
    handed = outs[len(slots) :]
    parts = [Part([out], *slot) for out, slot in zip(outs, slots)]
    sent = []
    for scatter in scatters:
        many, more = scatter.counts
        scatter.take(parts[:many], parts[many : many + more])
        sent += [p.arrays[0] for p in parts[:many]]
        parts = parts[many + more :]
    return sent, handed


def per_device(
    fast, n_wide, n_narrow,
    xp, xq, passage_lengths, query_lengths, pair_index, g_attn, w_query, w_key, w_value, w_out,
    bias_table, g_ffn, w_in, w_back, g_final, w_proj,
):
    lp, width = xp.shape
    lq = xq.shape[0]
    total = lp + lq
    heads = bias_table.shape[1]
    dk = width // heads
    ff = w_in.shape[1]
    segs = passage_lengths.shape[1]
    count = n_wide * n_narrow
    steps = heads // HS
    rows, cols = width // WB, width // NB
    wide_at, narrow_at = lax.axis_index("wide"), lax.axis_index("narrow")
    place = jnp.stack([wide_at, narrow_at]) if fast else jnp.zeros((2,), jnp.int32)
    info = (place.astype(jnp.int32), hbm(passage_lengths), hbm(query_lengths), hbm(pair_index))
    mm = 2 * total * width * width
    act, act32 = shaped((total, width), BF16), shaped((total, width), F32)
    act_hbm = pltpu.HBM((total, width), BF16)

    head_tile = pl.BlockSpec((total, HS * dk), lambda i, *_: (0, i))
    col_tile = pl.BlockSpec((width, HS * dk), lambda i, *_: (0, i))
    prob_tiles = [pl.BlockSpec((2 * HS, n // 2, n // 2), lambda i, *_: (i, 0, 0)) for n in (lp, lq)]
    x, normed, q, k, v, probs_p, probs_q, ctx = call(
        functools.partial(front_kernel, lp, lq, segs, dk),
        (steps,),
        info,
        (*(hbm(a) for a in (xp, xq, g_attn, w_query, w_key, w_value)), hbm(bias_table.T)),
        [whole(lp, width), whole(lq, width), whole(width)] + [col_tile] * 3
        + [whole(heads, BUCKETS)],
        [act, act_hbm, act_hbm, act_hbm, act_hbm]
        + [pltpu.HBM((2 * heads, n // 2, n // 2), BF16) for n in (lp, lq)]
        + [act],
        [near(), whole(total, width), head_tile, head_tile, head_tile, *prob_tiles, head_tile],
        [pltpu.VMEM((16, lp), F32)],
        flops=12 * 10**9,
        moved=13 * 2**20,
    )

    ff_tile = ff // NB
    ff_spec = pl.BlockSpec((total, ff_tile), lambda i, *_: (0, i))
    message = width + 128
    residual, normed_two, hidden, slope, output, pooled = call(
        functools.partial(ffn_kernel, lp, lq, segs),
        (NB,),
        info,
        (ctx, x, w_out, g_ffn, w_in, w_back, g_final),
        [near()] * 7,
        [
            act32, act, shaped((total, ff), BF16), pltpu.HBM((total, ff), BF16), act32,
            shaped((2 * segs, message), BF16),
        ],
        [near(), near(), near(), ff_spec, near(), near()],
        flops=9 * mm,
        moved=30 * 2**20,
        vmem=24,
    )

    if fast:
        one = jnp.concatenate([pooled] + [permute(pooled, b, count) for b in (Z0, Z1, Z0 | Z1)], axis=0)
        two = jnp.concatenate([one] + [permute(one, b, count) for b in (Y, X, Y | X)], axis=0)
        every = 2 * two.shape[0]
        query_loss, d_proj, d_pooled, gathered = call(
            functools.partial(loss_kernel, segs, GATHER),
            (1,),
            info,
            (two, permute(two, CORE, count), w_proj),
            [near(), near(), near()],
            [
                hbm_out((segs,), F32), shaped((every, width), BF16),
                shaped((2 * segs, width), F32), shaped((every, message), BF16),
            ],
            [whole(segs), near(), near(), near()],
            flops=10**9,
            moved=2**20,
        )
    else:
        gathered = lax.all_gather(pooled, AXES, axis=0, tiled=True)
        every = gathered.shape[0]
        block = jnp.arange(every, dtype=jnp.int32) // (2 * segs)
        loss, d_proj = loss_math(segs, block[:, None], block[None, :], gathered, w_proj)
        mine = (wide_at * n_narrow + narrow_at) * 2 * segs
        query_loss = lax.dynamic_slice_in_dim(loss, mine + segs, segs, 0)[:, 0]
        d_pooled = nt(lax.dynamic_slice_in_dim(d_proj, mine, 2 * segs, 0), w_proj)

    part1 = (2, WB // 2, 2, cols, LANES)
    block1 = pl.BlockSpec((2, 1, 2, cols, LANES), lambda i, *_: (0, i, 0, 0, 0))
    d_output, d_ffn, final_gain_grad, turned_ff, send1 = call(
        functools.partial(out_ff_send_kernel, lp, lq, segs),
        (WB // 2,),
        info,
        (d_pooled, output, g_final, hidden),
        [near(), near(), near(), near()],
        [act32, act, shaped((1, width), F32), shaped((width, total), BF16), shaped(part1, BF16)],
        [near(), near(), near(), near(), block1],
        flops=3 * mm,
        moved=10 * 2**20,
    )
    (keep1,) = call(
        out_ff_keep_kernel,
        (WB // 2,),
        info,
        (turned_ff, hidden),
        [near(), near()],
        [shaped(part1, BF16)],
        [block1],
        flops=2 * mm,
        moved=8 * 2**20,
    )

    after = []
    if fast:
        sc1 = Scatter((((0, 0, cols // 2),), ((0, cols // 2, cols),)), count)
        sc1.source(send1, [keep1], cols)
        after, _ = advance(info, [sc1])

    size2, size_o = 2 * rows, rows // 2
    part2 = shaped((2, WB, size2, LANES), BF16)
    part_o = shaped((2, WB, size_o, LANES), BF16)

    def tiles_at(first):
        return [
            near(),
            near(),
            pl.BlockSpec((total, ff_tile), lambda i, s, *_: (0, turn(i + first, s[1]))),
            near(),
        ]

    half2 = shaped((WB, size2, LANES), BF16)
    send2, keep2a, turned, so_far = call(
        ffn_back_first_kernel,
        (3,),
        info,
        (d_ffn, w_back, hbm(slope), w_in, normed_two),
        tiles_at(0) + [near()],
        [part2, half2, shaped((width, total), BF16), act32],
        [near()] * 4,
        flops=9 * mm,
        moved=16 * 2**20,
        vmem=16,
        after=after,
    )
    after = []
    if fast:
        after, (send2,) = advance(info, [sc1], [so_far], [send2])
    keep2b, d_resid, ffn_gain_grad, d_ctx, send_o, keep_o = call(
        ffn_back_last_kernel,
        (1,),
        info,
        (
            d_ffn, w_back, hbm(slope), w_in, turned, so_far, d_output, residual, g_ffn,
            ctx, w_out,
        ),
        tiles_at(3) + [near()] * 7,
        [half2, act32, shaped((1, width), F32), act, part_o, part_o],
        [near()] * 6,
        [pltpu.VMEM((width, total), BF16)],
        flops=5 * mm,
        moved=20 * 2**20,
        vmem=18,
        after=after,
    )

    after = []
    if fast:
        sc2 = Scatter((((0, 0, 128),), ((0, 128, size2), (1, 0, size_o))), count)
        sc2.source(send2, [keep2a, keep2b], size2)
        after, (send_o,) = advance(info, [sc1], [d_ctx], [send_o])
        sc2.source(send_o, [keep_o], size_o)
        more, _ = advance(info, [sc2], after)
        after = after + more
    d_qkv, sums = call(
        functools.partial(attn_back_kernel, dk, lp, lq),
        (steps,),
        info,
        (hbm(q), hbm(k), hbm(v), d_ctx, hbm(probs_p), hbm(probs_q)),
        [head_tile] * 4 + prob_tiles,
        [pltpu.HBM((3, total, width), BF16), shaped((16, lp), F32)],
        [pl.BlockSpec((3, total, HS * dk), lambda i, *_: (0, 0, i)), near()],
        flops=8 * 10**9,
        moved=16 * 2**20,
        after=after,
    )

    after = []
    if fast:
        after, _ = advance(info, [sc1, sc2], [sums])
    size3 = rows + rows // 2
    flat3 = shaped((16 * size3 + 16, LANES), BF16)
    send3, keep3 = call(
        functools.partial(qkv_grad_kernel, lp, heads),
        (3,),
        info,
        (
            hbm(normed), hbm(d_qkv), w_query, w_key, w_value, g_attn, ffn_gain_grad,
            final_gain_grad, sums,
        ),
        [whole(total, width), pl.BlockSpec((1, total, width), lambda i, *_: (i, 0, 0))]
        + [near()] * 7,
        [flat3, flat3],
        [near(), near()],
        [
            pltpu.VMEM((width, total), BF16), pltpu.VMEM((NB, WB, size3, LANES), BF16),
            pltpu.VMEM((width, width), F32), pltpu.VMEM((width, 128), F32),
        ],
        flops=3 * mm,
        moved=9 * 2**20,
        vmem=24,
        after=after,
    )

    after = []
    own_rows, own_cols = width // WB, width // NB
    square = hbm_out((own_rows, own_cols), F32)
    if fast:

        def finish(kernel, scatter, outs, after, more=()):
            parts, base = scatter.finish()
            parts = parts[:1] + list(more) + parts[1:]
            return call(
                functools.partial(kernel, base), (1,), info, parts, [near()] * len(parts), outs,
                [whole(*out_shape_of(out)) for out in outs], flops=10**6, moved=2**20, after=after,
            )

        (out_ff,) = finish(out_ff_finish_kernel, sc1, [hbm_out((cols, ff // WB), F32)], [keep3])
        out_ff = out_ff.T
        sc3 = Scatter((((0, 0, 80),), ((0, 80, size3),)), count, quad=True)
        after, (send3,) = advance(info, [sc2], [hbm(out_ff.T)], [send3])
        sc3.source(send3, [keep3], size3, small=True)


    def input_grad(tower, span, after):
        at = tower * (lp // span)
        tile = pl.BlockSpec((span, width), lambda *_: (at, 0))
        (grad,) = call(
            functools.partial(input_kernel, tower, segs),
            (1,),
            info,
            (hbm(d_qkv), w_query, w_key, w_value, hbm(d_resid), hbm(x), g_attn),
            [pl.BlockSpec((3, span, width), lambda *_: (0, at, 0))] + [near()] * 3
            + [tile, tile, near()],
            [hbm_out((span, width), F32)],
            [whole(span, width)],
            flops=mm,
            moved=6 * 2**20,
            vmem=20,
            after=after,
        )
        return grad

    grad_q = input_grad(1, lq, after)
    after = []
    if fast:
        after, _ = advance(info, [sc3], [hbm(grad_q)])
    grad_p = input_grad(0, lp, after)
    after = [hbm(grad_p)]
    if fast:
        after, _ = advance(info, [sc3, sc2], after)
    (proj_grad,) = call(
        proj_kernel,
        (1,),
        info,
        (gathered[:256], d_proj[:256]),
        [near(), near()],
        [square],
        [whole(own_rows, own_cols)],
        [pltpu.VMEM((width, width), F32)],
        flops=mm,
        moved=2**20,
        vmem=20,
        after=after,
    )

    if fast:
        after, _ = advance(info, [sc3], [hbm(proj_grad)])
        in_ff, out_w = finish(
            in_ff_finish_kernel, sc2, [hbm_out((rows, ff // NB), F32), square], after
        )
        query_w, key_w, value_w, gain_a, gain_f, gain_l, bias = finish(
            functools.partial(qkv_finish_kernel, heads), sc3,
            [square] * 3 + [hbm_out((width,), F32)] * 3 + [hbm_out((heads, BUCKETS), F32)],
            [hbm(out_w)], [sc3.first[0].arrays[0]],
        )
    else:
        own_rows, own_cols = width // n_wide, width // n_narrow
        left = lax.dynamic_slice(gathered, (0, wide_at * own_rows), (every, own_rows))
        right = lax.dynamic_slice(d_proj, (0, narrow_at * own_cols), (every, own_cols))
        proj_grad = tn(left, right)

        def blocks(send, keep):
            both = jnp.stack([keep, send], axis=1).astype(F32)
            return both.reshape((NB, WB) + both.shape[-2:])

        def spread(matrix):
            matrix = lax.psum_scatter(matrix, "wide", scatter_dimension=0, tiled=True)
            return lax.psum_scatter(matrix, "narrow", scatter_dimension=1, tiled=True)

        def side(part):
            half = part.shape[2] // 2
            return jnp.concatenate([part[:, :, :half], part[:, :, half:]], axis=3)

        def stack(part):
            half = part.shape[3] // 2
            return jnp.concatenate([part[..., :half], part[..., half:]], axis=2)

        def matrix(part):
            return part.transpose(1, 2, 0, 3).reshape(WB * part.shape[2], NB * part.shape[3])

        b1 = blocks(send1.reshape(2, WB, cols, LANES), keep1.reshape(2, WB, cols, LANES))
        b2 = blocks(send2, jnp.stack([keep2a, keep2b]))
        coded = keep3[16 * size3 :]
        b3 = blocks(*(a[: 16 * size3].reshape(2, WB, size3, LANES) for a in (send3, keep3)))
        out_ff = spread(matrix(b1.transpose(0, 1, 3, 2)))
        in_ff = spread(matrix(side(b2)))
        out_w = spread(matrix(stack(blocks(send_o, keep_o))))
        query_w = spread(matrix(b3[:, :, :rows, :cols]))
        key_w = spread(matrix(b3[:, :, :rows, cols:]))
        value_w = spread(matrix(stack(b3[:, :, rows:])))
        gains, bias = split_small(lax.psum(decode(coded), AXES), width, heads)
        gain_a, gain_f, gain_l = (gain[0] for gain in gains)
    return (
        query_loss, grad_p, grad_q, gain_a, query_w, key_w, value_w, out_w, bias.T, gain_f,
        in_ff, out_ff, gain_l, proj_grad,
    )


def solution(mesh):
    n_wide, n_narrow = mesh.shape["wide"], mesh.shape["narrow"]
    fast = (n_wide, n_narrow) == (WB, NB)
    rows = P(AXES, None)
    owned = P("wide", "narrow")
    return jax.shard_map(
        functools.partial(per_device, fast, n_wide, n_narrow),
        mesh=mesh,
        in_specs=(rows, rows, rows, rows, P(AXES)) + (P(),) * 11,
        out_specs=(
            P(AXES), rows, rows, P(), owned, owned, owned, owned, P(), P(),
            owned, owned, P(), owned,
        ),
        check_vma=False,
    )
```

```python
import functools

import jax
import jax.numpy as jnp
from jax import lax
from jax.experimental import pallas as pl
from jax.experimental.pallas import tpu as pltpu
from jax.sharding import PartitionSpec as P

BUCKETS = 32
MAX_DIST = 128
SCALE = 0.02
EPS = 1e-06
GELU = 0.7978845608028654
CUBE = 0.044715
HIGHEST = lax.Precision.HIGHEST
F32 = jnp.float32
BF16 = jnp.bfloat16
AXES = ("wide", "narrow")
NB = 4
WB = 8
CH = 128
LANES = 384
HS = 4
SMALL = 8


def bucket_edges():
    half = BUCKETS // 2
    exact = half // 2
    levels = half - exact
    ratio = MAX_DIST // exact
    edges = []
    for step in range(1, levels):
        target = exact**levels * ratio**step
        candidate = exact
        while candidate**levels < target:
            candidate += 1
        edges.append(candidate)
    return edges


def nn(a, b, **kw):
    return lax.dot_general(a, b, (((1,), (0,)), ((), ())), preferred_element_type=F32, **kw)


def tn(a, b):
    return lax.dot_general(a, b, (((0,), (0,)), ((), ())), preferred_element_type=F32)


def nt(a, b, **kw):
    return lax.dot_general(a, b, (((1,), (1,)), ((), ())), preferred_element_type=F32, **kw)


def bucket_hot(span, shift=0):
    shape = (BUCKETS, 2 * span)
    rel = lax.broadcasted_iota(jnp.int32, shape, 1) - shift
    rel = span - jnp.where(rel < 0, rel + 2 * span, rel)
    dist = jnp.abs(rel)
    half = BUCKETS // 2
    exact = half // 2
    far = jnp.full(shape, exact, jnp.int32)
    for edge in bucket_edges():
        far = far + jnp.where(dist >= edge, 1, 0)
    far = jnp.minimum(far, half - 1)
    bucket = jnp.where(dist < exact, dist, far) + jnp.where(rel > 0, half, 0)
    return bucket == lax.broadcasted_iota(jnp.int32, shape, 0)


def half_at(info, tower, segs, span):
    at, start = 0, 0
    for s in range(segs):
        size = info[2 + tower * segs + s]
        at = jnp.where(size == span // 2, start, at)
        start = start + size
    return at


def rolled_starts(info, tower, segs, span):
    at, start, starts = half_at(info, tower, segs, span), 0, []
    for s in range(segs):
        starts.append(jnp.where(start >= at, start - at, start - at + span))
        start = start + info[2 + tower * segs + s]
    return starts


def seg_bounds(info, segs, spans, shape, axis):
    at = lax.broadcasted_iota(jnp.int32, shape, axis)
    lo = jnp.zeros(shape, jnp.int32)
    hi = jnp.zeros(shape, jnp.int32)
    for tower, span in enumerate(spans):
        starts = rolled_starts(info, tower, segs, span)
        for s in range(segs):
            here = at == tower * segs + s
            start = starts[s] + tower * spans[0]
            lo = jnp.where(here, start, lo)
            hi = jnp.where(here, start + info[2 + tower * segs + s], hi)
    return lo, hi


def seg_of(info, tower, segs, span, shape, axis):
    at = lax.broadcasted_iota(jnp.int32, shape, axis) + span // 2
    seg = jnp.zeros(shape, jnp.int32)
    for start in rolled_starts(info, tower, segs, span):
        seg = seg + jnp.where(at >= start, 1, 0)
    return seg


def rms(v, gain):
    return v * lax.rsqrt(jnp.mean(v * v, axis=-1, keepdims=True) + EPS) * gain


def rms_back(v, gain, dy):
    r = lax.rsqrt(jnp.mean(v * v, axis=-1, keepdims=True) + EPS)
    gdy = gain * dy
    inner = jnp.mean(gdy * v, axis=-1, keepdims=True)
    return r * gdy - v * (r * r * r * inner), jnp.sum(dy * v * r, axis=0, keepdims=True)


def wide_row(gain):
    return gain[...].astype(F32).reshape(1, gain.shape[0])


def front_kernel(
    lp, lq, segs, dk, info, xp, xq, gain, wq, wk, wv, table,
    x, normed, q, k, v, probs_p, probs_q, ctx, rows,
):
    reach = lp // 2

    @pl.when(pl.program_id(0) == 0)
    def _():
        heads = table.shape[0]
        rows[:heads, :] = nn(table[...], bucket_hot(reach).astype(F32).astype(BF16))
        g = wide_row(gain)
        for tower, tokens, off, span in ((0, xp, 0, lp), (1, xq, lp, lq)):
            at = half_at(info, tower, segs, span)
            rolled = pltpu.roll(tokens[...].astype(F32), jnp.where(at == 0, 0, span - at), 0)
            here = slice(off, off + span)
            x[here, :] = rolled.astype(BF16)
            normed[here, :] = rms(rolled, g).astype(BF16)

    weights = jnp.concatenate([wq[...], wk[...], wv[...]], axis=1)
    qkv = nn(normed[...], weights).astype(BF16)
    cut = HS * dk
    q[...] = qkv[:, :cut]
    k[...] = qkv[:, cut : 2 * cut]
    v[...] = qkv[:, 2 * cut :]
    units = []
    for hh in range(HS):
        row = rows[pl.ds(HS * pl.program_id(0) + hh, 1), :]
        bias = pltpu.roll(jnp.broadcast_to(row, (CH, 2 * reach)), 0, 1, stride=1, stride_axis=0)
        cols = slice(hh * dk, (hh + 1) * dk)
        for tower, off, span, probs in ((0, 0, lp, probs_p), (1, lp, lq, probs_q)):
            half = span // 2
            full = jnp.concatenate(
                [bias[:, reach - r0 : reach - r0 + half] for r0 in range(0, half, CH)], axis=0
            )
            for part in range(2):
                here = slice(off + part * half, off + (part + 1) * half)
                units.append((tower, span, cols, here, full, probs, 2 * hh + part))
    scores = []
    for tower, span, cols, here, full, _, at in units:
        s = nt(k[here, cols], q[here, cols]) + full
        if at % 2:
            half = span // 2
            seg_j = seg_of(info, tower, segs, span, (half, 1), 0)
            seg_i = seg_of(info, tower, segs, span, (1, half), 1)
            s = jnp.where(seg_i == seg_j, s, -1000000000.0)
        scores.append(s)
    lows = []
    for (_, _, _, _, _, probs, at), s in zip(units, scores):
        e = jnp.exp(s - jnp.max(s, axis=0, keepdims=True))
        p = e * (1.0 / jnp.sum(e, axis=0, keepdims=True))
        p = p.astype(BF16)
        probs[at] = p
        lows.append(p)
    for (_, _, cols, here, _, _, _), p in zip(units, lows):
        ctx[here, cols] = tn(p, v[here, cols]).astype(BF16)


def ffn_kernel(
    lp, lq, segs, info, ctx, x, w_out, fgain, w_in, w_back, lgain,
    residual, normed_two, hidden, slope, output, pooled,
):
    step = pl.program_id(0)
    total = lp + lq

    @pl.when(step == 0)
    def _():
        g = wide_row(fgain)
        res = x[...].astype(F32) + nn(ctx[...], w_out[...])
        residual[...] = res
        output[...] = res
        normed_two[...] = rms(res, g).astype(BF16)

    part = 256
    parts = [slice(r0, r0 + part) for r0 in range(0, total, part)]

    tile = pl.ds(pl.multiple_of(step * slope.shape[1], slope.shape[1]), slope.shape[1])

    def up(here):
        return nn(normed_two[here, :], w_in[:, tile])

    u = up(parts[0])
    for n, here in enumerate(parts):
        following = up(parts[n + 1]) if n + 1 < len(parts) else None
        uu = u * u
        t = jnp.tanh(u * (GELU + (GELU * CUBE) * uu))
        half = 0.5 + 0.5 * t
        h = (u * half).astype(BF16)
        hidden[here, tile] = h
        slope[here, :] = (
            half + (u * (0.5 - (0.5 * t) * t)) * (GELU + (3.0 * GELU * CUBE) * uu)
        ).astype(BF16)
        output[here, :] += nn(h, w_back[tile, :])
        u = following

    @pl.when(step == pl.num_programs(0) - 1)
    def _():
        final = rms(output[...], wide_row(lgain))
        lo, hi = seg_bounds(info, segs, (lp, lq), (2 * segs, 1), 0)
        at = lax.broadcasted_iota(jnp.int32, (2 * segs, total), 1)
        hot = jnp.where((at >= lo) & (at < hi), 1.0, 0.0).astype(BF16)
        high = final.astype(BF16)
        mean = nn(hot, high) + nn(hot, (final - high.astype(F32)).astype(BF16))
        mean = mean / (hi - lo).astype(F32)
        width = final.shape[1]
        pooled[:, :width] = mean.astype(BF16)
        shape = (2 * segs, pooled.shape[1] - width)
        at_row = lax.broadcasted_iota(jnp.int32, shape, 0)
        at_col = lax.broadcasted_iota(jnp.int32, shape, 1)
        code = jnp.zeros(shape, jnp.int32)
        for s in range(segs):
            pair = info[2 + 2 * segs + s]
            code = jnp.where((at_row == segs + s) & (at_col == 0), pair // 64, code)
            code = jnp.where((at_row == segs + s) & (at_col == 1), pair % 64, code)
        pooled[:, width:] = code.astype(F32).astype(BF16)


def loss_math(segs, block_row, block_col, gathered, w_proj):
    count = gathered.shape[0]
    width = w_proj.shape[0]
    low = gathered[:, :width]
    code = gathered[:, width:].astype(F32)
    pair = code[:, 0:1] * 64.0 + code[:, 1:2]
    row = lax.broadcasted_iota(jnp.int32, (count, 1), 0) % (2 * segs)
    col = lax.broadcasted_iota(jnp.int32, (1, count), 1) % (2 * segs)
    number = (block_col * segs + col).astype(F32)
    is_query = row >= segs
    is_passage = col < segs
    proj = nn(low, w_proj)
    scale = lax.rsqrt(jnp.sum(proj * proj, axis=-1, keepdims=True) + EPS)
    embed = proj * scale
    embed_low = embed.astype(BF16)
    sims = nt(embed_low, embed_low) / SCALE
    masked = jnp.where(is_passage, sims, -1e30)
    top = jnp.max(masked, axis=1, keepdims=True)
    expo = jnp.where(is_passage, jnp.exp(masked - top), 0.0)
    total = jnp.sum(expo, axis=1, keepdims=True)
    hot = jnp.where(is_passage & (number == pair), 1.0, 0.0)
    loss = top + jnp.log(total) - jnp.sum(hot * sims, axis=1, keepdims=True)
    d_sims = jnp.where(is_query, (expo / total - hot) / SCALE, 0.0)
    d_embed = nn(d_sims + d_sims.T, embed_low.astype(F32), precision=HIGHEST)
    d_proj = (d_embed - embed * jnp.sum(embed * d_embed, axis=-1, keepdims=True)) * scale
    return loss, d_proj.astype(BF16)


def loss_kernel(segs, bits, info, near, far, w_proj, loss, d_proj, d_pooled, every):
    gathered = jnp.concatenate([near[...], far[...]], axis=0)
    every[...] = gathered
    count = gathered.shape[0]

    def device(shape, axis):
        place = lax.broadcasted_iota(jnp.int32, shape, axis) // (2 * segs)
        other = jnp.zeros(shape, jnp.int32)
        for at, bit in enumerate(bits):
            other = other + ((place >> at) & 1) * bit
        return other ^ (info[0] * NB + info[1])

    value, d_low = loss_math(
        segs, device((count, 1), 0), device((1, count), 1), gathered, w_proj[...]
    )
    flat = jnp.broadcast_to(value[: 2 * segs], (2 * segs, 128)).T
    loss[...] = flat[:1, segs : 2 * segs].reshape(segs)
    d_proj[...] = d_low
    d_pooled[...] = nt(d_low[: 2 * segs], w_proj[...])


def out_ff_blocks(info, rows, hidden, dst):
    size = 2 * LANES
    at = (pl.program_id(0) ^ (info[0] // 2)) * size
    res = nn(rows, hidden[:, pl.ds(pl.multiple_of(at, size), size)]).astype(BF16)
    cols = res.shape[0] // 2
    for y in range(2):
        for x in range(2):
            dst.at[y, 0][x ^ (info[0] % 2)] = res[
                y * cols : (y + 1) * cols, x * LANES : (x + 1) * LANES
            ]


def out_ff_send_kernel(
    lp, lq, segs, info, d_pooled, output, lgain, hidden,
    d_output, d_ffn, gain_grad, turned, send,
):
    total = lp + lq
    rows = output.shape[1] // NB
    half = 2 * rows

    @pl.when(pl.program_id(0) == 0)
    def _():
        lo, hi = seg_bounds(info, segs, (lp, lq), (1, 2 * segs), 1)
        lo_c, hi_c = seg_bounds(info, segs, (lp, lq), (2 * segs, 1), 0)
        at = lax.broadcasted_iota(jnp.int32, (total, 2 * segs), 0)
        hot = jnp.where((at >= lo) & (at < hi), 1.0, 0.0).astype(BF16)
        each = d_pooled[...] / (hi_c - lo_c).astype(F32)
        high = each.astype(BF16)
        dy = nn(hot, high) + nn(hot, (each - high.astype(F32)).astype(BF16))
        dv, dg = rms_back(output[...], wide_row(lgain), dy)
        d_output[...] = dv
        gain_grad[...] = dg
        low = dv.astype(BF16)
        d_ffn[...] = low
        flipped = low.T
        for n in range(NB):
            other = n ^ info[1]
            at_row = (other % 2) * half + (other // 2) * rows
            turned[pl.ds(pl.multiple_of(at_row, rows), rows), :] = flipped[
                n * rows : (n + 1) * rows
            ]

    out_ff_blocks(info, turned[half:, :], hidden, send)


def out_ff_keep_kernel(info, turned, hidden, keep):
    out_ff_blocks(info, turned[: turned.shape[0] // 2, :], hidden, keep)


def turn_rows(dst, value, wide):
    rows = value.shape[1] // WB
    flipped = value.T
    for w in range(WB):
        dst[pl.ds(pl.multiple_of((w ^ wide) * rows, rows), rows), :] = flipped[
            w * rows : (w + 1) * rows
        ]


def turn(step, narrow):
    return ((step % 2) * 2 + (1 - step // 2)) ^ narrow


def ffn_tile(number, d_ffn, w_back, slope, w_in, turned):
    size = slope.shape[1]
    tile = pl.ds(pl.multiple_of(number * size, size), size)
    d_up = (nt(d_ffn[...], w_back[tile, :]) * slope[...].astype(F32)).astype(BF16)
    res = nn(turned[...], d_up).astype(BF16)
    rows = res.shape[0] // WB
    blocks = jnp.concatenate(
        [
            res[:, half * LANES : (half + 1) * LANES].reshape(WB, rows, LANES)
            for half in range(2)
        ],
        axis=1,
    )
    return nt(d_up, w_in[:, tile]), blocks


def ffn_back_first_kernel(
    info, d_ffn, w_back, slope, w_in, normed_two, send, keep, turned, total
):
    step = pl.program_id(0)

    @pl.when(step == 0)
    def _():
        turn_rows(turned, normed_two[...], info[0])
        total[...] = jnp.zeros_like(total)

    part, blocks = ffn_tile(turn(step, info[1]), d_ffn, w_back, slope, w_in, turned)
    total[...] += part

    @pl.when(step < 2)
    def _():
        send[step] = blocks

    @pl.when(step == 2)
    def _():
        keep[...] = blocks


def ffn_back_last_kernel(
    info, d_ffn, w_back, slope, w_in, turned, so_far, d_output, residual, fgain, ctx, w_out,
    keep, d_resid, gain_grad, d_ctx, send_o, keep_o, turned_ctx,
):
    part, blocks = ffn_tile(turn(3, info[1]), d_ffn, w_back, slope, w_in, turned)
    keep[...] = blocks
    width = residual.shape[1]
    rows, cols = width // WB, width // NB
    dv, dg = rms_back(residual[...], wide_row(fgain), so_far[...] + part)
    dr = d_output[...] + dv
    d_resid[...] = dr
    gain_grad[...] = dg
    da = dr.astype(BF16)
    d_ctx[...] = nt(da, w_out[...]).astype(BF16)
    turn_rows(turned_ctx, ctx[...], info[0])
    grad = nn(turned_ctx[...], da)
    for n in range(NB):
        part = grad[:, n * cols : (n + 1) * cols].reshape(WB, rows, cols)
        part = jnp.concatenate([part[:, : rows // 2], part[:, rows // 2 :]], axis=2)
        part = part.astype(BF16)
        y = (n // 2) ^ (info[1] // 2)

        @pl.when((n % 2) == (info[1] % 2))
        def _():
            keep_o[y] = part

        @pl.when((n % 2) != (info[1] % 2))
        def _():
            send_o[y] = part


def attn_back_kernel(dk, lp, lq, info, q, k, v, d_ctx, probs_p, probs_q, d_qkv, sums):
    step = pl.program_id(0)
    reach = lp // 2
    size = HS * dk
    out = d_qkv.at[:, :, pl.ds(pl.multiple_of(step * size, size), size)]

    @pl.when(step == 0)
    def _():
        sums[...] = jnp.zeros_like(sums)

    units = []
    for hh in range(HS):
        cols = slice(hh * dk, (hh + 1) * dk)
        for off, span, probs in ((0, lp, probs_p), (lp, lq, probs_q)):
            half = span // 2
            for part in range(2):
                here = slice(off + part * half, off + (part + 1) * half)
                units.append((hh, cols, here, half, probs, 2 * hh + part))
    d_probs = [nt(v[here, cols], d_ctx[here, cols]) for _, cols, here, _, _, _ in units]
    tiles = [[jnp.zeros((CH, CH), F32)] * (2 * reach // CH) for _ in range(HS)]
    lows = []
    for (hh, _, _, half, probs, at), d_prob in zip(units, d_probs):
        p = probs[at].astype(F32)
        t = p * d_prob
        ds = t - p * jnp.sum(t, axis=0, keepdims=True)
        lows.append(ds.astype(BF16))
        for a in range(half // CH):
            for b in range(half // CH):
                to = b + reach // CH - a
                piece = ds[a * CH : (a + 1) * CH, b * CH : (b + 1) * CH]
                tiles[hh][to] = tiles[hh][to] + piece
    for (_, cols, here, _, probs, at), low in zip(units, lows):
        out[0, here, cols] = tn(low, k[here, cols]).astype(BF16)
        out[1, here, cols] = nn(low, q[here, cols]).astype(BF16)
        out[2, here, cols] = nn(probs[at], d_ctx[here, cols]).astype(BF16)
    at_i = lax.broadcasted_iota(jnp.int32, (CH, CH), 0)
    at_j = lax.broadcasted_iota(jnp.int32, (CH, CH), 1)
    mirror = jnp.where(at_i + at_j == CH - 1, 1.0, 0.0).astype(BF16)
    for hh in range(HS):
        flipped = nn(mirror, jnp.concatenate(tiles[hh], axis=1).astype(BF16))
        turn = pltpu.roll(flipped, 0, 1, stride=1, stride_axis=0)
        sums[pl.ds(HS * step + hh, 1), :] = jnp.sum(turn, axis=0, keepdims=True)


def qkv_grad_kernel(
    lp, heads, info, normed, d_qkv, wq, wk, wv, gain, g_ffn, g_final, sums,
    send, keep, turned, blocks, column,
):
    width = normed.shape[1]
    rows, cols = width // WB, width // NB
    size = blocks.shape[1] * blocks.shape[2]

    def gradient(grads, weight):
        grad = nn(turned[...], grads)
        for w in range(WB):
            at = pl.ds(pl.multiple_of((w ^ info[0]) * rows, rows), rows)
            part = grad[w * rows : (w + 1) * rows, :] * weight[at, :].astype(F32)
            column[at, :] += jnp.broadcast_to(
                jnp.sum(part, axis=1, keepdims=True), (rows, column.shape[1])
            )
        return grad

    turn_rows(turned, normed[...], info[0])
    column[...] = jnp.zeros_like(column)
    gq, gk = gradient(d_qkv[0], wq), gradient(d_qkv[1], wk)
    for n in range(NB):
        here = slice(n * cols, (n + 1) * cols)
        both = jnp.concatenate([gq[:, here], gk[:, here]], axis=1).astype(BF16)
        blocks[n, :, :rows, :] = both.reshape(WB, rows, LANES)
    gv = gradient(d_qkv[2], wv)
    for n in range(NB):
        part = gv[:, n * cols : (n + 1) * cols].reshape(WB, rows, cols)
        part = jnp.concatenate([part[:, : rows // 2], part[:, rows // 2 :]], axis=2)
        blocks[n, :, rows:, :] = part.astype(BF16)
    core, y0 = info[1] % 2, info[1] // 2
    for y in range(2):
        here = slice(y * size, (y + 1) * size)
        send[here, :] = blocks[(y ^ y0) * 2 + (1 - core)].reshape(size, LANES)
        keep[here, :] = blocks[(y ^ y0) * 2 + core].reshape(size, LANES)
    g_attn = column[...].T[:1, :] / wide_row(gain)
    hot = bucket_hot(lp // 2, CH - 1).astype(F32)
    bias = nt(sums[...], hot, precision=HIGHEST)
    pieces = []
    for grad in (g_attn, g_ffn[...], g_final[...]):
        pieces += [grad[:, i : i + LANES] for i in range(0, width, LANES)]
    pieces.append(jnp.concatenate([bias[h : h + 1, :] for h in range(heads)], axis=1))
    pieces.append(jnp.zeros((SMALL - len(pieces), LANES), F32))
    small = encode(jnp.concatenate(pieces, axis=0))
    send[2 * size :, :] = small
    keep[2 * size :, :] = small


def input_kernel(segs, info, d_qkv, wq, wk, wv, d_resid, x, gain, grad_p, grad_q):
    off = 0
    for tower, grad in enumerate((grad_p, grad_q)):
        span = grad.shape[0]
        here = slice(off, off + span)
        off += span
        dn = nt(d_qkv[0, here], wq[...]) + nt(d_qkv[1, here], wk[...])
        dn = dn + nt(d_qkv[2, here], wv[...])
        v = x[here, :].astype(F32)
        r = lax.rsqrt(jnp.mean(v * v, axis=-1, keepdims=True) + EPS)
        gdy = wide_row(gain) * dn
        inner = jnp.mean(gdy * v, axis=-1, keepdims=True)
        out = d_resid[here, :] + (r * gdy - v * (r * r * r * inner))
        grad[...] = pltpu.roll(out, half_at(info, tower, segs, span), 0)


def proj_kernel(info, every, d_proj, proj_grad, full):
    rows, cols = proj_grad.shape
    width = full.shape[0]
    full[...] = tn(every[:, :width], d_proj[...])
    mine = full[pl.ds(pl.multiple_of(info[0] * rows, 8), rows), :]
    for n in range(width // cols):

        @pl.when(info[1] == n)
        def _():
            proj_grad[...] = mine[:, n * cols : (n + 1) * cols]


class Info:
    def __init__(self, place, passages, queries, pairs):
        segs = passages.shape[1]
        self.at = [lambda: place[0], lambda: place[1]]
        self.at += [functools.partial(lambda r, i: r[0, i], passages, i) for i in range(segs)]
        self.at += [functools.partial(lambda r, i: r[0, i], queries, i) for i in range(segs)]
        self.at += [functools.partial(lambda r, i: r[i], pairs, i) for i in range(segs)]

    def __getitem__(self, i):
        return self.at[i]()


def call(
    kernel, grid, info, args, in_specs, outs, out_specs, scratch=(), flops=0, moved=0,
    vmem=16, after=(), through=(), through_specs=(),
):
    count, more = len(args), len(after) + len(through)
    outs, out_specs = list(outs), list(out_specs)
    made = len(outs)
    aliases = {len(info) + count + len(after) + i: made + i for i in range(len(through))}
    outs += [(hbm_out if through_specs else shaped)(a.shape, a.dtype) for a in through]
    out_specs += through_specs or [pl.BlockSpec(memory_space=pl.ANY)] * len(through)
    hidden = 0 if through_specs else len(through)

    def body(*refs):
        scalars, refs = refs[: len(info)], refs[len(info) :]
        results = refs[count + more :]
        kernel(
            Info(*scalars) if scalars else None,
            *refs[:count],
            *results[:made],
            *results[made + hidden :],
        )

    return pl.pallas_call(
        body,
        grid_spec=pltpu.PrefetchScalarGridSpec(
            num_scalar_prefetch=len(info),
            grid=grid,
            in_specs=list(in_specs) + [pl.BlockSpec(memory_space=pl.ANY)] * more,
            out_specs=out_specs,
            scratch_shapes=list(scratch),
        ),
        out_shape=outs,
        input_output_aliases=aliases,
        compiler_params=pltpu.CompilerParams(vmem_limit_bytes=vmem * 2**20),
        cost_estimate=pl.CostEstimate(flops=flops, bytes_accessed=moved, transcendentals=0),
    )(*info, *args, *after, *through)


def hbm(array):
    return pltpu.with_memory_space_constraint(array, pltpu.HBM)


def near(*shape):
    return pl.BlockSpec(memory_space=pltpu.VMEM)


def whole(*shape):
    return pl.BlockSpec(shape, lambda *_: (0,) * len(shape), pipeline_mode=pl.Buffered(1))


def hbm_out(shape, dtype):
    return pltpu.HBM(shape, dtype)


def out_shape_of(out):
    return out.inner_aval.shape


def shaped(shape, dtype):
    return jax.ShapeDtypeStruct(shape, dtype)


def permute(array, bit, count):
    return lax.ppermute(array, AXES, [(i, i ^ bit) for i in range(count)])


CORE, Y, X, Z0, Z1 = 1, 2, 4, 8, 16
GATHER = (Z0, Z1, Y, X, CORE)


def own_sum(base, refs):
    parts = [r[b:, :].astype(F32) for b, r in zip(base, refs)]
    while len(parts) > 1:
        parts = [a + b for a, b in zip(parts[::2], parts[1::2])]
    return parts[0]


def out_ff_finish_kernel(base, info, *refs):
    refs[-1][...] = own_sum(base, refs[:-1])


def in_ff_finish_kernel(base, info, *refs):
    *parts, in_ff, out_w = refs
    total = own_sum(base, parts)
    rows, cols = out_w.shape
    in_ff[...] = jnp.concatenate([total[:rows], total[rows : 2 * rows]], axis=1)
    out_w[...] = jnp.concatenate([total[2 * rows :, :cols], total[2 * rows :, cols:]], axis=0)


def split_small(small, width, heads):
    per = width // LANES
    gains = [
        jnp.concatenate([small[g * per + i : g * per + i + 1] for i in range(per)], axis=1)
        for g in range(3)
    ]
    row = small[3 * per : 3 * per + 1]
    bias = [row[:, h * BUCKETS : (h + 1) * BUCKETS] for h in range(heads)]
    return gains, jnp.concatenate(bias, axis=0)


def qkv_finish_kernel(heads, base, info, *refs):
    rest, own, *got, query_w, key_w, value_w, gain_a, gain_f, gain_l, bias = refs
    total = own_sum(base, (rest, *got))
    rows, cols = query_w.shape
    query_w[...] = total[:rows, :cols]
    key_w[...] = total[:rows, cols:]
    value_w[...] = jnp.concatenate([total[rows:, :cols], total[rows:, cols:]], axis=0)
    small = [decode(r[: 2 * SMALL, :]) for r in (own, *got)]
    small = (small[0] + small[1]) + (small[2] + small[3])
    gains, table = split_small(small, gain_a.shape[0], heads)
    for ref, gain in zip((gain_a, gain_f, gain_l), gains):
        ref[...] = gain.reshape(gain.shape[1])
    bias[...] = table


def encode(values):
    high = values.astype(BF16).astype(F32)
    return jnp.concatenate([high, values - high], axis=0).astype(BF16)


def decode(coded):
    half = coded.shape[0] // 2
    return coded[:half].astype(F32) + coded[half:].astype(F32)


class Part:
    def __init__(self, arrays, base, dims, rows, lo=0, hi=None):
        self.arrays, self.base, self.dims, self.rows = arrays, base, dims, rows
        self.lo, self.hi = lo, rows if hi is None else hi

    def at(self, where):
        dims, which = self.dims, 0
        if len(self.arrays) > 1:
            which, dims = where[dims[0]], dims[1:]
        index = 0
        for bit in dims:
            index = index * 2 + where[bit]
        return self.arrays[which], self.base + index * self.rows + self.lo


def add_kernel(plans, info, *refs):
    outs = refs[len(refs) - len(plans) :]
    for (sums, small), out in zip(plans, outs):
        if small:
            total = decode(refs[small[0]][small[1] : small[1] + 2 * SMALL, :])
            total = total + decode(refs[small[2]][small[3] : small[3] + 2 * SMALL, :])
            out[: 2 * SMALL, :] = encode(total)
        for to, a, at_a, b, at_b, rows in sums:
            out[to : to + rows, :] = (
                refs[a][at_a : at_a + rows, :] + refs[b][at_b : at_b + rows, :]
            )


class Scatter:
    def __init__(self, groups, count, quad=False):
        self.count, self.groups, self.quad = count, groups, quad
        self.sources = []
        self.small = None
        self.stage = -1

    def source(self, send, keeps, rows, small=False):
        send = send.reshape(-1, LANES)
        keeps = [k.reshape(-1, LANES) for k in keeps]
        got = permute(send, CORE, self.count)
        self.sources.append((keeps, got, rows))
        if small:
            at = 16 * rows
            self.small = (keeps[0], at, got, at)

    def jobs(self):
        self.stage += 1
        stage = self.stage
        if stage == 0:
            dims = (Y, Z1, Z0, X)
            groups = [
                [
                    (
                        Part(self.sources[n][0], 0, dims, self.sources[n][2], lo, hi),
                        Part([self.sources[n][1]], 0, dims, self.sources[n][2], lo, hi),
                    )
                    for n, lo, hi in group
                ]
                for group in self.groups
            ]
        else:
            groups = [[pair] for pair in zip(self.rest, self.got)]
        if stage < 2:
            bits = ((Y, X), (X, Y))[stage]
            first = [(g, {b: 1}) for g, b in zip(groups, bits)]
            rest = [(g, {b: 0}) for g, b in zip(groups, bits)]
            self.bits = bits
        else:
            merged = [pair for group in groups for pair in group]
            if self.quad:
                self.bits = (Z0, Z1, Z0 | Z1)
                first = [(merged, {Z0: a, Z1: b}) for a, b in ((1, 0), (0, 1), (1, 1))]
                rest = [(merged, {Z0: 0, Z1: 0})]
            else:
                bit = (Z0, Z1)[stage - 2]
                self.bits = (bit,)
                first, rest = [(merged, {bit: 1})], [(merged, {bit: 0})]
        carry = [self.small is not None and (stage >= 2 or i == 0) for i in range(len(first))]
        return first, rest, carry

    def take(self, first, rest):
        self.first, self.rest, self.got = first, rest, []
        for part, bit in zip(first, self.bits):
            got = permute(part.arrays[0], bit, self.count)
            self.got.append(Part([got], part.base, part.dims, part.rows))
        if self.small is not None:
            self.small = (first[0].arrays[0], 0, self.got[0].arrays[0], 0)

    def finish(self):
        parts = [self.rest[0], *self.got]
        return [p.arrays[0] for p in parts], tuple(p.base for p in parts)


def advance(info, scatters, after=(), through=()):
    inputs, plans, shapes, slots = [], [], [], []

    def find(array):
        for i, known in enumerate(inputs):
            if known is array:
                return i
        inputs.append(array)
        return len(inputs) - 1

    for scatter in scatters:
        first, rest, carry = scatter.jobs()
        for n, (pairs, fixed) in enumerate(first + rest):
            dims = tuple(d for d in pairs[0][0].dims if d not in fixed)
            rows = sum(a.hi - a.lo for a, _ in pairs)
            base, small = 0, ()
            if n < len(first) and carry[n]:
                own, at_own, got, at_got = scatter.small
                base, small = 2 * SMALL, (find(own), at_own, find(got), at_got)
            sums = []
            for index in range(2 ** len(dims)):
                where = dict(fixed)
                for i, d in enumerate(reversed(dims)):
                    where[d] = (index >> i) & 1
                to = base + index * rows
                for a, b in pairs:
                    (array_a, row_a), (array_b, row_b) = a.at(where), b.at(where)
                    size = a.hi - a.lo
                    sums.append((to, find(array_a), row_a, find(array_b), row_b, size))
                    to += size
            plans.append((sums, small))
            shapes.append(shaped((base + 2 ** len(dims) * rows, LANES), BF16))
            slots.append((base, dims, rows))
        scatter.counts = (len(first), len(rest))
    outs = call(
        functools.partial(add_kernel, plans), (1,), info, inputs, [near()] * len(inputs), shapes,
        [near()] * len(shapes), flops=10**6, moved=2**20, after=after, through=through,
    )
    handed = outs[len(slots) :]
    parts = [Part([out], *slot) for out, slot in zip(outs, slots)]
    sent = []
    for scatter in scatters:
        many, more = scatter.counts
        scatter.take(parts[:many], parts[many : many + more])
        sent += [p.arrays[0] for p in parts[:many]]
        parts = parts[many + more :]
    return sent, handed


def per_device(
    fast, n_wide, n_narrow,
    xp, xq, passage_lengths, query_lengths, pair_index, g_attn, w_query, w_key, w_value, w_out,
    bias_table, g_ffn, w_in, w_back, g_final, w_proj,
):
    lp, width = xp.shape
    lq = xq.shape[0]
    total = lp + lq
    heads = bias_table.shape[1]
    dk = width // heads
    ff = w_in.shape[1]
    segs = passage_lengths.shape[1]
    count = n_wide * n_narrow
    steps = heads // HS
    rows, cols = width // WB, width // NB
    wide_at, narrow_at = lax.axis_index("wide"), lax.axis_index("narrow")
    place = jnp.stack([wide_at, narrow_at]) if fast else jnp.zeros((2,), jnp.int32)
    info = (place.astype(jnp.int32), hbm(passage_lengths), hbm(query_lengths), hbm(pair_index))
    mm = 2 * total * width * width
    act, act32 = shaped((total, width), BF16), shaped((total, width), F32)
    act_hbm = pltpu.HBM((total, width), BF16)

    head_tile = pl.BlockSpec((total, HS * dk), lambda i, *_: (0, i))
    col_tile = pl.BlockSpec((width, HS * dk), lambda i, *_: (0, i))
    prob_tiles = [pl.BlockSpec((2 * HS, n // 2, n // 2), lambda i, *_: (i, 0, 0)) for n in (lp, lq)]
    x, normed, q, k, v, probs_p, probs_q, ctx = call(
        functools.partial(front_kernel, lp, lq, segs, dk),
        (steps,),
        info,
        (*(hbm(a) for a in (xp, xq, g_attn, w_query, w_key, w_value)), hbm(bias_table.T)),
        [whole(lp, width), whole(lq, width), whole(width)] + [col_tile] * 3
        + [whole(heads, BUCKETS)],
        [act, act_hbm, act_hbm, act_hbm, act_hbm]
        + [pltpu.HBM((2 * heads, n // 2, n // 2), BF16) for n in (lp, lq)]
        + [act],
        [near(), whole(total, width), head_tile, head_tile, head_tile, *prob_tiles, head_tile],
        [pltpu.VMEM((16, lp), F32)],
        flops=12 * 10**9,
        moved=13 * 2**20,
    )

    ff_tile = ff // NB
    ff_spec = pl.BlockSpec((total, ff_tile), lambda i, *_: (0, i))
    message = width + 128
    residual, normed_two, hidden, slope, output, pooled = call(
        functools.partial(ffn_kernel, lp, lq, segs),
        (NB,),
        info,
        (ctx, x, w_out, g_ffn, w_in, w_back, g_final),
        [near()] * 7,
        [
            act32, act, shaped((total, ff), BF16), pltpu.HBM((total, ff), BF16), act32,
            shaped((2 * segs, message), BF16),
        ],
        [near(), near(), near(), ff_spec, near(), near()],
        flops=9 * mm,
        moved=30 * 2**20,
        vmem=24,
    )

    if fast:
        one = jnp.concatenate([pooled] + [permute(pooled, b, count) for b in (Z0, Z1, Z0 | Z1)], axis=0)
        two = jnp.concatenate([one] + [permute(one, b, count) for b in (Y, X, Y | X)], axis=0)
        every = 2 * two.shape[0]
        query_loss, d_proj, d_pooled, gathered = call(
            functools.partial(loss_kernel, segs, GATHER),
            (1,),
            info,
            (two, permute(two, CORE, count), w_proj),
            [near(), near(), near()],
            [
                hbm_out((segs,), F32), shaped((every, width), BF16),
                shaped((2 * segs, width), F32), shaped((every, message), BF16),
            ],
            [whole(segs), near(), near(), near()],
            flops=10**9,
            moved=2**20,
        )
    else:
        gathered = lax.all_gather(pooled, AXES, axis=0, tiled=True)
        every = gathered.shape[0]
        block = jnp.arange(every, dtype=jnp.int32) // (2 * segs)
        loss, d_proj = loss_math(segs, block[:, None], block[None, :], gathered, w_proj)
        mine = (wide_at * n_narrow + narrow_at) * 2 * segs
        query_loss = lax.dynamic_slice_in_dim(loss, mine + segs, segs, 0)[:, 0]
        d_pooled = nt(lax.dynamic_slice_in_dim(d_proj, mine, 2 * segs, 0), w_proj)

    part1 = (2, WB // 2, 2, cols, LANES)
    block1 = pl.BlockSpec((2, 1, 2, cols, LANES), lambda i, *_: (0, i, 0, 0, 0))
    d_output, d_ffn, final_gain_grad, turned_ff, send1 = call(
        functools.partial(out_ff_send_kernel, lp, lq, segs),
        (WB // 2,),
        info,
        (d_pooled, output, g_final, hidden),
        [near(), near(), near(), near()],
        [act32, act, shaped((1, width), F32), shaped((width, total), BF16), shaped(part1, BF16)],
        [near(), near(), near(), near(), block1],
        flops=3 * mm,
        moved=10 * 2**20,
    )
    (keep1,) = call(
        out_ff_keep_kernel,
        (WB // 2,),
        info,
        (turned_ff, hidden),
        [near(), near()],
        [shaped(part1, BF16)],
        [block1],
        flops=2 * mm,
        moved=8 * 2**20,
    )

    after = []
    if fast:
        sc1 = Scatter((((0, 0, cols // 2),), ((0, cols // 2, cols),)), count, quad=True)
        sc1.source(send1, [keep1], cols)
        after, _ = advance(info, [sc1])

    size2, size_o = 2 * rows, rows // 2
    part2 = shaped((2, WB, size2, LANES), BF16)
    part_o = shaped((2, WB, size_o, LANES), BF16)

    def tiles_at(first):
        return [
            near(),
            near(),
            pl.BlockSpec((total, ff_tile), lambda i, s, *_: (0, turn(i + first, s[1]))),
            near(),
        ]

    half2 = shaped((WB, size2, LANES), BF16)
    send2, keep2a, turned, so_far = call(
        ffn_back_first_kernel,
        (3,),
        info,
        (d_ffn, w_back, hbm(slope), w_in, normed_two),
        tiles_at(0) + [near()],
        [part2, half2, shaped((width, total), BF16), act32],
        [near()] * 4,
        flops=9 * mm,
        moved=16 * 2**20,
        vmem=16,
        after=after,
    )
    after = []
    if fast:
        after, (send2,) = advance(info, [sc1], [so_far], [send2])
    keep2b, d_resid, ffn_gain_grad, d_ctx, send_o, keep_o = call(
        ffn_back_last_kernel,
        (1,),
        info,
        (
            d_ffn, w_back, hbm(slope), w_in, turned, so_far, d_output, residual, g_ffn,
            ctx, w_out,
        ),
        tiles_at(3) + [near()] * 7,
        [half2, act32, shaped((1, width), F32), act, part_o, part_o],
        [near()] * 6,
        [pltpu.VMEM((width, total), BF16)],
        flops=5 * mm,
        moved=20 * 2**20,
        vmem=18,
        after=after,
    )

    after = []
    if fast:
        sc2 = Scatter((((0, 0, 128),), ((0, 128, size2), (1, 0, size_o))), count)
        sc2.source(send2, [keep2a, keep2b], size2)
        after, (send_o,) = advance(info, [sc1], [d_ctx], [send_o])
        sc2.source(send_o, [keep_o], size_o)
        more, _ = advance(info, [sc2], after)
        after = after + more
    d_qkv, sums = call(
        functools.partial(attn_back_kernel, dk, lp, lq),
        (steps,),
        info,
        (hbm(q), hbm(k), hbm(v), d_ctx, hbm(probs_p), hbm(probs_q)),
        [head_tile] * 4 + prob_tiles,
        [shaped((3, total, width), BF16), shaped((16, lp), F32)],
        [near(), near()],
        flops=8 * 10**9,
        moved=16 * 2**20,
        after=after,
    )

    size3 = rows + rows // 2
    flat3 = shaped((16 * size3 + 16, LANES), BF16)
    send3, keep3 = call(
        functools.partial(qkv_grad_kernel, lp, heads),
        (1,),
        info,
        (
            normed, d_qkv, w_query, w_key, w_value, g_attn, ffn_gain_grad,
            final_gain_grad, sums,
        ),
        [near()] * 9,
        [flat3, flat3],
        [near(), near()],
        [
            pltpu.VMEM((width, total), BF16), pltpu.VMEM((NB, WB, size3, LANES), BF16),
            pltpu.VMEM((width, 128), F32),
        ],
        flops=3 * mm,
        moved=9 * 2**20,
        vmem=24,
        after=after,
    )

    after = []
    own_rows, own_cols = width // WB, width // NB
    square = hbm_out((own_rows, own_cols), F32)
    if fast:

        def finish(kernel, scatter, outs, after, more=()):
            parts, base = scatter.finish()
            parts = parts[:1] + list(more) + parts[1:]
            return call(
                functools.partial(kernel, base), (1,), info, parts, [near()] * len(parts), outs,
                [whole(*out_shape_of(out)) for out in outs], flops=10**6, moved=2**20, after=after,
            )

        sc3 = Scatter((((0, 0, 80),), ((0, 80, size3),)), count, quad=True)
        (out_ff,) = finish(out_ff_finish_kernel, sc1, [hbm_out((cols, ff // WB), F32)], [keep3])
        after, (send3,) = advance(info, [sc2], [hbm(out_ff)], [send3])
        out_ff = out_ff.T
        sc3.source(send3, [keep3], size3, small=True)

    grad_p, grad_q = call(
        functools.partial(input_kernel, segs),
        (1,),
        info,
        (d_qkv, w_query, w_key, w_value, d_resid, x, g_attn),
        [near()] * 7,
        [hbm_out((lp, width), F32), hbm_out((lq, width), F32)],
        [whole(lp, width), whole(lq, width)],
        flops=3 * mm,
        moved=6 * 2**20,
        vmem=20,
        after=after,
    )
    after = [hbm(grad_p)]
    if fast:
        after, _ = advance(info, [sc3, sc2], after)
    (proj_grad,) = call(
        proj_kernel,
        (1,),
        info,
        (gathered[:256], d_proj[:256]),
        [near(), near()],
        [square],
        [whole(own_rows, own_cols)],
        [pltpu.VMEM((width, width), F32)],
        flops=mm,
        moved=2**20,
        vmem=20,
        after=after,
    )

    if fast:
        after, _ = advance(info, [sc3, sc2], [hbm(proj_grad)])
        after, _ = advance(info, [sc3], after)
        in_ff, out_w = finish(
            in_ff_finish_kernel, sc2, [hbm_out((rows, ff // NB), F32), square], after
        )
        query_w, key_w, value_w, gain_a, gain_f, gain_l, bias = finish(
            functools.partial(qkv_finish_kernel, heads), sc3,
            [square] * 3 + [hbm_out((width,), F32)] * 3 + [hbm_out((heads, BUCKETS), F32)],
            [hbm(out_w)], [sc3.first[0].arrays[0]],
        )
    else:
        own_rows, own_cols = width // n_wide, width // n_narrow
        left = lax.dynamic_slice(gathered, (0, wide_at * own_rows), (every, own_rows))
        right = lax.dynamic_slice(d_proj, (0, narrow_at * own_cols), (every, own_cols))
        proj_grad = tn(left, right)

        def blocks(send, keep):
            both = jnp.stack([keep, send], axis=1).astype(F32)
            return both.reshape((NB, WB) + both.shape[-2:])

        def spread(matrix):
            matrix = lax.psum_scatter(matrix, "wide", scatter_dimension=0, tiled=True)
            return lax.psum_scatter(matrix, "narrow", scatter_dimension=1, tiled=True)

        def side(part):
            half = part.shape[2] // 2
            return jnp.concatenate([part[:, :, :half], part[:, :, half:]], axis=3)

        def stack(part):
            half = part.shape[3] // 2
            return jnp.concatenate([part[..., :half], part[..., half:]], axis=2)

        def matrix(part):
            return part.transpose(1, 2, 0, 3).reshape(WB * part.shape[2], NB * part.shape[3])

        b1 = blocks(send1.reshape(2, WB, cols, LANES), keep1.reshape(2, WB, cols, LANES))
        b2 = blocks(send2, jnp.stack([keep2a, keep2b]))
        coded = keep3[16 * size3 :]
        b3 = blocks(*(a[: 16 * size3].reshape(2, WB, size3, LANES) for a in (send3, keep3)))
        out_ff = spread(matrix(b1.transpose(0, 1, 3, 2)))
        in_ff = spread(matrix(side(b2)))
        out_w = spread(matrix(stack(blocks(send_o, keep_o))))
        query_w = spread(matrix(b3[:, :, :rows, :cols]))
        key_w = spread(matrix(b3[:, :, :rows, cols:]))
        value_w = spread(matrix(stack(b3[:, :, rows:])))
        gains, bias = split_small(lax.psum(decode(coded), AXES), width, heads)
        gain_a, gain_f, gain_l = (gain[0] for gain in gains)
    return (
        query_loss, grad_p, grad_q, gain_a, query_w, key_w, value_w, out_w, bias.T, gain_f,
        in_ff, out_ff, gain_l, proj_grad,
    )


def solution(mesh):
    n_wide, n_narrow = mesh.shape["wide"], mesh.shape["narrow"]
    fast = (n_wide, n_narrow) == (WB, NB)
    rows = P(AXES, None)
    owned = P("wide", "narrow")
    return jax.shard_map(
        functools.partial(per_device, fast, n_wide, n_narrow),
        mesh=mesh,
        in_specs=(rows, rows, rows, rows, P(AXES)) + (P(),) * 11,
        out_specs=(
            P(AXES), rows, rows, P(), owned, owned, owned, owned, P(), P(),
            owned, owned, P(), owned,
        ),
        check_vma=False,
    )
```

```python
import functools

import jax
import jax.numpy as jnp
from jax import lax
from jax.experimental import pallas as pl
from jax.experimental.pallas import tpu as pltpu
from jax.sharding import PartitionSpec as P

BUCKETS = 32
MAX_DIST = 128
SCALE = 0.02
EPS = 1e-06
GELU = 0.7978845608028654
CUBE = 0.044715
HIGHEST = lax.Precision.HIGHEST
F32 = jnp.float32
BF16 = jnp.bfloat16
AXES = ("wide", "narrow")
NB = 4
WB = 8
CH = 128
LANES = 384
HS = 4
SMALL = 8


def bucket_edges():
    half = BUCKETS // 2
    exact = half // 2
    levels = half - exact
    ratio = MAX_DIST // exact
    edges = []
    for step in range(1, levels):
        target = exact**levels * ratio**step
        candidate = exact
        while candidate**levels < target:
            candidate += 1
        edges.append(candidate)
    return edges


def nn(a, b, **kw):
    return lax.dot_general(a, b, (((1,), (0,)), ((), ())), preferred_element_type=F32, **kw)


def tn(a, b):
    return lax.dot_general(a, b, (((0,), (0,)), ((), ())), preferred_element_type=F32)


def nt(a, b, **kw):
    return lax.dot_general(a, b, (((1,), (1,)), ((), ())), preferred_element_type=F32, **kw)


def bucket_hot(span, shift=0):
    shape = (BUCKETS, 2 * span)
    rel = lax.broadcasted_iota(jnp.int32, shape, 1) - shift
    rel = span - jnp.where(rel < 0, rel + 2 * span, rel)
    dist = jnp.abs(rel)
    half = BUCKETS // 2
    exact = half // 2
    far = jnp.full(shape, exact, jnp.int32)
    for edge in bucket_edges():
        far = far + jnp.where(dist >= edge, 1, 0)
    far = jnp.minimum(far, half - 1)
    bucket = jnp.where(dist < exact, dist, far) + jnp.where(rel > 0, half, 0)
    return bucket == lax.broadcasted_iota(jnp.int32, shape, 0)


def half_at(info, tower, segs, span):
    at, start = 0, 0
    for s in range(segs):
        size = info[2 + tower * segs + s]
        at = jnp.where(size == span // 2, start, at)
        start = start + size
    return at


def rolled_starts(info, tower, segs, span):
    at, start, starts = half_at(info, tower, segs, span), 0, []
    for s in range(segs):
        starts.append(jnp.where(start >= at, start - at, start - at + span))
        start = start + info[2 + tower * segs + s]
    return starts


def seg_bounds(info, segs, spans, shape, axis):
    at = lax.broadcasted_iota(jnp.int32, shape, axis)
    lo = jnp.zeros(shape, jnp.int32)
    hi = jnp.zeros(shape, jnp.int32)
    for tower, span in enumerate(spans):
        starts = rolled_starts(info, tower, segs, span)
        for s in range(segs):
            here = at == tower * segs + s
            start = starts[s] + tower * spans[0]
            lo = jnp.where(here, start, lo)
            hi = jnp.where(here, start + info[2 + tower * segs + s], hi)
    return lo, hi


def seg_of(info, tower, segs, span, shape, axis):
    at = lax.broadcasted_iota(jnp.int32, shape, axis) + span // 2
    seg = jnp.zeros(shape, jnp.int32)
    for start in rolled_starts(info, tower, segs, span):
        seg = seg + jnp.where(at >= start, 1, 0)
    return seg


def rms(v, gain):
    return v * lax.rsqrt(jnp.mean(v * v, axis=-1, keepdims=True) + EPS) * gain


def rms_back(v, gain, dy):
    r = lax.rsqrt(jnp.mean(v * v, axis=-1, keepdims=True) + EPS)
    gdy = gain * dy
    inner = jnp.mean(gdy * v, axis=-1, keepdims=True)
    return r * gdy - v * (r * r * r * inner), jnp.sum(dy * v * r, axis=0, keepdims=True)


def wide_row(gain):
    return gain[...].astype(F32).reshape(1, gain.shape[0])


def front_kernel(
    lp, lq, segs, dk, info, xp, xq, gain, wq, wk, wv, table,
    x, normed, q, k, v, probs_p, probs_q, ctx, rows,
):
    reach = lp // 2

    @pl.when(pl.program_id(0) == 0)
    def _():
        heads = table.shape[0]
        rows[:heads, :] = nn(table[...], bucket_hot(reach).astype(F32).astype(BF16))
        g = wide_row(gain)
        for tower, tokens, off, span in ((0, xp, 0, lp), (1, xq, lp, lq)):
            at = half_at(info, tower, segs, span)
            rolled = pltpu.roll(tokens[...].astype(F32), jnp.where(at == 0, 0, span - at), 0)
            here = slice(off, off + span)
            x[here, :] = rolled.astype(BF16)
            normed[here, :] = rms(rolled, g).astype(BF16)

    weights = jnp.concatenate([wq[...], wk[...], wv[...]], axis=1)
    qkv = nn(normed[...], weights).astype(BF16)
    cut = HS * dk
    q[...] = qkv[:, :cut]
    k[...] = qkv[:, cut : 2 * cut]
    v[...] = qkv[:, 2 * cut :]
    units = []
    for hh in range(HS):
        row = rows[pl.ds(HS * pl.program_id(0) + hh, 1), :]
        bias = pltpu.roll(jnp.broadcast_to(row, (CH, 2 * reach)), 0, 1, stride=1, stride_axis=0)
        cols = slice(hh * dk, (hh + 1) * dk)
        for tower, off, span, probs in ((0, 0, lp, probs_p), (1, lp, lq, probs_q)):
            half = span // 2
            full = jnp.concatenate(
                [bias[:, reach - r0 : reach - r0 + half] for r0 in range(0, half, CH)], axis=0
            )
            for part in range(2):
                here = slice(off + part * half, off + (part + 1) * half)
                units.append((tower, span, cols, here, full, probs, 2 * hh + part))
    scores = []
    for tower, span, cols, here, full, _, at in units:
        s = nt(k[here, cols], q[here, cols]) + full
        if at % 2:
            half = span // 2
            seg_j = seg_of(info, tower, segs, span, (half, 1), 0)
            seg_i = seg_of(info, tower, segs, span, (1, half), 1)
            s = jnp.where(seg_i == seg_j, s, -1000000000.0)
        scores.append(s)
    lows = []
    for (_, _, _, _, _, probs, at), s in zip(units, scores):
        e = jnp.exp(s - jnp.max(s, axis=0, keepdims=True))
        p = e * (1.0 / jnp.sum(e, axis=0, keepdims=True))
        p = p.astype(BF16)
        probs[at] = p
        lows.append(p)
    for (_, _, cols, here, _, _, _), p in zip(units, lows):
        ctx[here, cols] = tn(p, v[here, cols]).astype(BF16)


def ffn_kernel(
    lp, lq, segs, info, ctx, x, w_out, fgain, w_in, w_back, lgain,
    residual, normed_two, hidden, slope, output, pooled,
):
    step = pl.program_id(0)
    total = lp + lq

    @pl.when(step == 0)
    def _():
        g = wide_row(fgain)
        res = x[...].astype(F32) + nn(ctx[...], w_out[...])
        residual[...] = res
        output[...] = res
        normed_two[...] = rms(res, g).astype(BF16)

    part = 256
    parts = [slice(r0, r0 + part) for r0 in range(0, total, part)]

    size = slope.shape[1] // NB
    tile = pl.ds(pl.multiple_of(step * size, size), size)

    def up(here):
        return nn(normed_two[here, :], w_in[:, tile])

    u = up(parts[0])
    for n, here in enumerate(parts):
        following = up(parts[n + 1]) if n + 1 < len(parts) else None
        uu = u * u
        t = jnp.tanh(u * (GELU + (GELU * CUBE) * uu))
        half = 0.5 + 0.5 * t
        h = (u * half).astype(BF16)
        hidden[here, tile] = h
        slope[here, tile] = (
            half + (u * (0.5 - (0.5 * t) * t)) * (GELU + (3.0 * GELU * CUBE) * uu)
        ).astype(BF16)
        output[here, :] += nn(h, w_back[tile, :])
        u = following

    @pl.when(step == pl.num_programs(0) - 1)
    def _():
        final = rms(output[...], wide_row(lgain))
        lo, hi = seg_bounds(info, segs, (lp, lq), (2 * segs, 1), 0)
        at = lax.broadcasted_iota(jnp.int32, (2 * segs, total), 1)
        hot = jnp.where((at >= lo) & (at < hi), 1.0, 0.0).astype(BF16)
        high = final.astype(BF16)
        mean = nn(hot, high) + nn(hot, (final - high.astype(F32)).astype(BF16))
        mean = mean / (hi - lo).astype(F32)
        width = final.shape[1]
        pooled[:, :width] = mean.astype(BF16)
        shape = (2 * segs, pooled.shape[1] - width)
        at_row = lax.broadcasted_iota(jnp.int32, shape, 0)
        at_col = lax.broadcasted_iota(jnp.int32, shape, 1)
        code = jnp.zeros(shape, jnp.int32)
        for s in range(segs):
            pair = info[2 + 2 * segs + s]
            code = jnp.where((at_row == segs + s) & (at_col == 0), pair // 64, code)
            code = jnp.where((at_row == segs + s) & (at_col == 1), pair % 64, code)
        pooled[:, width:] = code.astype(F32).astype(BF16)


def loss_math(segs, block_row, block_col, gathered, w_proj):
    count = gathered.shape[0]
    width = w_proj.shape[0]
    low = gathered[:, :width]
    code = gathered[:, width:].astype(F32)
    pair = code[:, 0:1] * 64.0 + code[:, 1:2]
    row = lax.broadcasted_iota(jnp.int32, (count, 1), 0) % (2 * segs)
    col = lax.broadcasted_iota(jnp.int32, (1, count), 1) % (2 * segs)
    number = (block_col * segs + col).astype(F32)
    is_query = row >= segs
    is_passage = col < segs
    proj = nn(low, w_proj)
    scale = lax.rsqrt(jnp.sum(proj * proj, axis=-1, keepdims=True) + EPS)
    embed = proj * scale
    embed_low = embed.astype(BF16)
    sims = nt(embed_low, embed_low) / SCALE
    masked = jnp.where(is_passage, sims, -1e30)
    top = jnp.max(masked, axis=1, keepdims=True)
    expo = jnp.where(is_passage, jnp.exp(masked - top), 0.0)
    total = jnp.sum(expo, axis=1, keepdims=True)
    hot = jnp.where(is_passage & (number == pair), 1.0, 0.0)
    loss = top + jnp.log(total) - jnp.sum(hot * sims, axis=1, keepdims=True)
    d_sims = jnp.where(is_query, (expo / total - hot) / SCALE, 0.0)
    d_embed = nn(d_sims + d_sims.T, embed_low.astype(F32), precision=HIGHEST)
    d_proj = (d_embed - embed * jnp.sum(embed * d_embed, axis=-1, keepdims=True)) * scale
    return loss, d_proj.astype(BF16)


def loss_kernel(segs, bits, info, near, far, w_proj, loss, d_proj, d_pooled, every):
    gathered = jnp.concatenate([near[...], far[...]], axis=0)
    every[...] = gathered
    count = gathered.shape[0]

    def device(shape, axis):
        place = lax.broadcasted_iota(jnp.int32, shape, axis) // (2 * segs)
        other = jnp.zeros(shape, jnp.int32)
        for at, bit in enumerate(bits):
            other = other + ((place >> at) & 1) * bit
        return other ^ (info[0] * NB + info[1])

    value, d_low = loss_math(
        segs, device((count, 1), 0), device((1, count), 1), gathered, w_proj[...]
    )
    flat = jnp.broadcast_to(value[: 2 * segs], (2 * segs, 128)).T
    loss[...] = flat[:1, segs : 2 * segs].reshape(segs)
    d_proj[...] = d_low
    d_pooled[...] = nt(d_low[: 2 * segs], w_proj[...])


def out_ff_blocks(info, rows, hidden, dst):
    size = 2 * LANES
    at = (pl.program_id(0) ^ (info[0] // 2)) * size
    res = nn(rows, hidden[:, pl.ds(pl.multiple_of(at, size), size)]).astype(BF16)
    cols = res.shape[0] // 2
    for y in range(2):
        for x in range(2):
            dst.at[y, 0][x ^ (info[0] % 2)] = res[
                y * cols : (y + 1) * cols, x * LANES : (x + 1) * LANES
            ]


def out_ff_send_kernel(
    lp, lq, segs, info, d_pooled, output, lgain, hidden,
    d_output, d_ffn, gain_grad, turned, send,
):
    total = lp + lq
    rows = output.shape[1] // NB
    half = 2 * rows

    @pl.when(pl.program_id(0) == 0)
    def _():
        lo, hi = seg_bounds(info, segs, (lp, lq), (1, 2 * segs), 1)
        lo_c, hi_c = seg_bounds(info, segs, (lp, lq), (2 * segs, 1), 0)
        at = lax.broadcasted_iota(jnp.int32, (total, 2 * segs), 0)
        hot = jnp.where((at >= lo) & (at < hi), 1.0, 0.0).astype(BF16)
        each = d_pooled[...] / (hi_c - lo_c).astype(F32)
        high = each.astype(BF16)
        dy = nn(hot, high) + nn(hot, (each - high.astype(F32)).astype(BF16))
        dv, dg = rms_back(output[...], wide_row(lgain), dy)
        d_output[...] = dv
        gain_grad[...] = dg
        low = dv.astype(BF16)
        d_ffn[...] = low
        flipped = low.T
        for n in range(NB):
            other = n ^ info[1]
            at_row = (other % 2) * half + (other // 2) * rows
            turned[pl.ds(pl.multiple_of(at_row, rows), rows), :] = flipped[
                n * rows : (n + 1) * rows
            ]

    out_ff_blocks(info, turned[half:, :], hidden, send)


def out_ff_keep_kernel(info, turned, hidden, keep):
    out_ff_blocks(info, turned[: turned.shape[0] // 2, :], hidden, keep)


def turn_rows(dst, value, wide):
    rows = value.shape[1] // WB
    flipped = value.T
    for w in range(WB):
        dst[pl.ds(pl.multiple_of((w ^ wide) * rows, rows), rows), :] = flipped[
            w * rows : (w + 1) * rows
        ]


def turn_kernel(info, normed_two, ctx, normed, turned_two, turned_ctx, turned):
    turn_rows(turned_two, normed_two[...], info[0])
    turn_rows(turned_ctx, ctx[...], info[0])
    turn_rows(turned, normed[...], info[0])


def join_kernel(info, *refs):
    parts = [r[...].astype(F32) for r in refs[:-1]]
    refs[-1][...] = jnp.concatenate(parts, axis=0).astype(BF16)


def turn(step, narrow):
    return ((step % 2) * 2 + (1 - step // 2)) ^ narrow


def ffn_tile(number, d_ffn, w_back, slope, w_in, turned):
    size = slope.shape[1] // NB
    tile = pl.ds(pl.multiple_of(number * size, size), size)
    d_up = (nt(d_ffn[...], w_back[tile, :]) * slope[:, tile].astype(F32)).astype(BF16)
    res = nn(turned[...], d_up).astype(BF16)
    rows = res.shape[0] // WB
    blocks = jnp.concatenate(
        [
            res[:, half * LANES : (half + 1) * LANES].reshape(WB, rows, LANES)
            for half in range(2)
        ],
        axis=1,
    )
    return nt(d_up, w_in[:, tile]), blocks


def ffn_back_first_kernel(info, d_ffn, w_back, slope, w_in, turned, send, keep, total):
    step = pl.program_id(0)

    @pl.when(step == 0)
    def _():
        total[...] = jnp.zeros_like(total)

    part, blocks = ffn_tile(turn(step, info[1]), d_ffn, w_back, slope, w_in, turned)
    total[...] += part

    @pl.when(step < 2)
    def _():
        send[step] = blocks

    @pl.when(step == 2)
    def _():
        keep[...] = blocks


def ffn_back_last_kernel(
    info, d_ffn, w_back, slope, w_in, turned, so_far, d_output, residual, fgain, turned_ctx, w_out,
    keep, d_resid, gain_grad, d_ctx, send_o, keep_o,
):
    part, blocks = ffn_tile(turn(3, info[1]), d_ffn, w_back, slope, w_in, turned)
    keep[...] = blocks
    width = residual.shape[1]
    rows, cols = width // WB, width // NB
    dv, dg = rms_back(residual[...], wide_row(fgain), so_far[...] + part)
    dr = d_output[...] + dv
    d_resid[...] = dr
    gain_grad[...] = dg
    da = dr.astype(BF16)
    d_ctx[...] = nt(da, w_out[...]).astype(BF16)
    grad = nn(turned_ctx[...], da)
    for n in range(NB):
        part = grad[:, n * cols : (n + 1) * cols].reshape(WB, rows, cols)
        part = jnp.concatenate([part[:, : rows // 2], part[:, rows // 2 :]], axis=2)
        part = part.astype(BF16)
        y = (n // 2) ^ (info[1] // 2)

        @pl.when((n % 2) == (info[1] % 2))
        def _():
            keep_o[y] = part

        @pl.when((n % 2) != (info[1] % 2))
        def _():
            send_o[y] = part


def attn_back_kernel(dk, lp, lq, info, q, k, v, d_ctx, probs_p, probs_q, d_qkv, sums):
    step = pl.program_id(0)
    reach = lp // 2
    size = HS * dk
    out = d_qkv.at[:, :, pl.ds(pl.multiple_of(step * size, size), size)]

    @pl.when(step == 0)
    def _():
        sums[...] = jnp.zeros_like(sums)

    units = []
    for hh in range(HS):
        cols = slice(hh * dk, (hh + 1) * dk)
        for off, span, probs in ((0, lp, probs_p), (lp, lq, probs_q)):
            half = span // 2
            for part in range(2):
                here = slice(off + part * half, off + (part + 1) * half)
                units.append((hh, cols, here, half, probs, 2 * hh + part))
    d_probs = [nt(v[here, cols], d_ctx[here, cols]) for _, cols, here, _, _, _ in units]
    tiles = [[jnp.zeros((CH, CH), F32)] * (2 * reach // CH) for _ in range(HS)]
    lows = []
    for (hh, _, _, half, probs, at), d_prob in zip(units, d_probs):
        p = probs[at].astype(F32)
        t = p * d_prob
        ds = t - p * jnp.sum(t, axis=0, keepdims=True)
        lows.append(ds.astype(BF16))
        for a in range(half // CH):
            for b in range(half // CH):
                to = b + reach // CH - a
                piece = ds[a * CH : (a + 1) * CH, b * CH : (b + 1) * CH]
                tiles[hh][to] = tiles[hh][to] + piece
    for (_, cols, here, _, probs, at), low in zip(units, lows):
        out[0, here, cols] = tn(low, k[here, cols]).astype(BF16)
        out[1, here, cols] = nn(low, q[here, cols]).astype(BF16)
        out[2, here, cols] = nn(probs[at], d_ctx[here, cols]).astype(BF16)
    at_i = lax.broadcasted_iota(jnp.int32, (CH, CH), 0)
    at_j = lax.broadcasted_iota(jnp.int32, (CH, CH), 1)
    mirror = jnp.where(at_i + at_j == CH - 1, 1.0, 0.0).astype(BF16)
    for hh in range(HS):
        flipped = nn(mirror, jnp.concatenate(tiles[hh], axis=1).astype(BF16))
        turn = pltpu.roll(flipped, 0, 1, stride=1, stride_axis=0)
        sums[pl.ds(HS * step + hh, 1), :] = jnp.sum(turn, axis=0, keepdims=True)


def qkv_grad_kernel(
    lp, heads, info, turned, d_qkv, wq, wk, wv, gain, g_ffn, g_final, sums,
    send, keep, column,
):
    width = turned.shape[0]
    rows, cols = width // WB, width // NB
    each = rows + rows // 2
    size = WB * each
    core, y0 = info[1] % 2, info[1] // 2

    def put(n, first, values):
        for dst, mine in ((keep, n % 2 == core), (send, n % 2 != core)):

            @pl.when(mine)
            def _():
                for w in range(WB):
                    at = pl.multiple_of(((n // 2) ^ y0) * size + (w * each + first), 16)
                    dst[pl.ds(at, values.shape[1]), :] = values[w]

    def gradient(grads, weight):
        grad = nn(turned[...], grads)
        for w in range(WB):
            at = pl.ds(pl.multiple_of((w ^ info[0]) * rows, rows), rows)
            part = grad[w * rows : (w + 1) * rows, :] * weight[at, :].astype(F32)
            column[at, :] += jnp.broadcast_to(
                jnp.sum(part, axis=1, keepdims=True), (rows, column.shape[1])
            )
        return grad

    column[...] = jnp.zeros_like(column)
    gq, gk = gradient(d_qkv[0], wq), gradient(d_qkv[1], wk)
    for n in range(NB):
        here = slice(n * cols, (n + 1) * cols)
        both = jnp.concatenate([gq[:, here], gk[:, here]], axis=1).astype(BF16)
        put(n, 0, both.reshape(WB, rows, LANES))
    gv = gradient(d_qkv[2], wv)
    for n in range(NB):
        part = gv[:, n * cols : (n + 1) * cols].reshape(WB, rows, cols)
        part = jnp.concatenate([part[:, : rows // 2], part[:, rows // 2 :]], axis=2)
        put(n, rows, part.astype(BF16))
    g_attn = column[...].T[:1, :] / wide_row(gain)
    hot = bucket_hot(lp // 2, CH - 1).astype(F32)
    bias = nt(sums[...], hot, precision=HIGHEST)
    pieces = []
    for grad in (g_attn, g_ffn[...], g_final[...]):
        pieces += [grad[:, i : i + LANES] for i in range(0, width, LANES)]
    pieces.append(jnp.concatenate([bias[h : h + 1, :] for h in range(heads)], axis=1))
    pieces.append(jnp.zeros((SMALL - len(pieces), LANES), F32))
    small = encode(jnp.concatenate(pieces, axis=0))
    send[2 * size :, :] = small
    keep[2 * size :, :] = small


def input_kernel(segs, info, d_qkv, wq, wk, wv, d_resid, x, gain, grad_p, grad_q):
    off = 0
    for tower, grad in enumerate((grad_p, grad_q)):
        span = grad.shape[0]
        here = slice(off, off + span)
        off += span
        dn = nt(d_qkv[0, here], wq[...]) + nt(d_qkv[1, here], wk[...])
        dn = dn + nt(d_qkv[2, here], wv[...])
        v = x[here, :].astype(F32)
        r = lax.rsqrt(jnp.mean(v * v, axis=-1, keepdims=True) + EPS)
        gdy = wide_row(gain) * dn
        inner = jnp.mean(gdy * v, axis=-1, keepdims=True)
        out = d_resid[here, :] + (r * gdy - v * (r * r * r * inner))
        grad[...] = pltpu.roll(out, half_at(info, tower, segs, span), 0)


def proj_kernel(info, every, d_proj, proj_grad, full):
    rows, cols = proj_grad.shape
    width = full.shape[0]
    full[...] = tn(every[:, :width], d_proj[...])
    mine = full[pl.ds(pl.multiple_of(info[0] * rows, 8), rows), :]
    for n in range(width // cols):

        @pl.when(info[1] == n)
        def _():
            proj_grad[...] = mine[:, n * cols : (n + 1) * cols]


class Info:
    def __init__(self, place, passages, queries, pairs):
        segs = passages.shape[1]
        self.at = [lambda: place[0], lambda: place[1]]
        self.at += [functools.partial(lambda r, i: r[0, i], passages, i) for i in range(segs)]
        self.at += [functools.partial(lambda r, i: r[0, i], queries, i) for i in range(segs)]
        self.at += [functools.partial(lambda r, i: r[i], pairs, i) for i in range(segs)]

    def __getitem__(self, i):
        return self.at[i]()


def call(
    kernel, grid, info, args, in_specs, outs, out_specs, scratch=(), flops=0, moved=0,
    vmem=16, after=(), through=(), through_specs=(),
):
    count, more = len(args), len(after) + len(through)
    outs, out_specs = list(outs), list(out_specs)
    made = len(outs)
    aliases = {len(info) + count + len(after) + i: made + i for i in range(len(through))}
    outs += [(hbm_out if through_specs else shaped)(a.shape, a.dtype) for a in through]
    out_specs += through_specs or [pl.BlockSpec(memory_space=pl.ANY)] * len(through)
    hidden = 0 if through_specs else len(through)

    def body(*refs):
        scalars, refs = refs[: len(info)], refs[len(info) :]
        results = refs[count + more :]
        kernel(
            Info(*scalars) if scalars else None,
            *refs[:count],
            *results[:made],
            *results[made + hidden :],
        )

    return pl.pallas_call(
        body,
        grid_spec=pltpu.PrefetchScalarGridSpec(
            num_scalar_prefetch=len(info),
            grid=grid,
            in_specs=list(in_specs) + [pl.BlockSpec(memory_space=pl.ANY)] * more,
            out_specs=out_specs,
            scratch_shapes=list(scratch),
        ),
        out_shape=outs,
        input_output_aliases=aliases,
        compiler_params=pltpu.CompilerParams(vmem_limit_bytes=vmem * 2**20),
        cost_estimate=pl.CostEstimate(flops=flops, bytes_accessed=moved, transcendentals=0),
    )(*info, *args, *after, *through)


def hbm(array):
    return pltpu.with_memory_space_constraint(array, pltpu.HBM)


def near(*shape):
    return pl.BlockSpec(memory_space=pltpu.VMEM)


def whole(*shape):
    return pl.BlockSpec(shape, lambda *_: (0,) * len(shape), pipeline_mode=pl.Buffered(1))


def hbm_out(shape, dtype):
    return pltpu.HBM(shape, dtype)


def out_shape_of(out):
    return out.inner_aval.shape


def shaped(shape, dtype):
    return jax.ShapeDtypeStruct(shape, dtype)


def permute(array, bit, count):
    return lax.ppermute(array, AXES, [(i, i ^ bit) for i in range(count)])


CORE, Y, X, Z0, Z1 = 1, 2, 4, 8, 16
GATHER = (Z0, Z1, Y, X, CORE)


def own_sum(base, refs):
    parts = [r[b:, :].astype(F32) for b, r in zip(base, refs)]
    while len(parts) > 1:
        parts = [a + b for a, b in zip(parts[::2], parts[1::2])]
    return parts[0]


def out_ff_finish_kernel(base, info, *refs):
    refs[-1][...] = own_sum(base, refs[:-1])


def in_ff_finish_kernel(base, info, *refs):
    *parts, in_ff, out_w = refs
    total = own_sum(base, parts)
    rows, cols = out_w.shape
    in_ff[...] = jnp.concatenate([total[:rows], total[rows : 2 * rows]], axis=1)
    out_w[...] = jnp.concatenate([total[2 * rows :, :cols], total[2 * rows :, cols:]], axis=0)


def split_small(small, width, heads):
    per = width // LANES
    gains = [
        jnp.concatenate([small[g * per + i : g * per + i + 1] for i in range(per)], axis=1)
        for g in range(3)
    ]
    row = small[3 * per : 3 * per + 1]
    bias = [row[:, h * BUCKETS : (h + 1) * BUCKETS] for h in range(heads)]
    return gains, jnp.concatenate(bias, axis=0)


def qkv_finish_kernel(heads, base, info, *refs):
    rest, own, *got, query_w, key_w, value_w, gain_a, gain_f, gain_l, bias = refs
    total = own_sum(base, (rest, *got))
    rows, cols = query_w.shape
    query_w[...] = total[:rows, :cols]
    key_w[...] = total[:rows, cols:]
    value_w[...] = jnp.concatenate([total[rows:, :cols], total[rows:, cols:]], axis=0)
    small = [decode(r[: 2 * SMALL, :]) for r in (own, *got)]
    small = (small[0] + small[1]) + (small[2] + small[3])
    gains, table = split_small(small, gain_a.shape[0], heads)
    for ref, gain in zip((gain_a, gain_f, gain_l), gains):
        ref[...] = gain.reshape(gain.shape[1])
    bias[...] = table


def encode(values):
    high = values.astype(BF16).astype(F32)
    return jnp.concatenate([high, values - high], axis=0).astype(BF16)


def decode(coded):
    half = coded.shape[0] // 2
    return coded[:half].astype(F32) + coded[half:].astype(F32)


class Part:
    def __init__(self, arrays, base, dims, rows, lo=0, hi=None):
        self.arrays, self.base, self.dims, self.rows = arrays, base, dims, rows
        self.lo, self.hi = lo, rows if hi is None else hi

    def at(self, where):
        dims, which = self.dims, 0
        if len(self.arrays) > 1:
            which, dims = where[dims[0]], dims[1:]
        index = 0
        for bit in dims:
            index = index * 2 + where[bit]
        return self.arrays[which], self.base + index * self.rows + self.lo


def add_kernel(plans, info, *refs):
    outs = refs[len(refs) - len(plans) :]
    for (sums, small), out in zip(plans, outs):
        if small:
            total = decode(refs[small[0]][small[1] : small[1] + 2 * SMALL, :])
            total = total + decode(refs[small[2]][small[3] : small[3] + 2 * SMALL, :])
            out[: 2 * SMALL, :] = encode(total)
        for to, a, at_a, b, at_b, rows in sums:
            value = refs[a][at_a : at_a + rows, :]
            out[to : to + rows, :] = value if b is None else value + refs[b][at_b : at_b + rows, :]


class Scatter:
    def __init__(self, groups, count, quad=False, z=(Z0, Z1)):
        self.count, self.groups, self.quad, self.z = count, groups, quad, z
        self.sources = []
        self.small = None
        self.stage = -1

    def source(self, send, keeps, rows, small=False):
        send = send.reshape(-1, LANES)
        keeps = [k.reshape(-1, LANES) for k in keeps]
        got = permute(send, CORE, self.count)
        self.sources.append((keeps, got, rows))
        if small:
            at = 16 * rows
            self.small = (keeps[0], at, got, at)

    def jobs(self):
        self.stage += 1
        stage = self.stage
        if stage == 0:
            dims = (Y, Z1, Z0, X)
            groups = [
                [
                    (
                        Part(self.sources[n][0], 0, dims, self.sources[n][2], lo, hi),
                        Part([self.sources[n][1]], 0, dims, self.sources[n][2], lo, hi),
                    )
                    for n, lo, hi in group
                ]
                for group in self.groups
            ]
        else:
            groups = [[pair] for pair in zip(self.rest, self.got)]
        if stage < 2:
            bits = ((Y, X), (X, Y))[stage]
            first = [(g, {b: 1}) for g, b in zip(groups, bits)]
            rest = [(g, {b: 0}) for g, b in zip(groups, bits)]
            self.bits = bits
        else:
            merged = [pair for group in groups for pair in group]
            if self.quad:
                self.bits = (Z0, Z1, Z0 | Z1)
                first = [(merged, {Z0: a, Z1: b}) for a, b in ((1, 0), (0, 1), (1, 1))]
                rest = [(merged, {Z0: 0, Z1: 0})]
            else:
                bit = self.z[stage - 2]
                self.bits = (bit,)
                first, rest = [(merged, {bit: 1})], [(merged, {bit: 0})]
        carry = [self.small is not None and (stage >= 2 or i == 1) for i in range(len(first))]
        return first, rest, carry

    def take(self, first, rest, hold=False):
        self.first, self.rest, self.got = first, rest, []
        if hold:
            return
        for part, bit in zip(first, self.bits):
            got = permute(part.arrays[0], bit, self.count)
            self.got.append(Part([got], part.base, part.dims, part.rows))
        if self.small is not None:
            at = 0 if self.stage >= 2 else 1
            self.small = (first[at].arrays[0], 0, self.got[at].arrays[0], 0)

    def finish(self):
        parts = [self.rest[0], *self.got]
        return [p.arrays[0] for p in parts], tuple(p.base for p in parts)


def advance(info, scatters, after=(), through=(), hold=None, join=None):
    inputs, plans, shapes, slots = [], [], [], []

    def find(array):
        for i, known in enumerate(inputs):
            if known is array:
                return i
        inputs.append(array)
        return len(inputs) - 1

    for scatter in scatters:
        first, rest, carry = scatter.jobs()
        for n, (pairs, fixed) in enumerate(first + rest):
            dims = tuple(d for d in pairs[0][0].dims if d not in fixed)
            rows = sum(a.hi - a.lo for a, _ in pairs)
            base, small = 0, ()
            if n < len(first) and carry[n]:
                own, at_own, got, at_got = scatter.small
                base, small = 2 * SMALL, (find(own), at_own, find(got), at_got)
            sums = []
            for index in range(2 ** len(dims)):
                where = dict(fixed)
                for i, d in enumerate(reversed(dims)):
                    where[d] = (index >> i) & 1
                to = base + index * rows
                for a, b in pairs:
                    (array_a, row_a), (array_b, row_b) = a.at(where), b.at(where)
                    size = a.hi - a.lo
                    sums.append((to, find(array_a), row_a, find(array_b), row_b, size))
                    to += size
            end = base + 2 ** len(dims) * rows
            if join is not None and scatter is join[0] and n == 0:
                (held,) = join[1].first
                sums.append((end, find(held.arrays[0]), held.base, None, 0, held.rows))
                joined = (end, held)
                end += held.rows
            plans.append((sums, small))
            shapes.append(shaped((end, LANES), BF16))
            slots.append((base, dims, rows))
        scatter.counts = (len(first), len(rest))
    outs = call(
        functools.partial(add_kernel, plans), (1,), info, inputs, [near()] * len(inputs), shapes,
        [near()] * len(shapes), flops=10**6, moved=2**20, vmem=4, after=after, through=through,
    )
    handed = outs[len(slots) :]
    parts = [Part([out], *slot) for out, slot in zip(outs, slots)]
    sent = []
    for scatter in scatters:
        many, more = scatter.counts
        scatter.take(parts[:many], parts[many : many + more], scatter is hold)
        sent += [p.arrays[0] for p in parts[:many]]
        if join is not None and scatter is join[0]:
            at, held = joined
            join[1].got = [Part(scatter.got[0].arrays, at, held.dims, held.rows)]
        parts = parts[many + more :]
    return sent, handed


def per_device(
    fast, n_wide, n_narrow,
    xp, xq, passage_lengths, query_lengths, pair_index, g_attn, w_query, w_key, w_value, w_out,
    bias_table, g_ffn, w_in, w_back, g_final, w_proj,
):
    lp, width = xp.shape
    lq = xq.shape[0]
    total = lp + lq
    heads = bias_table.shape[1]
    dk = width // heads
    ff = w_in.shape[1]
    segs = passage_lengths.shape[1]
    count = n_wide * n_narrow
    steps = heads // HS
    rows, cols = width // WB, width // NB
    wide_at, narrow_at = lax.axis_index("wide"), lax.axis_index("narrow")
    place = jnp.stack([wide_at, narrow_at]) if fast else jnp.zeros((2,), jnp.int32)
    info = (place.astype(jnp.int32), hbm(passage_lengths), hbm(query_lengths), hbm(pair_index))
    mm = 2 * total * width * width
    act, act32 = shaped((total, width), BF16), shaped((total, width), F32)
    act_hbm = pltpu.HBM((total, width), BF16)

    head_tile = pl.BlockSpec((total, HS * dk), lambda i, *_: (0, i))
    col_tile = pl.BlockSpec((width, HS * dk), lambda i, *_: (0, i))
    prob_tiles = [pl.BlockSpec((2 * HS, n // 2, n // 2), lambda i, *_: (i, 0, 0)) for n in (lp, lq)]
    x, normed, q, k, v, probs_p, probs_q, ctx = call(
        functools.partial(front_kernel, lp, lq, segs, dk),
        (steps,),
        info,
        (*(hbm(a) for a in (xp, xq, g_attn, w_query, w_key, w_value)), hbm(bias_table.T)),
        [whole(lp, width), whole(lq, width), whole(width)] + [col_tile] * 3
        + [whole(heads, BUCKETS)],
        [act, act_hbm, act_hbm, act_hbm, act_hbm]
        + [pltpu.HBM((2 * heads, n // 2, n // 2), BF16) for n in (lp, lq)]
        + [act],
        [near(), whole(total, width), head_tile, head_tile, head_tile, *prob_tiles, head_tile],
        [pltpu.VMEM((16, lp), F32)],
        flops=12 * 10**9,
        moved=13 * 2**20,
    )

    ff_tile = ff // NB
    ff_spec = pl.BlockSpec((total, ff_tile), lambda i, *_: (0, i))
    message = width + 128
    residual, normed_two, hidden, slope, output, pooled = call(
        functools.partial(ffn_kernel, lp, lq, segs),
        (NB,),
        info,
        (ctx, x, w_out, g_ffn, w_in, w_back, g_final),
        [near()] * 7,
        [
            act32, act, shaped((total, ff), BF16), shaped((total, ff), BF16), act32,
            shaped((2 * segs, message), BF16),
        ],
        [near()] * 6,
        flops=9 * mm,
        moved=30 * 2**20,
        vmem=24,
    )

    turned_two, turned_ctx, turned = call(
        turn_kernel,
        (1,),
        info,
        (normed_two, ctx, normed),
        [near()] * 3,
        [shaped((width, total), BF16)] + [pltpu.HBM((width, total), BF16)] * 2,
        [near(), whole(width, total), whole(width, total)],
        flops=10**6,
        moved=2**20,
        vmem=8,
        after=[pooled],
    )
    if fast:
        parts = [pooled] + [permute(pooled, b, count) for b in (Z0, Z1, Z0 | Z1)]
        (one,) = call(
            join_kernel, (1,), info, parts, [near()] * 4,
            [shaped((4 * 2 * segs, message), BF16)], [near()], flops=10**6, moved=2**20, vmem=4,
            after=[turned_two],
        )
        two = jnp.concatenate([one] + [permute(one, b, count) for b in (Y, X, Y | X)], axis=0)
        every = 2 * two.shape[0]
        query_loss, d_proj, d_pooled, gathered = call(
            functools.partial(loss_kernel, segs, GATHER),
            (1,),
            info,
            (two, permute(two, CORE, count), w_proj),
            [near(), near(), near()],
            [
                hbm_out((segs,), F32), shaped((every, width), BF16),
                shaped((2 * segs, width), F32), shaped((every, message), BF16),
            ],
            [whole(segs), near(), near(), near()],
            flops=10**9,
            moved=2**20,
        )
    else:
        gathered = lax.all_gather(pooled, AXES, axis=0, tiled=True)
        every = gathered.shape[0]
        block = jnp.arange(every, dtype=jnp.int32) // (2 * segs)
        loss, d_proj = loss_math(segs, block[:, None], block[None, :], gathered, w_proj)
        mine = (wide_at * n_narrow + narrow_at) * 2 * segs
        query_loss = lax.dynamic_slice_in_dim(loss, mine + segs, segs, 0)[:, 0]
        d_pooled = nt(lax.dynamic_slice_in_dim(d_proj, mine, 2 * segs, 0), w_proj)

    part1 = (2, WB // 2, 2, cols, LANES)
    block1 = pl.BlockSpec((2, 1, 2, cols, LANES), lambda i, *_: (0, i, 0, 0, 0))
    d_output, d_ffn, final_gain_grad, turned_ff, send1 = call(
        functools.partial(out_ff_send_kernel, lp, lq, segs),
        (WB // 2,),
        info,
        (d_pooled, output, g_final, hidden),
        [near(), near(), near(), near()],
        [act32, act, shaped((1, width), F32), shaped((width, total), BF16), shaped(part1, BF16)],
        [near(), near(), near(), near(), block1],
        flops=3 * mm,
        moved=10 * 2**20,
        vmem=12,
    )
    (keep1,) = call(
        out_ff_keep_kernel,
        (WB // 2,),
        info,
        (turned_ff, hidden),
        [near(), near()],
        [shaped(part1, BF16)],
        [block1],
        flops=2 * mm,
        moved=8 * 2**20,
        vmem=6,
    )

    after = []
    if fast:
        sc1 = Scatter((((0, 0, cols // 2),), ((0, cols // 2, cols),)), count, z=(Z1, Z0))
        sc1.source(send1, [keep1], cols)
        after, _ = advance(info, [sc1])

    size2, size_o = 2 * rows, rows // 2
    part2 = shaped((2, WB, size2, LANES), BF16)
    part_o = shaped((2, WB, size_o, LANES), BF16)

    def tiles_at(first):
        return [
            near(),
            near(),
            near(),
            near(),
        ]

    half2 = shaped((WB, size2, LANES), BF16)
    send2, keep2a, so_far = call(
        ffn_back_first_kernel,
        (3,),
        info,
        (d_ffn, w_back, slope, w_in, turned_two),
        tiles_at(0) + [near()],
        [part2, half2, act32],
        [near()] * 3,
        flops=9 * mm,
        moved=16 * 2**20,
        vmem=16,
        after=after,
    )
    after = []
    if fast:
        after, (send2,) = advance(info, [sc1], [so_far], [send2])
    keep2b, d_resid, ffn_gain_grad, d_ctx, send_o, keep_o = call(
        ffn_back_last_kernel,
        (1,),
        info,
        (
            d_ffn, w_back, slope, w_in, turned_two, so_far, d_output, residual, g_ffn,
            turned_ctx, w_out,
        ),
        tiles_at(3) + [near()] * 7,
        [half2, act32, shaped((1, width), F32), act, part_o, part_o],
        [near()] * 6,
        flops=5 * mm,
        moved=20 * 2**20,
        vmem=18,
        after=after,
    )

    after = []
    if fast:
        sc2 = Scatter((((0, 0, 128),), ((0, 128, size2), (1, 0, size_o))), count)
        sc2.source(send2, [keep2a, keep2b], size2)
        after, (send_o,) = advance(info, [sc1], [d_ctx], [send_o])
        sc2.source(send_o, [keep_o], size_o)
        more, _ = advance(info, [sc2], after)
        after = after + more
    d_qkv, sums = call(
        functools.partial(attn_back_kernel, dk, lp, lq),
        (steps,),
        info,
        (hbm(q), hbm(k), hbm(v), d_ctx, hbm(probs_p), hbm(probs_q)),
        [head_tile] * 4 + prob_tiles,
        [shaped((3, total, width), BF16), shaped((16, lp), F32)],
        [near(), near()],
        flops=8 * 10**9,
        moved=16 * 2**20,
        after=after,
    )

    size3 = rows + rows // 2
    flat3 = shaped((16 * size3 + 16, LANES), BF16)
    send3, keep3 = call(
        functools.partial(qkv_grad_kernel, lp, heads),
        (1,),
        info,
        (
            turned, d_qkv, w_query, w_key, w_value, g_attn, ffn_gain_grad,
            final_gain_grad, sums,
        ),
        [near()] * 9,
        [flat3, flat3],
        [near(), near()],
        [
            pltpu.VMEM((width, 128), F32),
        ],
        flops=3 * mm,
        moved=9 * 2**20,
        vmem=24,
        after=after,
    )

    after = []
    own_rows, own_cols = width // WB, width // NB
    square = hbm_out((own_rows, own_cols), F32)
    if fast:

        def finish(kernel, scatter, outs, after, more=()):
            parts, base = scatter.finish()
            parts = parts[:1] + list(more) + parts[1:]
            return call(
                functools.partial(kernel, base), (1,), info, parts, [near()] * len(parts), outs,
                [whole(*out_shape_of(out)) for out in outs], flops=10**6, moved=2**20, after=after,
            )

        sc3 = Scatter((((0, 0, 80),), ((0, 80, size3),)), count, quad=True)
        after, (send3,) = advance(info, [sc1, sc2], [keep3], [send3], hold=sc1)
        sc3.source(send3, [keep3], size3, small=True)

    grad_p, grad_q = call(
        functools.partial(input_kernel, segs),
        (1,),
        info,
        (d_qkv, w_query, w_key, w_value, d_resid, x, g_attn),
        [near()] * 7,
        [hbm_out((lp, width), F32), hbm_out((lq, width), F32)],
        [whole(lp, width), whole(lq, width)],
        flops=3 * mm,
        moved=6 * 2**20,
        vmem=20,
        after=after,
    )
    after = [hbm(grad_p)]
    if fast:
        after, _ = advance(info, [sc3, sc2], after, join=(sc2, sc1))
    (proj_grad,) = call(
        proj_kernel,
        (1,),
        info,
        (gathered[:256], d_proj[:256]),
        [near(), near()],
        [square],
        [whole(own_rows, own_cols)],
        [pltpu.VMEM((width, width), F32)],
        flops=mm,
        moved=2**20,
        vmem=20,
        after=after,
    )

    if fast:
        after, _ = advance(info, [sc3, sc2], [hbm(proj_grad)])
        (out_ff,) = finish(out_ff_finish_kernel, sc1, [hbm_out((cols, ff // WB), F32)], after)
        after, _ = advance(info, [sc3], [hbm(out_ff)])
        out_ff = out_ff.T
        in_ff, out_w = finish(
            in_ff_finish_kernel, sc2, [hbm_out((rows, ff // NB), F32), square], after
        )
        query_w, key_w, value_w, gain_a, gain_f, gain_l, bias = finish(
            functools.partial(qkv_finish_kernel, heads), sc3,
            [square] * 3 + [hbm_out((width,), F32)] * 3 + [hbm_out((heads, BUCKETS), F32)],
            [hbm(out_w)], [sc3.first[0].arrays[0]],
        )
    else:
        own_rows, own_cols = width // n_wide, width // n_narrow
        left = lax.dynamic_slice(gathered, (0, wide_at * own_rows), (every, own_rows))
        right = lax.dynamic_slice(d_proj, (0, narrow_at * own_cols), (every, own_cols))
        proj_grad = tn(left, right)

        def blocks(send, keep):
            both = jnp.stack([keep, send], axis=1).astype(F32)
            return both.reshape((NB, WB) + both.shape[-2:])

        def spread(matrix):
            matrix = lax.psum_scatter(matrix, "wide", scatter_dimension=0, tiled=True)
            return lax.psum_scatter(matrix, "narrow", scatter_dimension=1, tiled=True)

        def side(part):
            half = part.shape[2] // 2
            return jnp.concatenate([part[:, :, :half], part[:, :, half:]], axis=3)

        def stack(part):
            half = part.shape[3] // 2
            return jnp.concatenate([part[..., :half], part[..., half:]], axis=2)

        def matrix(part):
            return part.transpose(1, 2, 0, 3).reshape(WB * part.shape[2], NB * part.shape[3])

        b1 = blocks(send1.reshape(2, WB, cols, LANES), keep1.reshape(2, WB, cols, LANES))
        b2 = blocks(send2, jnp.stack([keep2a, keep2b]))
        coded = keep3[16 * size3 :]
        b3 = blocks(*(a[: 16 * size3].reshape(2, WB, size3, LANES) for a in (send3, keep3)))
        out_ff = spread(matrix(b1.transpose(0, 1, 3, 2)))
        in_ff = spread(matrix(side(b2)))
        out_w = spread(matrix(stack(blocks(send_o, keep_o))))
        query_w = spread(matrix(b3[:, :, :rows, :cols]))
        key_w = spread(matrix(b3[:, :, :rows, cols:]))
        value_w = spread(matrix(stack(b3[:, :, rows:])))
        gains, bias = split_small(lax.psum(decode(coded), AXES), width, heads)
        gain_a, gain_f, gain_l = (gain[0] for gain in gains)
    return (
        query_loss, grad_p, grad_q, gain_a, query_w, key_w, value_w, out_w, bias.T, gain_f,
        in_ff, out_ff, gain_l, proj_grad,
    )


def solution(mesh):
    n_wide, n_narrow = mesh.shape["wide"], mesh.shape["narrow"]
    fast = (n_wide, n_narrow) == (WB, NB)
    rows = P(AXES, None)
    owned = P("wide", "narrow")
    return jax.shard_map(
        functools.partial(per_device, fast, n_wide, n_narrow),
        mesh=mesh,
        in_specs=(rows, rows, rows, rows, P(AXES)) + (P(),) * 11,
        out_specs=(
            P(AXES), rows, rows, P(), owned, owned, owned, owned, P(), P(),
            owned, owned, P(), owned,
        ),
        check_vma=False,
    )
```

```python
import functools

import jax
import jax.numpy as jnp
from jax import lax
from jax.experimental import pallas as pl
from jax.experimental.pallas import tpu as pltpu
from jax.sharding import PartitionSpec as P

BUCKETS = 32
MAX_DIST = 128
SCALE = 0.02
EPS = 1e-06
GELU = 0.7978845608028654
CUBE = 0.044715
HIGHEST = lax.Precision.HIGHEST
F32 = jnp.float32
BF16 = jnp.bfloat16
AXES = ("wide", "narrow")
NB = 4
WB = 8
CH = 128
LANES = 384
HS = 4
SMALL = 8


def bucket_edges():
    half = BUCKETS // 2
    exact = half // 2
    levels = half - exact
    ratio = MAX_DIST // exact
    edges = []
    for step in range(1, levels):
        target = exact**levels * ratio**step
        candidate = exact
        while candidate**levels < target:
            candidate += 1
        edges.append(candidate)
    return edges


def nn(a, b, **kw):
    return lax.dot_general(a, b, (((1,), (0,)), ((), ())), preferred_element_type=F32, **kw)


def tn(a, b):
    return lax.dot_general(a, b, (((0,), (0,)), ((), ())), preferred_element_type=F32)


def nt(a, b, **kw):
    return lax.dot_general(a, b, (((1,), (1,)), ((), ())), preferred_element_type=F32, **kw)


def bucket_hot(span, shift=0):
    shape = (BUCKETS, 2 * span)
    rel = lax.broadcasted_iota(jnp.int32, shape, 1) - shift
    rel = span - jnp.where(rel < 0, rel + 2 * span, rel)
    dist = jnp.abs(rel)
    half = BUCKETS // 2
    exact = half // 2
    far = jnp.full(shape, exact, jnp.int32)
    for edge in bucket_edges():
        far = far + jnp.where(dist >= edge, 1, 0)
    far = jnp.minimum(far, half - 1)
    bucket = jnp.where(dist < exact, dist, far) + jnp.where(rel > 0, half, 0)
    return bucket == lax.broadcasted_iota(jnp.int32, shape, 0)


def half_at(info, tower, segs, span):
    at, start = 0, 0
    for s in range(segs):
        size = info[2 + tower * segs + s]
        at = jnp.where(size == span // 2, start, at)
        start = start + size
    return at


def rolled_starts(info, tower, segs, span):
    at, start, starts = half_at(info, tower, segs, span), 0, []
    for s in range(segs):
        starts.append(jnp.where(start >= at, start - at, start - at + span))
        start = start + info[2 + tower * segs + s]
    return starts


def seg_bounds(info, segs, spans, shape, axis):
    at = lax.broadcasted_iota(jnp.int32, shape, axis)
    lo = jnp.zeros(shape, jnp.int32)
    hi = jnp.zeros(shape, jnp.int32)
    for tower, span in enumerate(spans):
        starts = rolled_starts(info, tower, segs, span)
        for s in range(segs):
            here = at == tower * segs + s
            start = starts[s] + tower * spans[0]
            lo = jnp.where(here, start, lo)
            hi = jnp.where(here, start + info[2 + tower * segs + s], hi)
    return lo, hi


def seg_of(info, tower, segs, span, shape, axis):
    at = lax.broadcasted_iota(jnp.int32, shape, axis) + span // 2
    seg = jnp.zeros(shape, jnp.int32)
    for start in rolled_starts(info, tower, segs, span):
        seg = seg + jnp.where(at >= start, 1, 0)
    return seg


def rms(v, gain):
    return v * lax.rsqrt(jnp.mean(v * v, axis=-1, keepdims=True) + EPS) * gain


def rms_back(v, gain, dy):
    r = lax.rsqrt(jnp.mean(v * v, axis=-1, keepdims=True) + EPS)
    gdy = gain * dy
    inner = jnp.mean(gdy * v, axis=-1, keepdims=True)
    return r * gdy - v * (r * r * r * inner), jnp.sum(dy * v * r, axis=0, keepdims=True)


def wide_row(gain):
    return gain[...].astype(F32).reshape(1, gain.shape[0])


def front_kernel(
    lp, lq, segs, dk, info, xp, xq, gain, wq, wk, wv, table,
    x, normed, q, k, v, probs_p, probs_q, ctx, rows,
):
    reach = lp // 2

    @pl.when(pl.program_id(0) == 0)
    def _():
        heads = table.shape[0]
        rows[:heads, :] = nn(table[...], bucket_hot(reach).astype(F32).astype(BF16))
        g = wide_row(gain)
        for tower, tokens, off, span in ((0, xp, 0, lp), (1, xq, lp, lq)):
            at = half_at(info, tower, segs, span)
            rolled = pltpu.roll(tokens[...].astype(F32), jnp.where(at == 0, 0, span - at), 0)
            here = slice(off, off + span)
            x[here, :] = rolled.astype(BF16)
            normed[here, :] = rms(rolled, g).astype(BF16)

    weights = jnp.concatenate([wq[...], wk[...], wv[...]], axis=1)
    qkv = nn(normed[...], weights).astype(BF16)
    cut = HS * dk
    q[...] = qkv[:, :cut]
    k[...] = qkv[:, cut : 2 * cut]
    v[...] = qkv[:, 2 * cut :]
    units = []
    for hh in range(HS):
        row = rows[pl.ds(HS * pl.program_id(0) + hh, 1), :]
        bias = pltpu.roll(jnp.broadcast_to(row, (CH, 2 * reach)), 0, 1, stride=1, stride_axis=0)
        cols = slice(hh * dk, (hh + 1) * dk)
        for tower, off, span, probs in ((0, 0, lp, probs_p), (1, lp, lq, probs_q)):
            half = span // 2
            full = jnp.concatenate(
                [bias[:, reach - r0 : reach - r0 + half] for r0 in range(0, half, CH)], axis=0
            )
            for part in range(2):
                here = slice(off + part * half, off + (part + 1) * half)
                units.append((tower, span, cols, here, full, probs, 2 * hh + part))
    scores = []
    for tower, span, cols, here, full, _, at in units:
        s = nt(k[here, cols], q[here, cols]) + full
        if at % 2:
            half = span // 2
            seg_j = seg_of(info, tower, segs, span, (half, 1), 0)
            seg_i = seg_of(info, tower, segs, span, (1, half), 1)
            s = jnp.where(seg_i == seg_j, s, -1000000000.0)
        scores.append(s)
    lows = []
    for (_, _, _, _, _, probs, at), s in zip(units, scores):
        e = jnp.exp(s - jnp.max(s, axis=0, keepdims=True))
        p = e * (1.0 / jnp.sum(e, axis=0, keepdims=True))
        p = p.astype(BF16)
        probs[at] = p
        lows.append(p)
    for (_, _, cols, here, _, _, _), p in zip(units, lows):
        ctx[here, cols] = tn(p, v[here, cols]).astype(BF16)


def ffn_kernel(
    lp, lq, segs, info, ctx, x, w_out, fgain, w_in, w_back, lgain,
    residual, normed_two, hidden, slope, output, pooled,
):
    step = pl.program_id(0)
    total = lp + lq

    @pl.when(step == 0)
    def _():
        g = wide_row(fgain)
        res = x[...].astype(F32) + nn(ctx[...], w_out[...])
        residual[...] = res
        output[...] = res
        normed_two[...] = rms(res, g).astype(BF16)

    part = 256
    parts = [slice(r0, r0 + part) for r0 in range(0, total, part)]

    size = slope.shape[1] // NB
    tile = pl.ds(pl.multiple_of(step * size, size), size)

    def up(here):
        return nn(normed_two[here, :], w_in[:, tile])

    u = up(parts[0])
    for n, here in enumerate(parts):
        following = up(parts[n + 1]) if n + 1 < len(parts) else None
        uu = u * u
        t = jnp.tanh(u * (GELU + (GELU * CUBE) * uu))
        half = 0.5 + 0.5 * t
        h = (u * half).astype(BF16)
        hidden[here, tile] = h
        slope[here, tile] = (
            half + (u * (0.5 - (0.5 * t) * t)) * (GELU + (3.0 * GELU * CUBE) * uu)
        ).astype(BF16)
        output[here, :] += nn(h, w_back[tile, :])
        u = following

    @pl.when(step == pl.num_programs(0) - 1)
    def _():
        final = rms(output[...], wide_row(lgain))
        lo, hi = seg_bounds(info, segs, (lp, lq), (2 * segs, 1), 0)
        at = lax.broadcasted_iota(jnp.int32, (2 * segs, total), 1)
        hot = jnp.where((at >= lo) & (at < hi), 1.0, 0.0).astype(BF16)
        high = final.astype(BF16)
        mean = nn(hot, high) + nn(hot, (final - high.astype(F32)).astype(BF16))
        mean = mean / (hi - lo).astype(F32)
        width = final.shape[1]
        pooled[:, :width] = mean.astype(BF16)
        shape = (2 * segs, pooled.shape[1] - width)
        at_row = lax.broadcasted_iota(jnp.int32, shape, 0)
        at_col = lax.broadcasted_iota(jnp.int32, shape, 1)
        code = jnp.zeros(shape, jnp.int32)
        for s in range(segs):
            pair = info[2 + 2 * segs + s]
            code = jnp.where((at_row == segs + s) & (at_col == 0), pair // 64, code)
            code = jnp.where((at_row == segs + s) & (at_col == 1), pair % 64, code)
        pooled[:, width:] = code.astype(F32).astype(BF16)


def loss_math(segs, block_row, block_col, gathered, w_proj):
    count = gathered.shape[0]
    width = w_proj.shape[0]
    low = gathered[:, :width]
    code = gathered[:, width:].astype(F32)
    pair = code[:, 0:1] * 64.0 + code[:, 1:2]
    row = lax.broadcasted_iota(jnp.int32, (count, 1), 0) % (2 * segs)
    col = lax.broadcasted_iota(jnp.int32, (1, count), 1) % (2 * segs)
    number = (block_col * segs + col).astype(F32)
    is_query = row >= segs
    is_passage = col < segs
    proj = nn(low, w_proj)
    scale = lax.rsqrt(jnp.sum(proj * proj, axis=-1, keepdims=True) + EPS)
    embed = proj * scale
    embed_low = embed.astype(BF16)
    sims = nt(embed_low, embed_low) / SCALE
    masked = jnp.where(is_passage, sims, -1e30)
    top = jnp.max(masked, axis=1, keepdims=True)
    expo = jnp.where(is_passage, jnp.exp(masked - top), 0.0)
    total = jnp.sum(expo, axis=1, keepdims=True)
    hot = jnp.where(is_passage & (number == pair), 1.0, 0.0)
    loss = top + jnp.log(total) - jnp.sum(hot * sims, axis=1, keepdims=True)
    d_sims = jnp.where(is_query, (expo / total - hot) / SCALE, 0.0)
    both = d_sims + d_sims.T
    high = both.astype(BF16)
    rest = (both - high.astype(F32)).astype(BF16)
    d_embed = nn(high, embed_low) + nn(rest, embed_low)
    d_proj = (d_embed - embed * jnp.sum(embed * d_embed, axis=-1, keepdims=True)) * scale
    return loss, d_proj.astype(BF16)


def loss_kernel(segs, bits, info, near, far, w_proj, loss, d_proj, d_pooled, every):
    gathered = jnp.concatenate([near[...], far[...]], axis=0)
    every[...] = gathered
    count = gathered.shape[0]

    def device(shape, axis):
        place = lax.broadcasted_iota(jnp.int32, shape, axis) // (2 * segs)
        other = jnp.zeros(shape, jnp.int32)
        for at, bit in enumerate(bits):
            other = other + ((place >> at) & 1) * bit
        return other ^ (info[0] * NB + info[1])

    value, d_low = loss_math(
        segs, device((count, 1), 0), device((1, count), 1), gathered, w_proj[...]
    )
    flat = jnp.broadcast_to(value[: 2 * segs], (2 * segs, 128)).T
    loss[...] = flat[:1, segs : 2 * segs].reshape(segs)
    d_proj[...] = d_low
    d_pooled[...] = nt(d_low[: 2 * segs], w_proj[...])


def out_ff_blocks(info, rows, hidden, dst):
    size = 2 * LANES
    at = (pl.program_id(0) ^ (info[0] // 2)) * size
    res = nn(rows, hidden[:, pl.ds(pl.multiple_of(at, size), size)]).astype(BF16)
    cols = res.shape[0] // 2
    for y in range(2):
        for x in range(2):
            dst.at[y, 0][x ^ (info[0] % 2)] = res[
                y * cols : (y + 1) * cols, x * LANES : (x + 1) * LANES
            ]


def out_ff_send_kernel(
    lp, lq, segs, info, d_pooled, output, lgain, hidden,
    d_output, d_ffn, gain_grad, turned, send,
):
    total = lp + lq
    rows = output.shape[1] // NB
    half = 2 * rows

    @pl.when(pl.program_id(0) == 0)
    def _():
        lo, hi = seg_bounds(info, segs, (lp, lq), (1, 2 * segs), 1)
        lo_c, hi_c = seg_bounds(info, segs, (lp, lq), (2 * segs, 1), 0)
        lo, hi = (jnp.concatenate([v, v], axis=1) for v in (lo, hi))
        at = lax.broadcasted_iota(jnp.int32, (total, 4 * segs), 0)
        hot = jnp.where((at >= lo) & (at < hi), 1.0, 0.0).astype(BF16)
        dy = nn(hot, encode(d_pooled[...] / (hi_c - lo_c).astype(F32)))
        dv, dg = rms_back(output[...], wide_row(lgain), dy)
        d_output[...] = dv
        gain_grad[...] = dg
        low = dv.astype(BF16)
        d_ffn[...] = low
        flipped = low.T
        for n in range(NB):
            other = n ^ info[1]
            at_row = (other % 2) * half + (other // 2) * rows
            turned[pl.ds(pl.multiple_of(at_row, rows), rows), :] = flipped[
                n * rows : (n + 1) * rows
            ]

    out_ff_blocks(info, turned[half:, :], hidden, send)


def out_ff_keep_kernel(info, turned, hidden, keep):
    out_ff_blocks(info, turned[: turned.shape[0] // 2, :], hidden, keep)


def turn_rows(dst, value, wide):
    rows = value.shape[1] // WB
    flipped = value.T
    for w in range(WB):
        dst[pl.ds(pl.multiple_of((w ^ wide) * rows, rows), rows), :] = flipped[
            w * rows : (w + 1) * rows
        ]


def turn_kernel(info, normed_two, ctx, normed, turned_two, turned_ctx, turned):
    turn_rows(turned_two, normed_two[...], info[0])
    turn_rows(turned_ctx, ctx[...], info[0])
    turn_rows(turned, normed[...], info[0])


def join_kernel(info, *refs):
    parts = [r[...].astype(F32) for r in refs[:-1]]
    refs[-1][...] = jnp.concatenate(parts, axis=0).astype(BF16)


def turn(step, narrow):
    return ((step % 2) * 2 + (1 - step // 2)) ^ narrow


def ffn_tile(number, d_ffn, w_back, slope, w_in, turned):
    size = slope.shape[1] // NB
    tile = pl.ds(pl.multiple_of(number * size, size), size)
    d_up = (nt(d_ffn[...], w_back[tile, :]) * slope[:, tile].astype(F32)).astype(BF16)
    res = nn(turned[...], d_up).astype(BF16)
    rows = res.shape[0] // WB
    blocks = jnp.concatenate(
        [
            res[:, half * LANES : (half + 1) * LANES].reshape(WB, rows, LANES)
            for half in range(2)
        ],
        axis=1,
    )
    return nt(d_up, w_in[:, tile]), blocks


def ffn_back_first_kernel(info, d_ffn, w_back, slope, w_in, turned, send, keep, total):
    step = pl.program_id(0)

    @pl.when(step == 0)
    def _():
        total[...] = jnp.zeros_like(total)

    part, blocks = ffn_tile(turn(step, info[1]), d_ffn, w_back, slope, w_in, turned)
    total[...] += part

    @pl.when(step < 2)
    def _():
        send[step] = blocks

    @pl.when(step == 2)
    def _():
        keep[...] = blocks


def ffn_back_last_kernel(
    info, d_ffn, w_back, slope, w_in, turned, so_far, d_output, residual, fgain, turned_ctx, w_out,
    keep, d_resid, gain_grad, d_ctx, send_o, keep_o,
):
    part, blocks = ffn_tile(turn(3, info[1]), d_ffn, w_back, slope, w_in, turned)
    keep[...] = blocks
    width = residual.shape[1]
    rows, cols = width // WB, width // NB
    dv, dg = rms_back(residual[...], wide_row(fgain), so_far[...] + part)
    dr = d_output[...] + dv
    d_resid[...] = dr
    gain_grad[...] = dg
    da = dr.astype(BF16)
    d_ctx[...] = nt(da, w_out[...]).astype(BF16)
    grad = nn(turned_ctx[...], da)
    for n in range(NB):
        part = grad[:, n * cols : (n + 1) * cols].reshape(WB, rows, cols)
        part = jnp.concatenate([part[:, : rows // 2], part[:, rows // 2 :]], axis=2)
        part = part.astype(BF16)
        y = (n // 2) ^ (info[1] // 2)

        @pl.when((n % 2) == (info[1] % 2))
        def _():
            keep_o[y] = part

        @pl.when((n % 2) != (info[1] % 2))
        def _():
            send_o[y] = part


def attn_back_kernel(dk, lp, lq, info, q, k, v, d_ctx, probs_p, probs_q, d_qkv, sums):
    step = pl.program_id(0)
    reach = lp // 2
    size = HS * dk
    out = d_qkv.at[:, :, pl.ds(pl.multiple_of(step * size, size), size)]

    @pl.when(step == 0)
    def _():
        sums[...] = jnp.zeros_like(sums)

    units = []
    for hh in range(HS):
        cols = slice(hh * dk, (hh + 1) * dk)
        for off, span, probs in ((0, lp, probs_p), (lp, lq, probs_q)):
            half = span // 2
            for part in range(2):
                here = slice(off + part * half, off + (part + 1) * half)
                units.append((hh, cols, here, half, probs, 2 * hh + part))
    d_probs = [nt(v[here, cols], d_ctx[here, cols]) for _, cols, here, _, _, _ in units]
    tiles = [[jnp.zeros((CH, CH), F32)] * (2 * reach // CH) for _ in range(HS)]
    lows = []
    for (hh, _, _, half, probs, at), d_prob in zip(units, d_probs):
        p = probs[at].astype(F32)
        t = p * d_prob
        ds = t - p * jnp.sum(t, axis=0, keepdims=True)
        lows.append(ds.astype(BF16))
        for a in range(half // CH):
            for b in range(half // CH):
                to = b + reach // CH - a
                piece = ds[a * CH : (a + 1) * CH, b * CH : (b + 1) * CH]
                tiles[hh][to] = tiles[hh][to] + piece
    for (_, cols, here, _, probs, at), low in zip(units, lows):
        out[0, here, cols] = tn(low, k[here, cols]).astype(BF16)
        out[1, here, cols] = nn(low, q[here, cols]).astype(BF16)
        out[2, here, cols] = nn(probs[at], d_ctx[here, cols]).astype(BF16)
    at_i = lax.broadcasted_iota(jnp.int32, (CH, CH), 0)
    at_j = lax.broadcasted_iota(jnp.int32, (CH, CH), 1)
    mirror = jnp.where(at_i + at_j == CH - 1, 1.0, 0.0).astype(BF16)
    for hh in range(HS):
        flipped = nn(mirror, jnp.concatenate(tiles[hh], axis=1).astype(BF16))
        turn = pltpu.roll(flipped, 0, 1, stride=1, stride_axis=0)
        sums[pl.ds(HS * step + hh, 1), :] = jnp.sum(turn, axis=0, keepdims=True)


def qkv_grad_kernel(
    lp, heads, info, turned, d_qkv, wq, wk, wv, gain, g_ffn, g_final, sums,
    send, keep, column,
):
    width = turned.shape[0]
    rows, cols = width // WB, width // NB
    each = rows + rows // 2
    size = WB * each
    core, y0 = info[1] % 2, info[1] // 2

    def put(n, first, values):
        for dst, mine in ((keep, n % 2 == core), (send, n % 2 != core)):

            @pl.when(mine)
            def _():
                for w in range(WB):
                    at = pl.multiple_of(((n // 2) ^ y0) * size + (w * each + first), 16)
                    dst[pl.ds(at, values.shape[1]), :] = values[w]

    def gradient(grads, weight):
        grad = nn(turned[...], grads)
        for w in range(WB):
            at = pl.ds(pl.multiple_of((w ^ info[0]) * rows, rows), rows)
            part = grad[w * rows : (w + 1) * rows, :] * weight[at, :].astype(F32)
            column[at, :] += jnp.broadcast_to(
                jnp.sum(part, axis=1, keepdims=True), (rows, column.shape[1])
            )
        return grad

    column[...] = jnp.zeros_like(column)
    gq, gk = gradient(d_qkv[0], wq), gradient(d_qkv[1], wk)
    for n in range(NB):
        here = slice(n * cols, (n + 1) * cols)
        both = jnp.concatenate([gq[:, here], gk[:, here]], axis=1).astype(BF16)
        put(n, 0, both.reshape(WB, rows, LANES))
    gv = gradient(d_qkv[2], wv)
    for n in range(NB):
        part = gv[:, n * cols : (n + 1) * cols].reshape(WB, rows, cols)
        part = jnp.concatenate([part[:, : rows // 2], part[:, rows // 2 :]], axis=2)
        put(n, rows, part.astype(BF16))
    g_attn = column[...].T[:1, :] / wide_row(gain)
    hot = bucket_hot(lp // 2, CH - 1).astype(F32)
    bias = nt(sums[...], hot, precision=HIGHEST)
    pieces = []
    for grad in (g_attn, g_ffn[...], g_final[...]):
        pieces += [grad[:, i : i + LANES] for i in range(0, width, LANES)]
    pieces.append(jnp.concatenate([bias[h : h + 1, :] for h in range(heads)], axis=1))
    pieces.append(jnp.zeros((SMALL - len(pieces), LANES), F32))
    small = encode(jnp.concatenate(pieces, axis=0))
    send[2 * size :, :] = small
    keep[2 * size :, :] = small


def input_kernel(segs, info, d_qkv, wq, wk, wv, d_resid, x, gain, grad_p, grad_q):
    off = 0
    for tower, grad in enumerate((grad_p, grad_q)):
        span = grad.shape[0]
        here = slice(off, off + span)
        off += span
        dn = nt(d_qkv[0, here], wq[...]) + nt(d_qkv[1, here], wk[...])
        dn = dn + nt(d_qkv[2, here], wv[...])
        v = x[here, :].astype(F32)
        r = lax.rsqrt(jnp.mean(v * v, axis=-1, keepdims=True) + EPS)
        gdy = wide_row(gain) * dn
        inner = jnp.mean(gdy * v, axis=-1, keepdims=True)
        out = d_resid[here, :] + (r * gdy - v * (r * r * r * inner))
        grad[...] = pltpu.roll(out, half_at(info, tower, segs, span), 0)


def proj_kernel(info, every, d_proj, proj_grad, full):
    rows, cols = proj_grad.shape
    width = full.shape[0]
    full[...] = tn(every[:, :width], d_proj[...])
    mine = full[pl.ds(pl.multiple_of(info[0] * rows, 8), rows), :]
    for n in range(width // cols):

        @pl.when(info[1] == n)
        def _():
            proj_grad[...] = mine[:, n * cols : (n + 1) * cols]


class Info:
    def __init__(self, place, passages, queries, pairs):
        segs = passages.shape[1]
        self.at = [lambda: place[0], lambda: place[1]]
        self.at += [functools.partial(lambda r, i: r[0, i], passages, i) for i in range(segs)]
        self.at += [functools.partial(lambda r, i: r[0, i], queries, i) for i in range(segs)]
        self.at += [functools.partial(lambda r, i: r[i], pairs, i) for i in range(segs)]

    def __getitem__(self, i):
        return self.at[i]()


def call(
    kernel, grid, info, args, in_specs, outs, out_specs, scratch=(), flops=0, moved=0,
    vmem=16, after=(), through=(), through_specs=(),
):
    count, more = len(args), len(after) + len(through)
    outs, out_specs = list(outs), list(out_specs)
    made = len(outs)
    aliases = {len(info) + count + len(after) + i: made + i for i in range(len(through))}
    outs += [(hbm_out if through_specs else shaped)(a.shape, a.dtype) for a in through]
    out_specs += through_specs or [pl.BlockSpec(memory_space=pl.ANY)] * len(through)
    hidden = 0 if through_specs else len(through)

    def body(*refs):
        scalars, refs = refs[: len(info)], refs[len(info) :]
        results = refs[count + more :]
        kernel(
            Info(*scalars) if scalars else None,
            *refs[:count],
            *results[:made],
            *results[made + hidden :],
        )

    return pl.pallas_call(
        body,
        grid_spec=pltpu.PrefetchScalarGridSpec(
            num_scalar_prefetch=len(info),
            grid=grid,
            in_specs=list(in_specs) + [pl.BlockSpec(memory_space=pl.ANY)] * more,
            out_specs=out_specs,
            scratch_shapes=list(scratch),
        ),
        out_shape=outs,
        input_output_aliases=aliases,
        compiler_params=pltpu.CompilerParams(vmem_limit_bytes=vmem * 2**20),
        cost_estimate=pl.CostEstimate(flops=flops, bytes_accessed=moved, transcendentals=0),
    )(*info, *args, *after, *through)


def hbm(array):
    return pltpu.with_memory_space_constraint(array, pltpu.HBM)


def near(*shape):
    return pl.BlockSpec(memory_space=pltpu.VMEM)


def whole(*shape):
    return pl.BlockSpec(shape, lambda *_: (0,) * len(shape), pipeline_mode=pl.Buffered(1))


def hbm_out(shape, dtype):
    return pltpu.HBM(shape, dtype)


def out_shape_of(out):
    return out.inner_aval.shape


def shaped(shape, dtype):
    return jax.ShapeDtypeStruct(shape, dtype)


def permute(array, bit, count):
    return lax.ppermute(array, AXES, [(i, i ^ bit) for i in range(count)])


CORE, Y, X, Z0, Z1 = 1, 2, 4, 8, 16
GATHER = (Z0, Z1, Y, X, CORE)


def own_sum(base, refs):
    parts = [r[b:, :].astype(F32) for b, r in zip(base, refs)]
    while len(parts) > 1:
        parts = [a + b for a, b in zip(parts[::2], parts[1::2])]
    return parts[0]


def out_ff_finish_kernel(base, info, *refs):
    refs[-1][...] = own_sum(base, refs[:-1])


def in_ff_finish_kernel(base, info, *refs):
    *parts, in_ff, out_w = refs
    total = own_sum(base, parts)
    rows, cols = out_w.shape
    in_ff[...] = jnp.concatenate([total[:rows], total[rows : 2 * rows]], axis=1)
    out_w[...] = jnp.concatenate([total[2 * rows :, :cols], total[2 * rows :, cols:]], axis=0)


def split_small(small, width, heads):
    per = width // LANES
    gains = [
        jnp.concatenate([small[g * per + i : g * per + i + 1] for i in range(per)], axis=1)
        for g in range(3)
    ]
    row = small[3 * per : 3 * per + 1]
    bias = [row[:, h * BUCKETS : (h + 1) * BUCKETS] for h in range(heads)]
    return gains, jnp.concatenate(bias, axis=0)


def qkv_finish_kernel(heads, base, info, *refs):
    rest, own, *got, query_w, key_w, value_w, gain_a, gain_f, gain_l, bias = refs
    total = own_sum(base, (rest, *got))
    rows, cols = query_w.shape
    query_w[...] = total[:rows, :cols]
    key_w[...] = total[:rows, cols:]
    value_w[...] = jnp.concatenate([total[rows:, :cols], total[rows:, cols:]], axis=0)
    small = [decode(r[: 2 * SMALL, :]) for r in (own, *got)]
    small = (small[0] + small[1]) + (small[2] + small[3])
    gains, table = split_small(small, gain_a.shape[0], heads)
    for ref, gain in zip((gain_a, gain_f, gain_l), gains):
        ref[...] = gain.reshape(gain.shape[1])
    bias[...] = table


def encode(values):
    high = values.astype(BF16).astype(F32)
    return jnp.concatenate([high, values - high], axis=0).astype(BF16)


def decode(coded):
    half = coded.shape[0] // 2
    return coded[:half].astype(F32) + coded[half:].astype(F32)


class Part:
    def __init__(self, arrays, base, dims, rows, lo=0, hi=None):
        self.arrays, self.base, self.dims, self.rows = arrays, base, dims, rows
        self.lo, self.hi = lo, rows if hi is None else hi

    def at(self, where):
        dims, which = self.dims, 0
        if len(self.arrays) > 1:
            which, dims = where[dims[0]], dims[1:]
        index = 0
        for bit in dims:
            index = index * 2 + where[bit]
        return self.arrays[which], self.base + index * self.rows + self.lo


def add_kernel(plans, info, *refs):
    outs = refs[len(refs) - len(plans) :]
    for (sums, small), out in zip(plans, outs):
        if small:
            total = decode(refs[small[0]][small[1] : small[1] + 2 * SMALL, :])
            total = total + decode(refs[small[2]][small[3] : small[3] + 2 * SMALL, :])
            out[: 2 * SMALL, :] = encode(total)
        for to, a, at_a, b, at_b, rows in sums:
            value = refs[a][at_a : at_a + rows, :]
            out[to : to + rows, :] = value if b is None else value + refs[b][at_b : at_b + rows, :]


class Scatter:
    def __init__(self, groups, count, quad=False, z=(Z0, Z1)):
        self.count, self.groups, self.quad, self.z = count, groups, quad, z
        self.sources = []
        self.small = None
        self.stage = -1

    def source(self, send, keeps, rows, small=False):
        send = send.reshape(-1, LANES)
        keeps = [k.reshape(-1, LANES) for k in keeps]
        got = permute(send, CORE, self.count)
        self.sources.append((keeps, got, rows))
        if small:
            at = 16 * rows
            self.small = (keeps[0], at, got, at)

    def jobs(self):
        self.stage += 1
        stage = self.stage
        if stage == 0:
            dims = (Y, Z1, Z0, X)
            groups = [
                [
                    (
                        Part(self.sources[n][0], 0, dims, self.sources[n][2], lo, hi),
                        Part([self.sources[n][1]], 0, dims, self.sources[n][2], lo, hi),
                    )
                    for n, lo, hi in group
                ]
                for group in self.groups
            ]
        else:
            groups = [[pair] for pair in zip(self.rest, self.got)]
        if stage < 2:
            bits = ((Y, X), (X, Y))[stage]
            first = [(g, {b: 1}) for g, b in zip(groups, bits)]
            rest = [(g, {b: 0}) for g, b in zip(groups, bits)]
            self.bits = bits
        else:
            merged = [pair for group in groups for pair in group]
            if self.quad:
                self.bits = (Z0, Z1, Z0 | Z1)
                first = [(merged, {Z0: a, Z1: b}) for a, b in ((1, 0), (0, 1), (1, 1))]
                rest = [(merged, {Z0: 0, Z1: 0})]
            else:
                bit = self.z[stage - 2]
                self.bits = (bit,)
                first, rest = [(merged, {bit: 1})], [(merged, {bit: 0})]
        carry = [self.small is not None and (stage >= 2 or i == 1) for i in range(len(first))]
        return first, rest, carry

    def take(self, first, rest, hold=False):
        self.first, self.rest, self.got = first, rest, []
        if hold:
            return
        for part, bit in zip(first, self.bits):
            got = permute(part.arrays[0], bit, self.count)
            self.got.append(Part([got], part.base, part.dims, part.rows))
        if self.small is not None:
            at = 0 if self.stage >= 2 else 1
            self.small = (first[at].arrays[0], 0, self.got[at].arrays[0], 0)

    def finish(self):
        parts = [self.rest[0], *self.got]
        return [p.arrays[0] for p in parts], tuple(p.base for p in parts)


def advance(info, scatters, after=(), through=(), hold=None, join=None):
    inputs, plans, shapes, slots = [], [], [], []

    def find(array):
        for i, known in enumerate(inputs):
            if known is array:
                return i
        inputs.append(array)
        return len(inputs) - 1

    for scatter in scatters:
        first, rest, carry = scatter.jobs()
        for n, (pairs, fixed) in enumerate(first + rest):
            dims = tuple(d for d in pairs[0][0].dims if d not in fixed)
            rows = sum(a.hi - a.lo for a, _ in pairs)
            base, small = 0, ()
            if n < len(first) and carry[n]:
                own, at_own, got, at_got = scatter.small
                base, small = 2 * SMALL, (find(own), at_own, find(got), at_got)
            sums = []
            for index in range(2 ** len(dims)):
                where = dict(fixed)
                for i, d in enumerate(reversed(dims)):
                    where[d] = (index >> i) & 1
                to = base + index * rows
                for a, b in pairs:
                    (array_a, row_a), (array_b, row_b) = a.at(where), b.at(where)
                    size = a.hi - a.lo
                    sums.append((to, find(array_a), row_a, find(array_b), row_b, size))
                    to += size
            end = base + 2 ** len(dims) * rows
            if join is not None and scatter is join[0] and n == 0:
                (held,) = join[1].first
                sums.append((end, find(held.arrays[0]), held.base, None, 0, held.rows))
                joined = (end, held)
                end += held.rows
            plans.append((sums, small))
            shapes.append(shaped((end, LANES), BF16))
            slots.append((base, dims, rows))
        scatter.counts = (len(first), len(rest))
    outs = call(
        functools.partial(add_kernel, plans), (1,), info, inputs, [near()] * len(inputs), shapes,
        [near()] * len(shapes), flops=10**6, moved=2**20, vmem=4, after=after, through=through,
    )
    handed = outs[len(slots) :]
    parts = [Part([out], *slot) for out, slot in zip(outs, slots)]
    sent = []
    for scatter in scatters:
        many, more = scatter.counts
        scatter.take(parts[:many], parts[many : many + more], scatter is hold)
        sent += [p.arrays[0] for p in parts[:many]]
        if join is not None and scatter is join[0]:
            at, held = joined
            join[1].got = [Part(scatter.got[0].arrays, at, held.dims, held.rows)]
        parts = parts[many + more :]
    return sent, handed


def per_device(
    fast, n_wide, n_narrow,
    xp, xq, passage_lengths, query_lengths, pair_index, g_attn, w_query, w_key, w_value, w_out,
    bias_table, g_ffn, w_in, w_back, g_final, w_proj,
):
    lp, width = xp.shape
    lq = xq.shape[0]
    total = lp + lq
    heads = bias_table.shape[1]
    dk = width // heads
    ff = w_in.shape[1]
    segs = passage_lengths.shape[1]
    count = n_wide * n_narrow
    steps = heads // HS
    rows, cols = width // WB, width // NB
    wide_at, narrow_at = lax.axis_index("wide"), lax.axis_index("narrow")
    place = jnp.stack([wide_at, narrow_at]) if fast else jnp.zeros((2,), jnp.int32)
    info = (place.astype(jnp.int32), hbm(passage_lengths), hbm(query_lengths), hbm(pair_index))
    mm = 2 * total * width * width
    act, act32 = shaped((total, width), BF16), shaped((total, width), F32)
    act_hbm = pltpu.HBM((total, width), BF16)

    head_tile = pl.BlockSpec((total, HS * dk), lambda i, *_: (0, i))
    col_tile = pl.BlockSpec((width, HS * dk), lambda i, *_: (0, i))
    prob_tiles = [pl.BlockSpec((2 * HS, n // 2, n // 2), lambda i, *_: (i, 0, 0)) for n in (lp, lq)]
    x, normed, q, k, v, probs_p, probs_q, ctx = call(
        functools.partial(front_kernel, lp, lq, segs, dk),
        (steps,),
        info,
        (*(hbm(a) for a in (xp, xq, g_attn, w_query, w_key, w_value)), hbm(bias_table.T)),
        [whole(lp, width), whole(lq, width), whole(width)] + [col_tile] * 3
        + [whole(heads, BUCKETS)],
        [act, act_hbm, act_hbm, act_hbm, act_hbm]
        + [pltpu.HBM((2 * heads, n // 2, n // 2), BF16) for n in (lp, lq)]
        + [act],
        [near(), whole(total, width), head_tile, head_tile, head_tile, *prob_tiles, head_tile],
        [pltpu.VMEM((16, lp), F32)],
        flops=12 * 10**9,
        moved=13 * 2**20,
    )

    ff_tile = ff // NB
    ff_spec = pl.BlockSpec((total, ff_tile), lambda i, *_: (0, i))
    message = width + 128
    residual, normed_two, hidden, slope, output, pooled = call(
        functools.partial(ffn_kernel, lp, lq, segs),
        (NB,),
        info,
        (ctx, x, w_out, g_ffn, w_in, w_back, g_final),
        [near()] * 7,
        [
            act32, act, shaped((total, ff), BF16), shaped((total, ff), BF16), act32,
            shaped((2 * segs, message), BF16),
        ],
        [near()] * 6,
        flops=9 * mm,
        moved=30 * 2**20,
        vmem=24,
    )

    turned_two, turned_ctx, turned = call(
        turn_kernel,
        (1,),
        info,
        (normed_two, ctx, normed),
        [near()] * 3,
        [shaped((width, total), BF16)] + [pltpu.HBM((width, total), BF16)] * 2,
        [near(), whole(width, total), whole(width, total)],
        flops=10**6,
        moved=2**20,
        vmem=8,
        after=[pooled],
    )
    if fast:
        parts = [pooled] + [permute(pooled, b, count) for b in (Z0, Z1, Z0 | Z1)]
        (one,) = call(
            join_kernel, (1,), info, parts, [near()] * 4,
            [shaped((4 * 2 * segs, message), BF16)], [near()], flops=10**6, moved=2**20, vmem=4,
            after=[turned_two],
        )
        two = jnp.concatenate([one] + [permute(one, b, count) for b in (Y, X, Y | X)], axis=0)
        every = 2 * two.shape[0]
        query_loss, d_proj, d_pooled, gathered = call(
            functools.partial(loss_kernel, segs, GATHER),
            (1,),
            info,
            (two, permute(two, CORE, count), w_proj),
            [near(), near(), near()],
            [
                hbm_out((segs,), F32), shaped((every, width), BF16),
                shaped((2 * segs, width), F32), shaped((every, message), BF16),
            ],
            [whole(segs), near(), near(), near()],
            flops=10**9,
            moved=2**20,
        )
    else:
        gathered = lax.all_gather(pooled, AXES, axis=0, tiled=True)
        every = gathered.shape[0]
        block = jnp.arange(every, dtype=jnp.int32) // (2 * segs)
        loss, d_proj = loss_math(segs, block[:, None], block[None, :], gathered, w_proj)
        mine = (wide_at * n_narrow + narrow_at) * 2 * segs
        query_loss = lax.dynamic_slice_in_dim(loss, mine + segs, segs, 0)[:, 0]
        d_pooled = nt(lax.dynamic_slice_in_dim(d_proj, mine, 2 * segs, 0), w_proj)

    part1 = (2, WB // 2, 2, cols, LANES)
    block1 = pl.BlockSpec((2, 1, 2, cols, LANES), lambda i, *_: (0, i, 0, 0, 0))
    d_output, d_ffn, final_gain_grad, turned_ff, send1 = call(
        functools.partial(out_ff_send_kernel, lp, lq, segs),
        (WB // 2,),
        info,
        (d_pooled, output, g_final, hidden),
        [near(), near(), near(), near()],
        [act32, act, shaped((1, width), F32), shaped((width, total), BF16), shaped(part1, BF16)],
        [near(), near(), near(), near(), block1],
        flops=3 * mm,
        moved=10 * 2**20,
        vmem=12,
    )
    (keep1,) = call(
        out_ff_keep_kernel,
        (WB // 2,),
        info,
        (turned_ff, hidden),
        [near(), near()],
        [shaped(part1, BF16)],
        [block1],
        flops=2 * mm,
        moved=8 * 2**20,
        vmem=6,
    )

    after = []
    if fast:
        sc1 = Scatter((((0, 0, cols // 2),), ((0, cols // 2, cols),)), count, z=(Z1, Z0))
        sc1.source(send1, [keep1], cols)
        after, _ = advance(info, [sc1])

    size2, size_o = 2 * rows, rows // 2
    part2 = shaped((2, WB, size2, LANES), BF16)
    part_o = shaped((2, WB, size_o, LANES), BF16)

    def tiles_at(first):
        return [
            near(),
            near(),
            near(),
            near(),
        ]

    half2 = shaped((WB, size2, LANES), BF16)
    send2, keep2a, so_far = call(
        ffn_back_first_kernel,
        (3,),
        info,
        (d_ffn, w_back, slope, w_in, turned_two),
        tiles_at(0) + [near()],
        [part2, half2, act32],
        [near()] * 3,
        flops=9 * mm,
        moved=16 * 2**20,
        vmem=16,
        after=after,
    )
    after = []
    if fast:
        after, (send2,) = advance(info, [sc1], [so_far], [send2])
    keep2b, d_resid, ffn_gain_grad, d_ctx, send_o, keep_o = call(
        ffn_back_last_kernel,
        (1,),
        info,
        (
            d_ffn, w_back, slope, w_in, turned_two, so_far, d_output, residual, g_ffn,
            turned_ctx, w_out,
        ),
        tiles_at(3) + [near()] * 7,
        [half2, act32, shaped((1, width), F32), act, part_o, part_o],
        [near()] * 6,
        flops=5 * mm,
        moved=20 * 2**20,
        vmem=18,
        after=after,
    )

    after = []
    if fast:
        sc2 = Scatter((((0, 0, 128),), ((0, 128, size2), (1, 0, size_o))), count)
        sc2.source(send2, [keep2a, keep2b], size2)
        after, (send_o,) = advance(info, [sc1], [d_ctx], [send_o])
        sc2.source(send_o, [keep_o], size_o)
        more, _ = advance(info, [sc2], after)
        after = after + more
    d_qkv, sums = call(
        functools.partial(attn_back_kernel, dk, lp, lq),
        (steps,),
        info,
        (hbm(q), hbm(k), hbm(v), d_ctx, hbm(probs_p), hbm(probs_q)),
        [head_tile] * 4 + prob_tiles,
        [shaped((3, total, width), BF16), shaped((16, lp), F32)],
        [near(), near()],
        flops=8 * 10**9,
        moved=16 * 2**20,
        after=after,
    )

    size3 = rows + rows // 2
    flat3 = shaped((16 * size3 + 16, LANES), BF16)
    send3, keep3 = call(
        functools.partial(qkv_grad_kernel, lp, heads),
        (1,),
        info,
        (
            turned, d_qkv, w_query, w_key, w_value, g_attn, ffn_gain_grad,
            final_gain_grad, sums,
        ),
        [near()] * 9,
        [flat3, flat3],
        [near(), near()],
        [
            pltpu.VMEM((width, 128), F32),
        ],
        flops=3 * mm,
        moved=9 * 2**20,
        vmem=24,
        after=after,
    )

    after = []
    own_rows, own_cols = width // WB, width // NB
    square = hbm_out((own_rows, own_cols), F32)
    if fast:

        def finish(kernel, scatter, outs, after, more=()):
            parts, base = scatter.finish()
            parts = parts[:1] + list(more) + parts[1:]
            return call(
                functools.partial(kernel, base), (1,), info, parts, [near()] * len(parts), outs,
                [whole(*out_shape_of(out)) for out in outs], flops=10**6, moved=2**20, after=after,
            )

        sc3 = Scatter((((0, 0, 80),), ((0, 80, size3),)), count, quad=True)
        after, (send3,) = advance(info, [sc1, sc2], [keep3], [send3], hold=sc1)
        sc3.source(send3, [keep3], size3, small=True)

    grad_p, grad_q = call(
        functools.partial(input_kernel, segs),
        (1,),
        info,
        (d_qkv, w_query, w_key, w_value, d_resid, x, g_attn),
        [near()] * 7,
        [hbm_out((lp, width), F32), hbm_out((lq, width), F32)],
        [whole(lp, width), whole(lq, width)],
        flops=3 * mm,
        moved=6 * 2**20,
        vmem=20,
        after=after,
    )
    after = [hbm(grad_p)]
    if fast:
        after, _ = advance(info, [sc3, sc2], after, join=(sc2, sc1))
    (proj_grad,) = call(
        proj_kernel,
        (1,),
        info,
        (gathered[:256], d_proj[:256]),
        [near(), near()],
        [square],
        [whole(own_rows, own_cols)],
        [pltpu.VMEM((width, width), F32)],
        flops=mm,
        moved=2**20,
        vmem=20,
        after=after,
    )

    if fast:
        after, _ = advance(info, [sc3, sc2], [hbm(proj_grad)])
        (out_ff,) = finish(out_ff_finish_kernel, sc1, [hbm_out((cols, ff // WB), F32)], after)
        after, _ = advance(info, [sc3], [hbm(out_ff)])
        out_ff = out_ff.T
        in_ff, out_w = finish(
            in_ff_finish_kernel, sc2, [hbm_out((rows, ff // NB), F32), square], after
        )
        query_w, key_w, value_w, gain_a, gain_f, gain_l, bias = finish(
            functools.partial(qkv_finish_kernel, heads), sc3,
            [square] * 3 + [hbm_out((width,), F32)] * 3 + [hbm_out((heads, BUCKETS), F32)],
            [hbm(out_w)], [sc3.first[0].arrays[0]],
        )
    else:
        own_rows, own_cols = width // n_wide, width // n_narrow
        left = lax.dynamic_slice(gathered, (0, wide_at * own_rows), (every, own_rows))
        right = lax.dynamic_slice(d_proj, (0, narrow_at * own_cols), (every, own_cols))
        proj_grad = tn(left, right)

        def blocks(send, keep):
            both = jnp.stack([keep, send], axis=1).astype(F32)
            return both.reshape((NB, WB) + both.shape[-2:])

        def spread(matrix):
            matrix = lax.psum_scatter(matrix, "wide", scatter_dimension=0, tiled=True)
            return lax.psum_scatter(matrix, "narrow", scatter_dimension=1, tiled=True)

        def side(part):
            half = part.shape[2] // 2
            return jnp.concatenate([part[:, :, :half], part[:, :, half:]], axis=3)

        def stack(part):
            half = part.shape[3] // 2
            return jnp.concatenate([part[..., :half], part[..., half:]], axis=2)

        def matrix(part):
            return part.transpose(1, 2, 0, 3).reshape(WB * part.shape[2], NB * part.shape[3])

        b1 = blocks(send1.reshape(2, WB, cols, LANES), keep1.reshape(2, WB, cols, LANES))
        b2 = blocks(send2, jnp.stack([keep2a, keep2b]))
        coded = keep3[16 * size3 :]
        b3 = blocks(*(a[: 16 * size3].reshape(2, WB, size3, LANES) for a in (send3, keep3)))
        out_ff = spread(matrix(b1.transpose(0, 1, 3, 2)))
        in_ff = spread(matrix(side(b2)))
        out_w = spread(matrix(stack(blocks(send_o, keep_o))))
        query_w = spread(matrix(b3[:, :, :rows, :cols]))
        key_w = spread(matrix(b3[:, :, :rows, cols:]))
        value_w = spread(matrix(stack(b3[:, :, rows:])))
        gains, bias = split_small(lax.psum(decode(coded), AXES), width, heads)
        gain_a, gain_f, gain_l = (gain[0] for gain in gains)
    return (
        query_loss, grad_p, grad_q, gain_a, query_w, key_w, value_w, out_w, bias.T, gain_f,
        in_ff, out_ff, gain_l, proj_grad,
    )


def solution(mesh):
    n_wide, n_narrow = mesh.shape["wide"], mesh.shape["narrow"]
    fast = (n_wide, n_narrow) == (WB, NB)
    rows = P(AXES, None)
    owned = P("wide", "narrow")
    return jax.shard_map(
        functools.partial(per_device, fast, n_wide, n_narrow),
        mesh=mesh,
        in_specs=(rows, rows, rows, rows, P(AXES)) + (P(),) * 11,
        out_specs=(
            P(AXES), rows, rows, P(), owned, owned, owned, owned, P(), P(),
            owned, owned, P(), owned,
        ),
        check_vma=False,
    )
```

```python
import functools

import jax
import jax.numpy as jnp
from jax import lax
from jax.experimental import pallas as pl
from jax.experimental.pallas import tpu as pltpu
from jax.sharding import PartitionSpec as P

BUCKETS = 32
MAX_DIST = 128
SCALE = 0.02
EPS = 1e-06
GELU = 0.7978845608028654
CUBE = 0.044715
HIGHEST = lax.Precision.HIGHEST
F32 = jnp.float32
BF16 = jnp.bfloat16
AXES = ("wide", "narrow")
NB = 4
WB = 8
CH = 128
LANES = 384
HS = 4
SMALL = 8


def bucket_edges():
    half = BUCKETS // 2
    exact = half // 2
    levels = half - exact
    ratio = MAX_DIST // exact
    edges = []
    for step in range(1, levels):
        target = exact**levels * ratio**step
        candidate = exact
        while candidate**levels < target:
            candidate += 1
        edges.append(candidate)
    return edges


def nn(a, b, **kw):
    return lax.dot_general(a, b, (((1,), (0,)), ((), ())), preferred_element_type=F32, **kw)


def tn(a, b):
    return lax.dot_general(a, b, (((0,), (0,)), ((), ())), preferred_element_type=F32)


def nt(a, b, **kw):
    return lax.dot_general(a, b, (((1,), (1,)), ((), ())), preferred_element_type=F32, **kw)


def bucket_hot(span, shift=0):
    shape = (BUCKETS, 2 * span)
    rel = lax.broadcasted_iota(jnp.int32, shape, 1) - shift
    rel = span - jnp.where(rel < 0, rel + 2 * span, rel)
    dist = jnp.abs(rel)
    half = BUCKETS // 2
    exact = half // 2
    far = jnp.full(shape, exact, jnp.int32)
    for edge in bucket_edges():
        far = far + jnp.where(dist >= edge, 1, 0)
    far = jnp.minimum(far, half - 1)
    bucket = jnp.where(dist < exact, dist, far) + jnp.where(rel > 0, half, 0)
    return bucket == lax.broadcasted_iota(jnp.int32, shape, 0)


def half_at(info, tower, segs, span):
    at, start = 0, 0
    for s in range(segs):
        size = info[2 + tower * segs + s]
        at = jnp.where(size == span // 2, start, at)
        start = start + size
    return at


def rolled_starts(info, tower, segs, span):
    at, start, starts = half_at(info, tower, segs, span), 0, []
    for s in range(segs):
        starts.append(jnp.where(start >= at, start - at, start - at + span))
        start = start + info[2 + tower * segs + s]
    return starts


def seg_bounds(info, segs, spans, shape, axis):
    at = lax.broadcasted_iota(jnp.int32, shape, axis)
    lo = jnp.zeros(shape, jnp.int32)
    hi = jnp.zeros(shape, jnp.int32)
    for tower, span in enumerate(spans):
        starts = rolled_starts(info, tower, segs, span)
        for s in range(segs):
            here = at == tower * segs + s
            start = starts[s] + tower * spans[0]
            lo = jnp.where(here, start, lo)
            hi = jnp.where(here, start + info[2 + tower * segs + s], hi)
    return lo, hi


def seg_of(info, tower, segs, span, shape, axis):
    at = lax.broadcasted_iota(jnp.int32, shape, axis) + span // 2
    seg = jnp.zeros(shape, jnp.int32)
    for start in rolled_starts(info, tower, segs, span):
        seg = seg + jnp.where(at >= start, 1, 0)
    return seg


def rms(v, gain):
    return v * lax.rsqrt(jnp.mean(v * v, axis=-1, keepdims=True) + EPS) * gain


def rms_back(v, gain, dy):
    r = lax.rsqrt(jnp.mean(v * v, axis=-1, keepdims=True) + EPS)
    gdy = gain * dy
    inner = jnp.mean(gdy * v, axis=-1, keepdims=True)
    return r * gdy - v * (r * r * r * inner), jnp.sum(dy * v * r, axis=0, keepdims=True)


def wide_row(gain):
    return gain[...].astype(F32).reshape(1, gain.shape[0])


def front_kernel(
    lp, lq, segs, dk, info, xp, xq, gain, wq, wk, wv, table,
    x, normed, q, k, v, probs_p, probs_q, ctx, rows,
):
    reach = lp // 2

    @pl.when(pl.program_id(0) == 0)
    def _():
        heads = table.shape[0]
        rows[:heads, :] = nn(table[...], bucket_hot(reach).astype(F32).astype(BF16))
        g = wide_row(gain)
        for tower, tokens, off, span in ((0, xp, 0, lp), (1, xq, lp, lq)):
            at = half_at(info, tower, segs, span)
            rolled = pltpu.roll(tokens[...].astype(F32), jnp.where(at == 0, 0, span - at), 0)
            here = slice(off, off + span)
            x[here, :] = rolled.astype(BF16)
            normed[here, :] = rms(rolled, g).astype(BF16)

    weights = jnp.concatenate([wq[...], wk[...], wv[...]], axis=1)
    qkv = nn(normed[...], weights).astype(BF16)
    cut = HS * dk
    q[...] = qkv[:, :cut]
    k[...] = qkv[:, cut : 2 * cut]
    v[...] = qkv[:, 2 * cut :]
    units = []
    for hh in range(HS):
        row = rows[pl.ds(HS * pl.program_id(0) + hh, 1), :]
        bias = pltpu.roll(jnp.broadcast_to(row, (CH, 2 * reach)), 0, 1, stride=1, stride_axis=0)
        cols = slice(hh * dk, (hh + 1) * dk)
        for tower, off, span, probs in ((0, 0, lp, probs_p), (1, lp, lq, probs_q)):
            half = span // 2
            full = jnp.concatenate(
                [bias[:, reach - r0 : reach - r0 + half] for r0 in range(0, half, CH)], axis=0
            )
            for part in range(2):
                here = slice(off + part * half, off + (part + 1) * half)
                units.append((tower, span, cols, here, full, probs, 2 * hh + part))
    scores = []
    for tower, span, cols, here, full, _, at in units:
        s = nt(k[here, cols], q[here, cols]) + full
        if at % 2:
            half = span // 2
            seg_j = seg_of(info, tower, segs, span, (half, 1), 0)
            seg_i = seg_of(info, tower, segs, span, (1, half), 1)
            s = jnp.where(seg_i == seg_j, s, -1000000000.0)
        scores.append(s)
    lows = []
    for (_, _, _, _, _, probs, at), s in zip(units, scores):
        e = jnp.exp(s - jnp.max(s, axis=0, keepdims=True))
        p = e * (1.0 / jnp.sum(e, axis=0, keepdims=True))
        p = p.astype(BF16)
        probs[at] = p
        lows.append(p)
    for (_, _, cols, here, _, _, _), p in zip(units, lows):
        ctx[here, cols] = tn(p, v[here, cols]).astype(BF16)


def ffn_kernel(
    lp, lq, segs, info, ctx, x, w_out, fgain, w_in, w_back, lgain,
    residual, normed_two, hidden, slope, output, pooled,
):
    step = pl.program_id(0)
    total = lp + lq

    @pl.when(step == 0)
    def _():
        g = wide_row(fgain)
        res = x[...].astype(F32) + nn(ctx[...], w_out[...])
        residual[...] = res
        output[...] = res
        normed_two[...] = rms(res, g).astype(BF16)

    part = 256
    parts = [slice(r0, r0 + part) for r0 in range(0, total, part)]

    size = slope.shape[1] // NB
    tile = pl.ds(pl.multiple_of(step * size, size), size)

    def up(here):
        return nn(normed_two[here, :], w_in[:, tile])

    u = up(parts[0])
    for n, here in enumerate(parts):
        following = up(parts[n + 1]) if n + 1 < len(parts) else None
        uu = u * u
        t = jnp.tanh(u * (GELU + (GELU * CUBE) * uu))
        half = 0.5 + 0.5 * t
        h = (u * half).astype(BF16)
        hidden[here, tile] = h
        slope[here, tile] = (
            half + (u * (0.5 - (0.5 * t) * t)) * (GELU + (3.0 * GELU * CUBE) * uu)
        ).astype(BF16)
        output[here, :] += nn(h, w_back[tile, :])
        u = following

    @pl.when(step == pl.num_programs(0) - 1)
    def _():
        final = rms(output[...], wide_row(lgain))
        lo, hi = seg_bounds(info, segs, (lp, lq), (2 * segs, 1), 0)
        at = lax.broadcasted_iota(jnp.int32, (2 * segs, total), 1)
        hot = jnp.where((at >= lo) & (at < hi), 1.0, 0.0).astype(BF16)
        high = final.astype(BF16)
        mean = nn(hot, high) + nn(hot, (final - high.astype(F32)).astype(BF16))
        mean = mean / (hi - lo).astype(F32)
        width = final.shape[1]
        pooled[:, :width] = mean.astype(BF16)
        shape = (2 * segs, pooled.shape[1] - width)
        at_row = lax.broadcasted_iota(jnp.int32, shape, 0)
        at_col = lax.broadcasted_iota(jnp.int32, shape, 1)
        code = jnp.zeros(shape, jnp.int32)
        for s in range(segs):
            pair = info[2 + 2 * segs + s]
            code = jnp.where((at_row == segs + s) & (at_col == 0), pair // 64, code)
            code = jnp.where((at_row == segs + s) & (at_col == 1), pair % 64, code)
        pooled[:, width:] = code.astype(F32).astype(BF16)


def loss_math(segs, block_row, block_col, gathered, w_proj):
    count = gathered.shape[0]
    width = w_proj.shape[0]
    low = gathered[:, :width]
    code = gathered[:, width:].astype(F32)
    pair = code[:, 0:1] * 64.0 + code[:, 1:2]
    row = lax.broadcasted_iota(jnp.int32, (count, 1), 0) % (2 * segs)
    col = lax.broadcasted_iota(jnp.int32, (1, count), 1) % (2 * segs)
    number = (block_col * segs + col).astype(F32)
    is_query = row >= segs
    is_passage = col < segs
    proj = nn(low, w_proj)
    scale = lax.rsqrt(jnp.sum(proj * proj, axis=-1, keepdims=True) + EPS)
    embed = proj * scale
    embed_low = embed.astype(BF16)
    sims = nt(embed_low, embed_low) / SCALE
    masked = jnp.where(is_passage, sims, -1e30)
    top = jnp.max(masked, axis=1, keepdims=True)
    expo = jnp.where(is_passage, jnp.exp(masked - top), 0.0)
    total = jnp.sum(expo, axis=1, keepdims=True)
    hot = jnp.where(is_passage & (number == pair), 1.0, 0.0)
    loss = top + jnp.log(total) - jnp.sum(hot * sims, axis=1, keepdims=True)
    d_sims = jnp.where(is_query, (expo / total - hot) / SCALE, 0.0)
    both = d_sims + d_sims.T
    high = both.astype(BF16)
    rest = (both - high.astype(F32)).astype(BF16)
    d_embed = nn(high, embed_low) + nn(rest, embed_low)
    d_proj = (d_embed - embed * jnp.sum(embed * d_embed, axis=-1, keepdims=True)) * scale
    return loss, d_proj.astype(BF16)


def loss_kernel(segs, bits, info, near, far, w_proj, loss, d_proj, d_pooled, every):
    gathered = jnp.concatenate([near[...], far[...]], axis=0)
    every[...] = gathered
    count = gathered.shape[0]

    def device(shape, axis):
        place = lax.broadcasted_iota(jnp.int32, shape, axis) // (2 * segs)
        other = jnp.zeros(shape, jnp.int32)
        for at, bit in enumerate(bits):
            other = other + ((place >> at) & 1) * bit
        return other ^ (info[0] * NB + info[1])

    value, d_low = loss_math(
        segs, device((count, 1), 0), device((1, count), 1), gathered, w_proj[...]
    )
    flat = jnp.broadcast_to(value[: 2 * segs], (2 * segs, 128)).T
    loss[...] = flat[:1, segs : 2 * segs].reshape(segs)
    d_proj[...] = d_low
    d_pooled[...] = nt(d_low[: 2 * segs], w_proj[...])


def out_ff_blocks(info, rows, hidden, dst):
    size = 2 * LANES
    at = (pl.program_id(0) ^ (info[0] // 2)) * size
    res = nn(rows, hidden[:, pl.ds(pl.multiple_of(at, size), size)]).astype(BF16)
    cols = res.shape[0] // 2
    for y in range(2):
        for x in range(2):
            dst.at[y, 0][x ^ (info[0] % 2)] = res[
                y * cols : (y + 1) * cols, x * LANES : (x + 1) * LANES
            ]


def out_ff_send_kernel(
    lp, lq, segs, info, d_pooled, output, lgain, hidden,
    d_output, d_ffn, gain_grad, turned, send,
):
    total = lp + lq
    rows = output.shape[1] // NB
    half = 2 * rows

    @pl.when(pl.program_id(0) == 0)
    def _():
        lo, hi = seg_bounds(info, segs, (lp, lq), (1, 2 * segs), 1)
        lo_c, hi_c = seg_bounds(info, segs, (lp, lq), (2 * segs, 1), 0)
        lo, hi = (jnp.concatenate([v, v], axis=1) for v in (lo, hi))
        at = lax.broadcasted_iota(jnp.int32, (total, 4 * segs), 0)
        hot = jnp.where((at >= lo) & (at < hi), 1.0, 0.0).astype(BF16)
        dy = nn(hot, encode(d_pooled[...] / (hi_c - lo_c).astype(F32)))
        dv, dg = rms_back(output[...], wide_row(lgain), dy)
        d_output[...] = dv
        gain_grad[...] = dg
        low = dv.astype(BF16)
        d_ffn[...] = low
        flipped = low.T
        for n in range(NB):
            other = n ^ info[1]
            at_row = (other % 2) * half + (other // 2) * rows
            turned[pl.ds(pl.multiple_of(at_row, rows), rows), :] = flipped[
                n * rows : (n + 1) * rows
            ]

    out_ff_blocks(info, turned[half:, :], hidden, send)


def out_ff_keep_kernel(info, turned, hidden, normed_two, keep, turned_two):
    @pl.when(pl.program_id(0) == 0)
    def _():
        turn_rows(turned_two, normed_two[...], info[0])

    out_ff_blocks(info, turned[: turned.shape[0] // 2, :], hidden, keep)


def turn_rows(dst, value, wide):
    rows = value.shape[1] // WB
    flipped = value.T
    for w in range(WB):
        dst[pl.ds(pl.multiple_of((w ^ wide) * rows, rows), rows), :] = flipped[
            w * rows : (w + 1) * rows
        ]


def turn_kernel(info, ctx, normed, turned_ctx, turned):
    turn_rows(turned_ctx, ctx[...], info[0])
    turn_rows(turned, normed[...], info[0])


def turn(step, narrow):
    return ((step % 2) * 2 + (1 - step // 2)) ^ narrow


def ffn_tile(number, d_ffn, w_back, slope, w_in, turned):
    size = slope.shape[1] // NB
    tile = pl.ds(pl.multiple_of(number * size, size), size)
    d_up = (nt(d_ffn[...], w_back[tile, :]) * slope[:, tile].astype(F32)).astype(BF16)
    res = nn(turned[...], d_up).astype(BF16)
    rows = res.shape[0] // WB
    blocks = jnp.concatenate(
        [
            res[:, half * LANES : (half + 1) * LANES].reshape(WB, rows, LANES)
            for half in range(2)
        ],
        axis=1,
    )
    return nt(d_up, w_in[:, tile]), blocks


def ffn_back_first_kernel(info, d_ffn, w_back, slope, w_in, turned, send, keep, total):
    step = pl.program_id(0)

    @pl.when(step == 0)
    def _():
        total[...] = jnp.zeros_like(total)

    part, blocks = ffn_tile(turn(step, info[1]), d_ffn, w_back, slope, w_in, turned)
    total[...] += part

    @pl.when(step < 2)
    def _():
        send[step] = blocks

    @pl.when(step == 2)
    def _():
        keep[...] = blocks


def ffn_back_last_kernel(
    info, d_ffn, w_back, slope, w_in, turned, so_far, d_output, residual, fgain, turned_ctx, w_out,
    keep, d_resid, gain_grad, d_ctx, send_o, keep_o,
):
    part, blocks = ffn_tile(turn(3, info[1]), d_ffn, w_back, slope, w_in, turned)
    keep[...] = blocks
    width = residual.shape[1]
    rows, cols = width // WB, width // NB
    dv, dg = rms_back(residual[...], wide_row(fgain), so_far[...] + part)
    dr = d_output[...] + dv
    d_resid[...] = dr
    gain_grad[...] = dg
    da = dr.astype(BF16)
    d_ctx[...] = nt(da, w_out[...]).astype(BF16)
    grad = nn(turned_ctx[...], da)
    for n in range(NB):
        part = grad[:, n * cols : (n + 1) * cols].reshape(WB, rows, cols)
        part = jnp.concatenate([part[:, : rows // 2], part[:, rows // 2 :]], axis=2)
        part = part.astype(BF16)
        y = (n // 2) ^ (info[1] // 2)

        @pl.when((n % 2) == (info[1] % 2))
        def _():
            keep_o[y] = part

        @pl.when((n % 2) != (info[1] % 2))
        def _():
            send_o[y] = part


def attn_back_kernel(dk, lp, lq, info, q, k, v, d_ctx, probs_p, probs_q, d_qkv, sums):
    step = pl.program_id(0)
    reach = lp // 2
    size = HS * dk
    out = d_qkv.at[:, :, pl.ds(pl.multiple_of(step * size, size), size)]

    @pl.when(step == 0)
    def _():
        sums[...] = jnp.zeros_like(sums)

    units = []
    for hh in range(HS):
        cols = slice(hh * dk, (hh + 1) * dk)
        for off, span, probs in ((0, lp, probs_p), (lp, lq, probs_q)):
            half = span // 2
            for part in range(2):
                here = slice(off + part * half, off + (part + 1) * half)
                units.append((hh, cols, here, half, probs, 2 * hh + part))
    d_probs = [nt(v[here, cols], d_ctx[here, cols]) for _, cols, here, _, _, _ in units]
    tiles = [[jnp.zeros((CH, CH), F32)] * (2 * reach // CH) for _ in range(HS)]
    lows = []
    for (hh, _, _, half, probs, at), d_prob in zip(units, d_probs):
        p = probs[at].astype(F32)
        t = p * d_prob
        ds = t - p * jnp.sum(t, axis=0, keepdims=True)
        lows.append(ds.astype(BF16))
        for a in range(half // CH):
            for b in range(half // CH):
                to = b + reach // CH - a
                piece = ds[a * CH : (a + 1) * CH, b * CH : (b + 1) * CH]
                tiles[hh][to] = tiles[hh][to] + piece
    for (_, cols, here, _, probs, at), low in zip(units, lows):
        out[0, here, cols] = tn(low, k[here, cols]).astype(BF16)
        out[1, here, cols] = nn(low, q[here, cols]).astype(BF16)
        out[2, here, cols] = nn(probs[at], d_ctx[here, cols]).astype(BF16)
    at_i = lax.broadcasted_iota(jnp.int32, (CH, CH), 0)
    at_j = lax.broadcasted_iota(jnp.int32, (CH, CH), 1)
    mirror = jnp.where(at_i + at_j == CH - 1, 1.0, 0.0).astype(BF16)
    for hh in range(HS):
        flipped = nn(mirror, jnp.concatenate(tiles[hh], axis=1).astype(BF16))
        turn = pltpu.roll(flipped, 0, 1, stride=1, stride_axis=0)
        sums[pl.ds(HS * step + hh, 1), :] = jnp.sum(turn, axis=0, keepdims=True)


def qkv_grad_kernel(
    lp, heads, info, turned, d_qkv, wq, wk, wv, gain, g_ffn, g_final, sums,
    send, keep, column,
):
    width = turned.shape[0]
    rows, cols = width // WB, width // NB
    each = rows + rows // 2
    size = WB * each
    core, y0 = info[1] % 2, info[1] // 2

    def put(n, first, values):
        for dst, mine in ((keep, n % 2 == core), (send, n % 2 != core)):

            @pl.when(mine)
            def _():
                for w in range(WB):
                    at = pl.multiple_of(((n // 2) ^ y0) * size + (w * each + first), 16)
                    dst[pl.ds(at, values.shape[1]), :] = values[w]

    def gradient(grads, weight):
        grad = nn(turned[...], grads)
        for w in range(WB):
            at = pl.ds(pl.multiple_of((w ^ info[0]) * rows, rows), rows)
            part = grad[w * rows : (w + 1) * rows, :] * weight[at, :].astype(F32)
            column[at, :] += jnp.broadcast_to(
                jnp.sum(part, axis=1, keepdims=True), (rows, column.shape[1])
            )
        return grad

    column[...] = jnp.zeros_like(column)
    gq, gk = gradient(d_qkv[0], wq), gradient(d_qkv[1], wk)
    for n in range(NB):
        here = slice(n * cols, (n + 1) * cols)
        both = jnp.concatenate([gq[:, here], gk[:, here]], axis=1).astype(BF16)
        put(n, 0, both.reshape(WB, rows, LANES))
    gv = gradient(d_qkv[2], wv)
    for n in range(NB):
        part = gv[:, n * cols : (n + 1) * cols].reshape(WB, rows, cols)
        part = jnp.concatenate([part[:, : rows // 2], part[:, rows // 2 :]], axis=2)
        put(n, rows, part.astype(BF16))
    g_attn = column[...].T[:1, :] / wide_row(gain)
    hot = bucket_hot(lp // 2, CH - 1).astype(F32)
    bias = nt(sums[...], hot, precision=HIGHEST)
    pieces = []
    for grad in (g_attn, g_ffn[...], g_final[...]):
        pieces += [grad[:, i : i + LANES] for i in range(0, width, LANES)]
    pieces.append(jnp.concatenate([bias[h : h + 1, :] for h in range(heads)], axis=1))
    pieces.append(jnp.zeros((SMALL - len(pieces), LANES), F32))
    small = encode(jnp.concatenate(pieces, axis=0))
    send[2 * size :, :] = small
    keep[2 * size :, :] = small


def input_kernel(segs, info, d_qkv, wq, wk, wv, d_resid, x, gain, grad_p, grad_q):
    off = 0
    for tower, grad in enumerate((grad_p, grad_q)):
        span = grad.shape[0]
        here = slice(off, off + span)
        off += span
        dn = nt(d_qkv[0, here], wq[...]) + nt(d_qkv[1, here], wk[...])
        dn = dn + nt(d_qkv[2, here], wv[...])
        v = x[here, :].astype(F32)
        r = lax.rsqrt(jnp.mean(v * v, axis=-1, keepdims=True) + EPS)
        gdy = wide_row(gain) * dn
        inner = jnp.mean(gdy * v, axis=-1, keepdims=True)
        out = d_resid[here, :] + (r * gdy - v * (r * r * r * inner))
        grad[...] = pltpu.roll(out, half_at(info, tower, segs, span), 0)


def proj_kernel(info, every, d_proj, proj_grad, full):
    rows, cols = proj_grad.shape
    width = full.shape[0]
    full[...] = tn(every[:, :width], d_proj[...])
    mine = full[pl.ds(pl.multiple_of(info[0] * rows, 8), rows), :]
    for n in range(width // cols):

        @pl.when(info[1] == n)
        def _():
            proj_grad[...] = mine[:, n * cols : (n + 1) * cols]


class Info:
    def __init__(self, place, passages, queries, pairs):
        segs = passages.shape[1]
        self.at = [lambda: place[0], lambda: place[1]]
        self.at += [functools.partial(lambda r, i: r[0, i], passages, i) for i in range(segs)]
        self.at += [functools.partial(lambda r, i: r[0, i], queries, i) for i in range(segs)]
        self.at += [functools.partial(lambda r, i: r[i], pairs, i) for i in range(segs)]

    def __getitem__(self, i):
        return self.at[i]()


def call(
    kernel, grid, info, args, in_specs, outs, out_specs, scratch=(), flops=0, moved=0,
    vmem=16, after=(), through=(), through_specs=(),
):
    count, more = len(args), len(after) + len(through)
    outs, out_specs = list(outs), list(out_specs)
    made = len(outs)
    aliases = {len(info) + count + len(after) + i: made + i for i in range(len(through))}
    outs += [(hbm_out if through_specs else shaped)(a.shape, a.dtype) for a in through]
    out_specs += through_specs or [pl.BlockSpec(memory_space=pl.ANY)] * len(through)
    hidden = 0 if through_specs else len(through)

    def body(*refs):
        scalars, refs = refs[: len(info)], refs[len(info) :]
        results = refs[count + more :]
        kernel(
            Info(*scalars) if scalars else None,
            *refs[:count],
            *results[:made],
            *results[made + hidden :],
        )

    return pl.pallas_call(
        body,
        grid_spec=pltpu.PrefetchScalarGridSpec(
            num_scalar_prefetch=len(info),
            grid=grid,
            in_specs=list(in_specs) + [pl.BlockSpec(memory_space=pl.ANY)] * more,
            out_specs=out_specs,
            scratch_shapes=list(scratch),
        ),
        out_shape=outs,
        input_output_aliases=aliases,
        compiler_params=pltpu.CompilerParams(vmem_limit_bytes=vmem * 2**20),
        cost_estimate=pl.CostEstimate(flops=flops, bytes_accessed=moved, transcendentals=0),
    )(*info, *args, *after, *through)


def hbm(array):
    return pltpu.with_memory_space_constraint(array, pltpu.HBM)


def near(*shape):
    return pl.BlockSpec(memory_space=pltpu.VMEM)


def whole(*shape):
    return pl.BlockSpec(shape, lambda *_: (0,) * len(shape), pipeline_mode=pl.Buffered(1))


def hbm_out(shape, dtype):
    return pltpu.HBM(shape, dtype)


def out_shape_of(out):
    return out.inner_aval.shape


def shaped(shape, dtype):
    return jax.ShapeDtypeStruct(shape, dtype)


def permute(array, bit, count):
    return lax.ppermute(array, AXES, [(i, i ^ bit) for i in range(count)])


CORE, Y, X, Z0, Z1 = 1, 2, 4, 8, 16
GATHER = (Z0, Z1, Y, X, CORE)


def own_sum(base, refs):
    parts = [r[b:, :].astype(F32) for b, r in zip(base, refs)]
    while len(parts) > 1:
        parts = [a + b for a, b in zip(parts[::2], parts[1::2])]
    return parts[0]


def out_ff_finish_kernel(base, info, *refs):
    refs[-1][...] = own_sum(base, refs[:-1])


def in_ff_finish_kernel(base, info, *refs):
    *parts, in_ff, out_w = refs
    total = own_sum(base, parts)
    rows, cols = out_w.shape
    in_ff[...] = jnp.concatenate([total[:rows], total[rows : 2 * rows]], axis=1)
    out_w[...] = jnp.concatenate([total[2 * rows :, :cols], total[2 * rows :, cols:]], axis=0)


def split_small(small, width, heads):
    per = width // LANES
    gains = [
        jnp.concatenate([small[g * per + i : g * per + i + 1] for i in range(per)], axis=1)
        for g in range(3)
    ]
    row = small[3 * per : 3 * per + 1]
    bias = [row[:, h * BUCKETS : (h + 1) * BUCKETS] for h in range(heads)]
    return gains, jnp.concatenate(bias, axis=0)


def qkv_finish_kernel(heads, base, info, *refs):
    rest, own, *got, query_w, key_w, value_w, gain_a, gain_f, gain_l, bias = refs
    total = own_sum(base, (rest, *got))
    rows, cols = query_w.shape
    query_w[...] = total[:rows, :cols]
    key_w[...] = total[:rows, cols:]
    value_w[...] = jnp.concatenate([total[rows:, :cols], total[rows:, cols:]], axis=0)
    small = [decode(r[: 2 * SMALL, :]) for r in (own, *got)]
    small = (small[0] + small[1]) + (small[2] + small[3])
    gains, table = split_small(small, gain_a.shape[0], heads)
    for ref, gain in zip((gain_a, gain_f, gain_l), gains):
        ref[...] = gain.reshape(gain.shape[1])
    bias[...] = table


def encode(values):
    high = values.astype(BF16).astype(F32)
    return jnp.concatenate([high, values - high], axis=0).astype(BF16)


def decode(coded):
    half = coded.shape[0] // 2
    return coded[:half].astype(F32) + coded[half:].astype(F32)


class Part:
    def __init__(self, arrays, base, dims, rows, lo=0, hi=None):
        self.arrays, self.base, self.dims, self.rows = arrays, base, dims, rows
        self.lo, self.hi = lo, rows if hi is None else hi

    def at(self, where):
        dims, which = self.dims, 0
        if len(self.arrays) > 1:
            which, dims = where[dims[0]], dims[1:]
        index = 0
        for bit in dims:
            index = index * 2 + where[bit]
        return self.arrays[which], self.base + index * self.rows + self.lo


def add_kernel(plans, info, *refs):
    outs = refs[len(refs) - len(plans) :]
    for (sums, small), out in zip(plans, outs):
        if small:
            total = decode(refs[small[0]][small[1] : small[1] + 2 * SMALL, :])
            total = total + decode(refs[small[2]][small[3] : small[3] + 2 * SMALL, :])
            out[: 2 * SMALL, :] = encode(total)
        for to, a, at_a, b, at_b, rows in sums:
            value = refs[a][at_a : at_a + rows, :]
            out[to : to + rows, :] = value if b is None else value + refs[b][at_b : at_b + rows, :]


class Scatter:
    def __init__(self, groups, count, quad=False, z=(Z0, Z1)):
        self.count, self.groups, self.quad, self.z = count, groups, quad, z
        self.sources = []
        self.small = None
        self.stage = -1

    def source(self, send, keeps, rows, small=False):
        send = send.reshape(-1, LANES)
        keeps = [k.reshape(-1, LANES) for k in keeps]
        got = permute(send, CORE, self.count)
        self.sources.append((keeps, got, rows))
        if small:
            at = 16 * rows
            self.small = (keeps[0], at, got, at)

    def jobs(self):
        self.stage += 1
        stage = self.stage
        if stage == 0:
            dims = (Y, Z1, Z0, X)
            groups = [
                [
                    (
                        Part(self.sources[n][0], 0, dims, self.sources[n][2], lo, hi),
                        Part([self.sources[n][1]], 0, dims, self.sources[n][2], lo, hi),
                    )
                    for n, lo, hi in group
                ]
                for group in self.groups
            ]
        else:
            groups = [[pair] for pair in zip(self.rest, self.got)]
        if stage < 2:
            bits = ((Y, X), (X, Y))[stage]
            first = [(g, {b: 1}) for g, b in zip(groups, bits)]
            rest = [(g, {b: 0}) for g, b in zip(groups, bits)]
            self.bits = bits
        else:
            merged = [pair for group in groups for pair in group]
            if self.quad:
                self.bits = (Z0, Z1, Z0 | Z1)
                first = [(merged, {Z0: a, Z1: b}) for a, b in ((1, 0), (0, 1), (1, 1))]
                rest = [(merged, {Z0: 0, Z1: 0})]
            else:
                bit = self.z[stage - 2]
                self.bits = (bit,)
                first, rest = [(merged, {bit: 1})], [(merged, {bit: 0})]
        carry = [self.small is not None and (stage >= 2 or i == 1) for i in range(len(first))]
        return first, rest, carry

    def take(self, first, rest, hold=False):
        self.first, self.rest, self.got = first, rest, []
        if hold:
            return
        for part, bit in zip(first, self.bits):
            got = permute(part.arrays[0], bit, self.count)
            self.got.append(Part([got], part.base, part.dims, part.rows))
        if self.small is not None:
            at = 0 if self.stage >= 2 else 1
            self.small = (first[at].arrays[0], 0, self.got[at].arrays[0], 0)

    def finish(self):
        parts = [self.rest[0], *self.got]
        return [p.arrays[0] for p in parts], tuple(p.base for p in parts)


def advance(info, scatters, after=(), through=(), hold=None, join=None):
    inputs, plans, shapes, slots = [], [], [], []

    def find(array):
        for i, known in enumerate(inputs):
            if known is array:
                return i
        inputs.append(array)
        return len(inputs) - 1

    for scatter in scatters:
        first, rest, carry = scatter.jobs()
        for n, (pairs, fixed) in enumerate(first + rest):
            dims = tuple(d for d in pairs[0][0].dims if d not in fixed)
            rows = sum(a.hi - a.lo for a, _ in pairs)
            base, small = 0, ()
            if n < len(first) and carry[n]:
                own, at_own, got, at_got = scatter.small
                base, small = 2 * SMALL, (find(own), at_own, find(got), at_got)
            sums = []
            for index in range(2 ** len(dims)):
                where = dict(fixed)
                for i, d in enumerate(reversed(dims)):
                    where[d] = (index >> i) & 1
                to = base + index * rows
                for a, b in pairs:
                    (array_a, row_a), (array_b, row_b) = a.at(where), b.at(where)
                    size = a.hi - a.lo
                    sums.append((to, find(array_a), row_a, find(array_b), row_b, size))
                    to += size
            end = base + 2 ** len(dims) * rows
            if join is not None and scatter is join[0] and n == 0:
                (held,) = join[1].first
                sums.append((end, find(held.arrays[0]), held.base, None, 0, held.rows))
                joined = (end, held)
                end += held.rows
            plans.append((sums, small))
            shapes.append(shaped((end, LANES), BF16))
            slots.append((base, dims, rows))
        scatter.counts = (len(first), len(rest))
    outs = call(
        functools.partial(add_kernel, plans), (1,), info, inputs, [near()] * len(inputs), shapes,
        [near()] * len(shapes), flops=10**6, moved=2**20, vmem=4, after=after, through=through,
    )
    handed = outs[len(slots) :]
    parts = [Part([out], *slot) for out, slot in zip(outs, slots)]
    sent = []
    for scatter in scatters:
        many, more = scatter.counts
        scatter.take(parts[:many], parts[many : many + more], scatter is hold)
        sent += [p.arrays[0] for p in parts[:many]]
        if join is not None and scatter is join[0]:
            at, held = joined
            join[1].got = [Part(scatter.got[0].arrays, at, held.dims, held.rows)]
        parts = parts[many + more :]
    return sent, handed


def per_device(
    fast, n_wide, n_narrow,
    xp, xq, passage_lengths, query_lengths, pair_index, g_attn, w_query, w_key, w_value, w_out,
    bias_table, g_ffn, w_in, w_back, g_final, w_proj,
):
    lp, width = xp.shape
    lq = xq.shape[0]
    total = lp + lq
    heads = bias_table.shape[1]
    dk = width // heads
    ff = w_in.shape[1]
    segs = passage_lengths.shape[1]
    count = n_wide * n_narrow
    steps = heads // HS
    rows, cols = width // WB, width // NB
    wide_at, narrow_at = lax.axis_index("wide"), lax.axis_index("narrow")
    place = jnp.stack([wide_at, narrow_at]) if fast else jnp.zeros((2,), jnp.int32)
    info = (place.astype(jnp.int32), hbm(passage_lengths), hbm(query_lengths), hbm(pair_index))
    mm = 2 * total * width * width
    act, act32 = shaped((total, width), BF16), shaped((total, width), F32)
    act_hbm = pltpu.HBM((total, width), BF16)

    head_tile = pl.BlockSpec((total, HS * dk), lambda i, *_: (0, i))
    col_tile = pl.BlockSpec((width, HS * dk), lambda i, *_: (0, i))
    prob_tiles = [pl.BlockSpec((2 * HS, n // 2, n // 2), lambda i, *_: (i, 0, 0)) for n in (lp, lq)]
    x, normed, q, k, v, probs_p, probs_q, ctx = call(
        functools.partial(front_kernel, lp, lq, segs, dk),
        (steps,),
        info,
        (*(hbm(a) for a in (xp, xq, g_attn, w_query, w_key, w_value)), hbm(bias_table.T)),
        [whole(lp, width), whole(lq, width), whole(width)] + [col_tile] * 3
        + [whole(heads, BUCKETS)],
        [act, act_hbm, act_hbm, act_hbm, act_hbm]
        + [pltpu.HBM((2 * heads, n // 2, n // 2), BF16) for n in (lp, lq)]
        + [act],
        [near(), whole(total, width), head_tile, head_tile, head_tile, *prob_tiles, head_tile],
        [pltpu.VMEM((16, lp), F32)],
        flops=12 * 10**9,
        moved=13 * 2**20,
    )

    ff_tile = ff // NB
    ff_spec = pl.BlockSpec((total, ff_tile), lambda i, *_: (0, i))
    message = width + 128
    residual, normed_two, hidden, slope, output, pooled = call(
        functools.partial(ffn_kernel, lp, lq, segs),
        (NB,),
        info,
        (ctx, x, w_out, g_ffn, w_in, w_back, g_final),
        [near()] * 7,
        [
            act32, act, shaped((total, ff), BF16), shaped((total, ff), BF16), act32,
            shaped((2 * segs, message), BF16),
        ],
        [near()] * 6,
        flops=9 * mm,
        moved=30 * 2**20,
        vmem=24,
    )

    if fast:
        parts = [pooled] + [permute(pooled, b, count) for b in (Z0, Z1, Z0 | Z1)]
        one = jnp.concatenate(parts, axis=0)
        two = jnp.concatenate([one] + [permute(one, b, count) for b in (Y, X, Y | X)], axis=0)
        every = 2 * two.shape[0]
        query_loss, d_proj, d_pooled, gathered = call(
            functools.partial(loss_kernel, segs, GATHER),
            (1,),
            info,
            (two, permute(two, CORE, count), w_proj),
            [near(), near(), near()],
            [
                hbm_out((segs,), F32), hbm_out((every, width), BF16),
                shaped((2 * segs, width), F32), hbm_out((every, message), BF16),
            ],
            [whole(segs), whole(every, width), near(), whole(every, message)],
            flops=10**9,
            moved=2**20,
        )
    else:
        gathered = lax.all_gather(pooled, AXES, axis=0, tiled=True)
        every = gathered.shape[0]
        block = jnp.arange(every, dtype=jnp.int32) // (2 * segs)
        loss, d_proj = loss_math(segs, block[:, None], block[None, :], gathered, w_proj)
        mine = (wide_at * n_narrow + narrow_at) * 2 * segs
        query_loss = lax.dynamic_slice_in_dim(loss, mine + segs, segs, 0)[:, 0]
        d_pooled = nt(lax.dynamic_slice_in_dim(d_proj, mine, 2 * segs, 0), w_proj)

    part1 = (2, WB // 2, 2, cols, LANES)
    block1 = pl.BlockSpec((2, 1, 2, cols, LANES), lambda i, *_: (0, i, 0, 0, 0))
    d_output, d_ffn, final_gain_grad, turned_ff, send1 = call(
        functools.partial(out_ff_send_kernel, lp, lq, segs),
        (WB // 2,),
        info,
        (d_pooled, output, g_final, hidden),
        [near(), near(), near(), near()],
        [act32, act, shaped((1, width), F32), shaped((width, total), BF16), shaped(part1, BF16)],
        [near(), near(), near(), near(), block1],
        flops=3 * mm,
        moved=10 * 2**20,
        vmem=12,
    )
    keep1, turned_two = call(
        out_ff_keep_kernel,
        (WB // 2,),
        info,
        (turned_ff, hidden, normed_two),
        [near(), near(), near()],
        [shaped(part1, BF16), shaped((width, total), BF16)],
        [block1, near()],
        flops=2 * mm,
        moved=8 * 2**20,
        vmem=6,
    )

    after = []
    if fast:
        sc1 = Scatter((((0, 0, cols // 2),), ((0, cols // 2, cols),)), count, z=(Z1, Z0))
        sc1.source(send1, [keep1], cols)
        after, _ = advance(info, [sc1])

    size2, size_o = 2 * rows, rows // 2
    part2 = shaped((2, WB, size2, LANES), BF16)
    part_o = shaped((2, WB, size_o, LANES), BF16)

    def tiles_at(first):
        return [
            near(),
            near(),
            near(),
            near(),
        ]

    half2 = shaped((WB, size2, LANES), BF16)
    send2, keep2a, so_far = call(
        ffn_back_first_kernel,
        (3,),
        info,
        (d_ffn, w_back, slope, w_in, turned_two),
        tiles_at(0) + [near()],
        [part2, half2, act32],
        [near()] * 3,
        flops=9 * mm,
        moved=16 * 2**20,
        vmem=16,
        after=after,
    )
    turned_ctx, turned = call(
        turn_kernel,
        (1,),
        info,
        (ctx, normed),
        [near()] * 2,
        [shaped((width, total), BF16), pltpu.HBM((width, total), BF16)],
        [near(), whole(width, total)],
        flops=10**6,
        moved=2**20,
        vmem=6,
        after=[so_far],
    )
    after = []
    if fast:
        after, (send2,) = advance(info, [sc1], [hbm(turned)], [send2])
    keep2b, d_resid, ffn_gain_grad, d_ctx, send_o, keep_o = call(
        ffn_back_last_kernel,
        (1,),
        info,
        (
            d_ffn, w_back, slope, w_in, turned_two, so_far, d_output, residual, g_ffn,
            turned_ctx, w_out,
        ),
        tiles_at(3) + [near()] * 7,
        [half2, act32, shaped((1, width), F32), act, part_o, part_o],
        [near()] * 6,
        flops=5 * mm,
        moved=20 * 2**20,
        vmem=18,
        after=after,
    )

    after = []
    if fast:
        sc2 = Scatter((((0, 0, 128),), ((0, 128, size2), (1, 0, size_o))), count)
        sc2.source(send2, [keep2a, keep2b], size2)
        after, (send_o,) = advance(info, [sc1], [d_ctx], [send_o])
        sc2.source(send_o, [keep_o], size_o)
        more, _ = advance(info, [sc2], after)
        after = after + more
    d_qkv, sums = call(
        functools.partial(attn_back_kernel, dk, lp, lq),
        (steps,),
        info,
        (hbm(q), hbm(k), hbm(v), d_ctx, hbm(probs_p), hbm(probs_q)),
        [head_tile] * 4 + prob_tiles,
        [shaped((3, total, width), BF16), shaped((16, lp), F32)],
        [near(), near()],
        flops=8 * 10**9,
        moved=16 * 2**20,
        after=after,
    )

    size3 = rows + rows // 2
    flat3 = shaped((16 * size3 + 16, LANES), BF16)
    send3, keep3 = call(
        functools.partial(qkv_grad_kernel, lp, heads),
        (1,),
        info,
        (
            turned, d_qkv, w_query, w_key, w_value, g_attn, ffn_gain_grad,
            final_gain_grad, sums,
        ),
        [near()] * 9,
        [flat3, flat3],
        [near(), near()],
        [
            pltpu.VMEM((width, 128), F32),
        ],
        flops=3 * mm,
        moved=9 * 2**20,
        vmem=24,
        after=after,
    )

    after = []
    own_rows, own_cols = width // WB, width // NB
    square = hbm_out((own_rows, own_cols), F32)
    if fast:

        def finish(kernel, scatter, outs, after, more=()):
            parts, base = scatter.finish()
            parts = parts[:1] + list(more) + parts[1:]
            return call(
                functools.partial(kernel, base), (1,), info, parts, [near()] * len(parts), outs,
                [whole(*out_shape_of(out)) for out in outs], flops=10**6, moved=2**20, after=after,
            )

        sc3 = Scatter((((0, 0, 80),), ((0, 80, size3),)), count, quad=True)
        after, (send3,) = advance(info, [sc1, sc2], [keep3], [send3], hold=sc1)
        sc3.source(send3, [keep3], size3, small=True)

    grad_p, grad_q = call(
        functools.partial(input_kernel, segs),
        (1,),
        info,
        (d_qkv, w_query, w_key, w_value, d_resid, x, g_attn),
        [near()] * 7,
        [hbm_out((lp, width), F32), hbm_out((lq, width), F32)],
        [whole(lp, width), whole(lq, width)],
        flops=3 * mm,
        moved=6 * 2**20,
        vmem=20,
        after=after,
    )
    after = [hbm(grad_p)]
    if fast:
        after, _ = advance(info, [sc3, sc2], after, join=(sc2, sc1))
    (proj_grad,) = call(
        proj_kernel,
        (1,),
        info,
        (gathered[:256], d_proj[:256]),
        [near(), near()],
        [square],
        [whole(own_rows, own_cols)],
        [pltpu.VMEM((width, width), F32)],
        flops=mm,
        moved=2**20,
        vmem=20,
        after=after,
    )

    if fast:
        after, _ = advance(info, [sc3, sc2], [hbm(proj_grad)])
        (out_ff,) = finish(out_ff_finish_kernel, sc1, [hbm_out((cols, ff // WB), F32)], after)
        after, _ = advance(info, [sc3], [hbm(out_ff)])
        out_ff = out_ff.T
        in_ff, out_w = finish(
            in_ff_finish_kernel, sc2, [hbm_out((rows, ff // NB), F32), square], after
        )
        query_w, key_w, value_w, gain_a, gain_f, gain_l, bias = finish(
            functools.partial(qkv_finish_kernel, heads), sc3,
            [square] * 3 + [hbm_out((width,), F32)] * 3 + [hbm_out((heads, BUCKETS), F32)],
            [hbm(out_w)], [sc3.first[0].arrays[0]],
        )
    else:
        own_rows, own_cols = width // n_wide, width // n_narrow
        left = lax.dynamic_slice(gathered, (0, wide_at * own_rows), (every, own_rows))
        right = lax.dynamic_slice(d_proj, (0, narrow_at * own_cols), (every, own_cols))
        proj_grad = tn(left, right)

        def blocks(send, keep):
            both = jnp.stack([keep, send], axis=1).astype(F32)
            return both.reshape((NB, WB) + both.shape[-2:])

        def spread(matrix):
            matrix = lax.psum_scatter(matrix, "wide", scatter_dimension=0, tiled=True)
            return lax.psum_scatter(matrix, "narrow", scatter_dimension=1, tiled=True)

        def side(part):
            half = part.shape[2] // 2
            return jnp.concatenate([part[:, :, :half], part[:, :, half:]], axis=3)

        def stack(part):
            half = part.shape[3] // 2
            return jnp.concatenate([part[..., :half], part[..., half:]], axis=2)

        def matrix(part):
            return part.transpose(1, 2, 0, 3).reshape(WB * part.shape[2], NB * part.shape[3])

        b1 = blocks(send1.reshape(2, WB, cols, LANES), keep1.reshape(2, WB, cols, LANES))
        b2 = blocks(send2, jnp.stack([keep2a, keep2b]))
        coded = keep3[16 * size3 :]
        b3 = blocks(*(a[: 16 * size3].reshape(2, WB, size3, LANES) for a in (send3, keep3)))
        out_ff = spread(matrix(b1.transpose(0, 1, 3, 2)))
        in_ff = spread(matrix(side(b2)))
        out_w = spread(matrix(stack(blocks(send_o, keep_o))))
        query_w = spread(matrix(b3[:, :, :rows, :cols]))
        key_w = spread(matrix(b3[:, :, :rows, cols:]))
        value_w = spread(matrix(stack(b3[:, :, rows:])))
        gains, bias = split_small(lax.psum(decode(coded), AXES), width, heads)
        gain_a, gain_f, gain_l = (gain[0] for gain in gains)
    return (
        query_loss, grad_p, grad_q, gain_a, query_w, key_w, value_w, out_w, bias.T, gain_f,
        in_ff, out_ff, gain_l, proj_grad,
    )


def solution(mesh):
    n_wide, n_narrow = mesh.shape["wide"], mesh.shape["narrow"]
    fast = (n_wide, n_narrow) == (WB, NB)
    rows = P(AXES, None)
    owned = P("wide", "narrow")
    return jax.shard_map(
        functools.partial(per_device, fast, n_wide, n_narrow),
        mesh=mesh,
        in_specs=(rows, rows, rows, rows, P(AXES)) + (P(),) * 11,
        out_specs=(
            P(AXES), rows, rows, P(), owned, owned, owned, owned, P(), P(),
            owned, owned, P(), owned,
        ),
        check_vma=False,
    )
```
